32 devices in a mesh: dp: 8 (over y, x, core), tensor: 4 (over z).
Axes of the slice: x: 2, y: 2, z: 4, core: 2. Of those that a mesh axis runs over, the one named last changes fastest.
Arguments:
- tokens: bfloat16 [1024, 1152], P('dp', 'tensor'), may hold values from -6 to 6
- resets: int32 [1024], P('dp'), may hold values 0 or 1
- routes: int32 [1024, 1], P('dp'), may hold values from 0 to 7; in each aligned block of 128 rows (0 to 127, 128 to 255, ...) at most 32 rows name the same one
- norm_one: float32 [1152], replicated, may hold values from 0.5 to 1.5
- in_proj: bfloat16 [2, 1152, 2304], P(None, None, 'tensor'), may hold values from -0.1875 to 0.1875
- conv_weight: float32 [4, 2304], P(None, 'tensor'), may hold values from -3 to 3
- conv_bias: float32 [2304], P('tensor'), may hold values from -3 to 3
- x_proj: bfloat16 [2304, 104], P('tensor'), may hold values from -0.125 to 0.125
- dt_proj: bfloat16 [72, 2304], P(None, 'tensor'), may hold values from -0.75 to 0.75
- dt_bias: float32 [2304], P('tensor'), may hold values from -4 to -1
- decay_log: float32 [16, 2304], P(None, 'tensor'), may hold values from 0 to 2.77
- skip_gain: float32 [2304], P('tensor'), may hold values from 0.5 to 1.5
- out_proj: bfloat16 [2304, 1152], P('tensor'), may hold values from -0.5 to 0.5
- norm_two: float32 [1152], replicated, may hold values from 0.5 to 1.5
- expert_in: bfloat16 [8, 1152, 3072], P(None, 'dp', 'tensor'), may hold values from -0.1875 to 0.1875
- expert_out: bfloat16 [8, 1152, 3072], P(None, 'dp', 'tensor'), may hold values from -0.15625 to 0.15625
- cotangent: bfloat16 [1024, 1152], P('dp'), may hold values from -6 to 6
Outputs:
- result: bfloat16 [1024, 1152], P('dp', 'tensor')
- grad_tokens: float32 [1024, 1152], P('dp', 'tensor')
- grad_norm_one: float32 [1152], replicated
- grad_in_proj: float32 [2, 1152, 2304], P(None, None, 'tensor')
- grad_conv_weight: float32 [4, 2304], P(None, 'tensor')
- grad_conv_bias: float32 [2304], P('tensor')
- grad_x_proj: float32 [2304, 104], P('tensor')
- grad_dt_proj: float32 [72, 2304], P(None, 'tensor')
- grad_dt_bias: float32 [2304], P('tensor')
- grad_decay_log: float32 [16, 2304], P(None, 'tensor')
- grad_skip_gain: float32 [2304], P('tensor')
- grad_out_proj: float32 [2304, 1152], P('tensor')
- grad_norm_two: float32 [1152], replicated
- grad_expert_in: float32 [8, 1152, 3072], P(None, 'dp', 'tensor')
- grad_expert_out: float32 [8, 1152, 3072], P(None, 'dp', 'tensor')
The draws below stay inside these ranges and needn't reach their ends.
Inputs may be any that keep to these rules, and one draw needn't show every extreme that they name: `routes`: in each aligned block of 128 rows no expert is named by more than 32 rows.
All inputs are finite; a program needn't handle non-finite values. No bound on the sum of `resets` on one device may be relied on, other than what follows from the above.
Results may differ from the reference program's by a relative error of at most 0.02.
Values may be sent and summed in bfloat16 or wider, within the bound.
No kernel may reach another device: no remote copies, remote signals or barrier semaphores. Data moves between devices by JAX's collectives and lax.ppermute only.
A program may use at most 128 MiB of HBM per device.

```python
import math
import jax
import jax.numpy as jnp
import numpy as np
from jax import lax

D = 1152
INNER = 2304
STATE = 16
DT_RANK = 72
CONV = 4
EXPERTS = 8
HIDDEN_SIZE = 3072
SEQ_LEN = 128
PROJ = 104
TOKENS = 1024
BLOCK = 128
CAP = 32
N_DP = 8
N_TENSOR = 4


def place_ends(result, key, low, top_value):
    longest = result.shape.index(max(result.shape))
    spots = []
    for shift in (0, 1):
        where = [jax.random.randint(jax.random.fold_in(key, axis), (), 0, length) for axis, length in enumerate(result.shape)]
        where[longest] = (where[longest] + shift) % result.shape[longest]
        spots.append(tuple(where))
    return result.at[spots[0]].set(low).at[spots[1]].set(top_value)


def shard_levels(own_key, extent, shards, least, largest):
    def one(dim, shards_of):
        draws = jax.random.uniform(jax.random.fold_in(jax.random.fold_in(own_key, 6), dim), (shards_of,), jnp.float32, least / len(shards), largest / len(shards))
        return jnp.repeat(jnp.exp(draws), extent[dim] // shards_of).reshape((-1,) + (1,) * (len(extent) - dim - 1))

    loudness = one(*shards[0])
    for cut in shards[1:]:
        loudness = loudness * one(*cut)
    return loudness


def assign_block(rng, own, number, rows, count, top, bound, slope):
    sequence = jax.random.permutation(rng, count)
    packed, ordinary = load_shares(count, rows * top, bound, slope, True), load_shares(count, rows * top, bound, slope, False)
    places = jnp.arange(count)

    def named(lengths, rotation):
        used = int((lengths > 0).sum())
        fixed = max(1, used // 4)
        shifted = fixed + (places - fixed + rotation * (used - fixed)) % max(1, count - fixed)
        return jnp.zeros((count,), jnp.int32).at[sequence[jnp.where(places < fixed, places, shifted)]].set(jnp.asarray(lengths, jnp.int32))

    lengths = jnp.where(number % 4 == 0, named(packed, number // 4), named(ordinary, number - number // 4 - 1))
    mixed = jax.random.permutation(jax.random.fold_in(own, 3), count)
    giver, taker = mixed[0:count // 2 * 2:2], mixed[1:count // 2 * 2:2]
    slack = jnp.minimum(lengths[giver] - 1, bound - lengths[taker]) // 2
    slack = jnp.where((giver == sequence[0]) | (taker == sequence[0]) | (lengths[taker] == 0), 0, jnp.maximum(slack, 0))
    shifted = jax.random.randint(jax.random.fold_in(own, 4), (count // 2,), 0, 1 << 20) % (slack + 1)
    lengths = lengths.at[giver].add(-shifted).at[taker].add(shifted)
    members = jnp.searchsorted(jnp.cumsum(lengths), jnp.arange(rows * top), side="right").astype(jnp.int32)
    grid = members.reshape(top, rows).T
    grid = grid[jax.random.permutation(jax.random.fold_in(own, 1), rows)]
    rotation = jax.random.randint(jax.random.fold_in(own, 2), (rows, 1), 0, top)
    return jnp.take_along_axis(grid, (jnp.arange(top)[None, :] + rotation) % top, axis=1)


def load_shares(number_of, total, most, slope, full):
    weights = [(1 << 20) // math.isqrt(rank ** slope) + 1 for rank in range(1, number_of + 1)]
    largest = most if full else min(most, max(-(-total // number_of), total * weights[0] // sum(weights)))
    least = 1 if total - largest >= number_of - 1 else 0
    counts, spare = [largest] + [least] * (number_of - 1), total - largest - least * (number_of - 1)
    while spare > 0:
        free = [i for i in range(1, number_of) if counts[i] < largest] or [i for i in range(1, number_of) if counts[i] < most]
        mass, left = sum([weights[i] for i in free]), spare
        for i in free:
            extra = min(most - counts[i], max(1, left * weights[i] // mass), spare)
            counts[i] = counts[i] + extra
            spare = spare - extra
    return np.array(counts)


def bell_draw(rng, extent, width, bound, split=(), held_as=jnp.bfloat16):
    result = jax.random.normal(rng, extent, jnp.float32) * width
    if len(split) > 0:
        result = shard_levels(rng, extent, split, -0.22, 0.18) * result
    return jnp.clip(result, min=-bound, max=bound).astype(held_as)


def setup_inputs(seed: int = 0) -> dict:
    key_of = jax.random.split(jax.random.key(seed), 18)
    tokens = bell_draw(key_of[0], (TOKENS, D), 1.0, 6.0, ((0, 8), (1, 4)))
    resets = place_ends((jax.random.randint(key_of[1], (TOKENS,), 0, 128) < 1).astype(jnp.int32), jax.random.fold_in(key_of[1], 1), 0, 1)
    routes_keys = jax.random.split(jax.random.fold_in(key_of[2], 1), TOKENS // BLOCK)
    routes_turns = jax.random.permutation(jax.random.fold_in(key_of[2], 3), TOKENS // BLOCK)
    routes = jax.vmap(lambda own, number: assign_block(jax.random.fold_in(key_of[2], 2), own, number, BLOCK, EXPERTS, 1, CAP, 2))(routes_keys, routes_turns).reshape((TOKENS, 1))
    norm_one = jnp.clip(1.0 + 0.1 * jax.random.normal(key_of[3], (D,), jnp.float32), 0.5, 1.5)
    in_proj = bell_draw(key_of[4], (2, D, INNER), D ** -0.5, 0.1875, ((2, 4),))
    conv_weight = bell_draw(key_of[5], (CONV, INNER), CONV ** -0.5, 3.0, ((1, 4),), jnp.float32)
    conv_bias = bell_draw(key_of[6], (INNER,), 0.5, 3.0, ((0, 4),), jnp.float32)
    x_proj = bell_draw(key_of[7], (INNER, PROJ), INNER ** -0.5, 0.125, ((0, 4),))
    dt_proj = bell_draw(key_of[8], (DT_RANK, INNER), DT_RANK ** -0.5, 0.75, ((1, 4),))
    dt_bias = jnp.clip(-4.0 + 3.0 * jax.random.uniform(key_of[9], (INNER,), jnp.float32) ** shard_levels(key_of[9], (INNER,), ((0, 4),), -0.2, 0.2), -4.0, -1.0)
    decay_log = jnp.clip(2.77 * jax.random.uniform(key_of[10], (STATE, INNER), jnp.float32) ** shard_levels(key_of[10], (STATE, INNER), ((1, 4),), -0.2, 0.2), 0.0, 2.77)
    skip_gain = jnp.clip(0.5 + 1.0 * jax.random.uniform(key_of[11], (INNER,), jnp.float32) ** shard_levels(key_of[11], (INNER,), ((0, 4),), -0.2, 0.2), 0.5, 1.5)
    out_proj = bell_draw(key_of[12], (INNER, D), (INNER // 16) ** -0.5, 0.5, ((0, 4),))
    norm_two = jnp.clip(1.0 + 0.1 * jax.random.normal(key_of[13], (D,), jnp.float32), 0.5, 1.5)
    expert_in = bell_draw(key_of[14], (EXPERTS, D, HIDDEN_SIZE), D ** -0.5, 0.1875, ((1, 8), (2, 4)))
    expert_out = bell_draw(key_of[15], (EXPERTS, D, HIDDEN_SIZE), (HIDDEN_SIZE // 2) ** -0.5, 0.15625, ((1, 8), (2, 4)))
    cotangent = bell_draw(key_of[16], (TOKENS, D), 1.0, 6.0, ((0, 8),))
    return dict(tokens=tokens, resets=resets, routes=routes, norm_one=norm_one, in_proj=in_proj, conv_weight=conv_weight, conv_bias=conv_bias, x_proj=x_proj, dt_proj=dt_proj, dt_bias=dt_bias, decay_log=decay_log, skip_gain=skip_gain, out_proj=out_proj, norm_two=norm_two, expert_in=expert_in, expert_out=expert_out, cotangent=cotangent)


EPSILON = 1e-05
PRECISE = lax.Precision.HIGHEST

@jax.custom_vjp
def low(v):
    return lax.optimization_barrier(v.astype(jnp.bfloat16)).astype(jnp.float32)

@jax.custom_vjp
def low_back(v):
    return v

def low_keep(v):
    return (low(v), None)

def low_pass(kept, grad):
    return (grad,)

def back_keep(v):
    return (v, None)

def back_low(kept, grad):
    return (low(grad),)
low.defvjp(low_keep, low_pass)
low_back.defvjp(back_keep, back_low)

def rms_scale(values, gain):
    return values * lax.rsqrt(lax.optimization_barrier(jnp.mean(values * values, axis=-1, keepdims=True)) + EPSILON) * gain

def conv_mix(values, weight, offset, segment):
    length = values.shape[0]
    tap_count = weight.shape[0]
    running_sum = offset + weight[tap_count - 1] * values
    for shift_by in range(1, tap_count):
        moved_rows = jnp.concatenate([jnp.zeros((shift_by, values.shape[1]), values.dtype), values[:length - shift_by]], axis=0)
        earlier = jnp.concatenate([jnp.full((shift_by,), -1, jnp.int32), segment[:length - shift_by]], axis=0)
        same_doc = (earlier == segment).astype(values.dtype)
        running_sum = running_sum + weight[tap_count - 1 - shift_by] * moved_rows * same_doc[:, None]
    return running_sum

def scan_piece(activ_in, step_prod, step_bias, decay_in, skip_in, b_input, c_input, gate_in, keep_mask):
    length, chans = activ_in.shape
    states = decay_in.shape[0]
    block_len = math.gcd(length, 16)
    block_num = length // block_len
    step_size = jax.nn.softplus(step_prod + step_bias)
    rate_flat = -jnp.exp(decay_in).reshape(1, states * chans)
    row_ids = jnp.arange(block_len, dtype=jnp.int32)
    lower = row_ids[:, None] >= row_ids[None, :]

    def block_fn(carried, pieces):
        step_b, activ_b, b_block, c_block, keep_b = pieces
        log_decay = rate_flat * jnp.tile(step_b, (1, states))
        cum = jnp.cumsum(log_decay, axis=0)
        reset_count = jnp.cumsum((keep_b == 0).astype(jnp.int32)).astype(jnp.int32)
        allowed = jnp.logical_and(lower, reset_count[:, None] == reset_count[None, :])
        allowed_f = allowed.astype(activ_b.dtype)
        diff = cum[:, None, :] - cum[None, :, :]
        weights = jnp.exp(jnp.where(allowed[:, :, None], diff, 0.0)) * allowed_f[:, :, None]
        drive_in = (b_block[:, :, None] * (step_b * activ_b)[:, None, :]).reshape(block_len, states * chans)
        from_block = lax.optimization_barrier(jnp.sum(weights * drive_in[None, :, :], axis=1))
        carry_keep = (reset_count == 0).astype(activ_b.dtype)
        new_states = from_block + jnp.exp(cum) * carry_keep[:, None] * carried[None, :]
        out_rows = jnp.einsum('snc,sn->sc', new_states.reshape(block_len, states, chans), c_block, precision=PRECISE)
        return (new_states[-1], out_rows)
    pieces = (step_size.reshape(block_num, block_len, chans), activ_in.reshape(block_num, block_len, chans), b_input.reshape(block_num, block_len, states), c_input.reshape(block_num, block_len, states), keep_mask.reshape(block_num, block_len))
    start_state = jnp.zeros((states * chans,), activ_in.dtype)
    last_state, out_blocks = lax.scan(jax.checkpoint(block_fn), start_state, pieces)
    y_rows = out_blocks.reshape(length, chans) + skip_in * activ_in
    return y_rows * jax.nn.silu(gate_in)

def expert_apply(entry_tuple):
    slot_rows, first_proj, second_proj = entry_tuple
    pre_gelu = low_back(jnp.dot(slot_rows, first_proj, precision=PRECISE))
    hidden = low(jax.nn.gelu(pre_gelu))
    return jnp.dot(hidden, second_proj.T, precision=PRECISE)

def experts_rows(normed, expert_ids, expert_in, expert_out):
    length = normed.shape[0]
    block_num = length // BLOCK
    choose = (expert_ids[:, None] == jnp.arange(EXPERTS, dtype=jnp.int32)[None, :]).astype(jnp.int32)
    running = jnp.cumsum(choose.reshape(block_num, BLOCK, EXPERTS), axis=1).reshape(length, EXPERTS).astype(jnp.int32)
    slot_rank = lax.optimization_barrier(jnp.sum((running - 1) * choose, axis=1)).astype(jnp.int32)
    position = jnp.arange(length, dtype=jnp.int32)
    slot_index = (expert_ids * (block_num * CAP) + position // BLOCK * CAP + slot_rank).astype(jnp.int32)
    source = jnp.full((EXPERTS * block_num * CAP,), length, jnp.int32).at[slot_index].set(position)
    padded = jnp.concatenate([normed, jnp.zeros((1, normed.shape[1]), normed.dtype)], axis=0)
    buffer = padded[source].reshape(EXPERTS, block_num * CAP, normed.shape[1])
    results = lax.map(jax.checkpoint(expert_apply), (buffer, expert_in, expert_out))
    return results.reshape(EXPERTS * block_num * CAP, normed.shape[1])[slot_index]

def layer_rows(row_data, reset_row, expert_ids, params):
    norm_one, in_proj, conv_weight, conv_bias, x_proj, dt_proj, dt_bias, decay_log, skip_gain, out_proj, norm_two, expert_in, expert_out = params
    length = row_data.shape[0]
    chans = INNER // N_TENSOR
    normed = low(rms_scale(row_data, norm_one))
    inner_raw = low_back(jnp.dot(normed, in_proj[0], precision=PRECISE))
    gate_in = low_back(jnp.dot(normed, in_proj[1], precision=PRECISE))
    segment = jnp.cumsum(reset_row).astype(jnp.int32)
    activ = low(jax.nn.silu(conv_mix(inner_raw, conv_weight, conv_bias, segment)))
    proj_parts = jnp.einsum('lkc,kcp->klp', activ.reshape(length, N_TENSOR, chans), x_proj.reshape(N_TENSOR, chans, PROJ), precision=PRECISE)
    mixed_proj = low_back(lax.optimization_barrier(jnp.sum(low(proj_parts), axis=0)))
    dt_low = low(mixed_proj[:, :DT_RANK])
    b_input = mixed_proj[:, DT_RANK:DT_RANK + STATE]
    c_input = mixed_proj[:, DT_RANK + STATE:]
    step_prod = low_back(jnp.dot(dt_low, dt_proj, precision=PRECISE))
    keep_mask = (reset_row == 0).astype(row_data.dtype)
    gated_out = low(scan_piece(activ, step_prod, dt_bias, decay_log, skip_gain, b_input, c_input, gate_in, keep_mask))
    out_parts = jnp.einsum('lkc,kcd->kld', gated_out.reshape(length, N_TENSOR, chans), out_proj.reshape(N_TENSOR, chans, D), precision=PRECISE)
    mixer_out = low_back(lax.optimization_barrier(jnp.sum(low(out_parts), axis=0)))
    residual = row_data + mixer_out
    send_rows = low(rms_scale(residual, norm_two))
    moe_out = low_back(experts_rows(send_rows, expert_ids, expert_in, expert_out))
    return residual + moe_out

def reference(tokens, resets, routes, norm_one, in_proj, conv_weight, conv_bias, x_proj, dt_proj, dt_bias, decay_log, skip_gain, out_proj, norm_two, expert_in, expert_out, cotangent):
    params = tuple((weight.astype(jnp.float32) for weight in (norm_one, in_proj, conv_weight, conv_bias, x_proj, dt_proj, dt_bias, decay_log, skip_gain, out_proj, norm_two, expert_in, expert_out)))
    row_data = tokens.astype(jnp.float32).reshape(N_DP, SEQ_LEN, D)
    reset_rows = resets.reshape(N_DP, SEQ_LEN)
    route_rows = routes.reshape(N_DP, SEQ_LEN)

    def forward(row_input, weights):

        def one_sequence(entry_tuple):
            return layer_rows(entry_tuple[0], entry_tuple[1], entry_tuple[2], weights)
        return lax.map(jax.checkpoint(one_sequence), (row_input, reset_rows, route_rows))
    outcome, pullback = jax.vjp(forward, row_data, params)
    grad_rows, grads = pullback(cotangent.astype(jnp.float32).reshape(N_DP, SEQ_LEN, D))
    return (outcome.reshape(TOKENS, D).astype(jnp.bfloat16), grad_rows.reshape(TOKENS, D), grads[0], grads[1], grads[2], grads[3], grads[4], grads[5], grads[6], grads[7], grads[8], grads[9], grads[10], grads[11], grads[12])
```

```python
import functools
import math

import jax
import jax.numpy as jnp
from jax import lax
from jax.experimental import pallas as pl
from jax.experimental.pallas import tpu as pltpu
from jax.sharding import PartitionSpec as P

EPSILON = 1e-05
F32 = jnp.float32
BF16 = jnp.bfloat16
NEVER = 1e4
LOG2E = 1.4426950408889634
GELU_SCALE = math.sqrt(2.0 / math.pi)
GELU_CUBE = 0.044715
VMEM_BYTES = 56 * 1024 * 1024
WIDEST_GATHER = 8


def run_kernel(kernel, outs, args, scratch=(), scalars=0):
    return pl.pallas_call(
        kernel,
        out_shape=[jax.ShapeDtypeStruct(shape, dtype) for shape, dtype in outs],
        in_specs=[pl.BlockSpec(memory_space=pltpu.SMEM)] * scalars
        + [pl.BlockSpec(memory_space=pltpu.VMEM)] * (len(args) - scalars),
        out_specs=[pl.BlockSpec(memory_space=pltpu.VMEM)] * len(outs),
        scratch_shapes=[pltpu.VMEM(shape, dtype) for shape, dtype in scratch],
        compiler_params=pltpu.CompilerParams(vmem_limit_bytes=VMEM_BYTES),
    )(*args)


def dot_nn(left, right):
    return lax.dot_general(left, right, (((1,), (0,)), ((), ())), preferred_element_type=F32)


def dot_nt(left, right):
    return lax.dot_general(left, right, (((1,), (1,)), ((), ())), preferred_element_type=F32)


def dot_tn(left, right):
    return lax.dot_general(left, right, (((0,), (0,)), ((), ())), preferred_element_type=F32)


def lane_tiles(column, tiles):
    return jnp.concatenate([column] * tiles, axis=1)


def fold_tiles(values):
    total = values[:, :128]
    for tile in range(1, values.shape[1] // 128):
        total = total + values[:, 128 * tile : 128 * (tile + 1)]
    return total


def wide_masks(masks, index, chans):
    return lane_tiles(masks[index], -(-chans // 128))[:, :chans]


def rms_rate(values):
    return lax.rsqrt(jnp.mean(values * values, axis=-1, keepdims=True) + EPSILON)


def prepare_kernel(
    experts, capacity, block_rows, resets, route_col, route_row, cotangent, masks, choose, slots
):
    length = route_col.shape[0]
    square = (length, length)
    earlier = lax.broadcasted_iota(jnp.int32, square, 0)
    later = lax.broadcasted_iota(jnp.int32, square, 1)
    route_of = jnp.broadcast_to(route_row[...], square)
    same = (jnp.broadcast_to(route_col[...], square) == route_of) & (earlier < later)
    if block_rows < length:
        same = same & (earlier // block_rows == later // block_rows)
    rank = jnp.sum(same.astype(F32), axis=0, keepdims=True).astype(jnp.int32)
    place = route_row[...]
    if block_rows < length:
        place = place + experts * (later[:1] // block_rows)
    slot = place * capacity + rank
    slot_count = choose.shape[0]
    slot_ids = lax.broadcasted_iota(jnp.int32, (slot_count, length), 0)
    chosen = (slot_ids == jnp.broadcast_to(slot, (slot_count, length))).astype(F32).astype(BF16)
    choose[...] = chosen
    slots[...] = dot_nn(chosen, cotangent[...]).astype(BF16)
    keep = jnp.where(jnp.broadcast_to(resets[...], square) == 0, 1.0, 0.0)
    joined = jnp.where(earlier > 0, keep, 0.0)
    one_back = pltpu.roll(joined, 1, 0)
    two_back = pltpu.roll(joined, 2, 0)
    masks[0] = keep
    masks[1] = joined
    masks[2] = joined * one_back
    masks[3] = joined * one_back * two_back


def enter_kernel(
    place,
    piece_0,
    piece_1,
    piece_2,
    piece_3,
    gain,
    in_proj,
    conv_weight,
    conv_bias,
    x_proj,
    masks,
    rows_out,
    share_out,
    inner_out,
    conv_out,
    gate_out,
    mixed_out,
    held,
):
    pieces = (piece_0, piece_1, piece_2, piece_3)
    count = len(pieces)
    for step, piece in enumerate(pieces):
        held[lax.rem(place[0] - step + count, count)] = piece[...].astype(F32)
    rows = jnp.concatenate([held[index] for index in range(count)], axis=1)
    rows_out[...] = rows.astype(BF16)
    normed = (rows * rms_rate(rows) * gain[...]).astype(BF16)
    width = rows.shape[1]
    share_out[:, :width] = normed
    inner = dot_nn(normed, in_proj[0])
    gate_out[...] = dot_nn(normed, in_proj[1])
    chans = inner.shape[1]
    inner_out[...] = inner
    total = conv_bias[...] + conv_weight[3:4, :] * inner
    for shift in (1, 2, 3):
        moved = pltpu.roll(inner, shift, 0) * wide_masks(masks, shift, chans)
        total = total + conv_weight[3 - shift : 4 - shift, :] * moved
    conv_out[...] = total
    act = (total * jax.nn.sigmoid(total)).astype(BF16)
    share_out[:, width : width + chans] = act
    mixed_out[...] = dot_nn(act, x_proj[...]).astype(BF16)


def sum_pieces(place, pieces, held):
    count = len(pieces)
    for step, piece in enumerate(pieces):
        held[lax.rem(place[0] - step + count, count)] = piece[...]
    total = held[0].astype(F32)
    for index in range(1, count):
        total = total + held[index].astype(F32)
    return total


def put_row_chunks(place, source, outs):
    count = len(outs)
    rows = source.shape[0] // count
    for step, out in enumerate(outs):
        start = pl.multiple_of(lax.rem(place[0] + step, count) * rows, rows)
        out[...] = source[pl.ds(start, rows), :].astype(out.dtype)


def take_row_pieces(place, pieces, target):
    count = len(pieces)
    rows = target.shape[0] // count
    for step, piece in enumerate(pieces):
        start = pl.multiple_of(lax.rem(place[0] - step + count, count) * rows, rows)
        target[pl.ds(start, rows), :] = piece[...].astype(target.dtype)


def block_columns(transposed, block):
    length = transposed.shape[1]
    return pltpu.roll(transposed, lax.rem(length - 8 * block, length), 1)


def spread_column(columns, row, tiles):
    return lane_tiles(jnp.broadcast_to(columns[:, row : row + 1], (columns.shape[0], 128)), tiles)


def padded_copy(target, values):
    target[...] = jnp.zeros(target.shape, target.dtype)
    target[:, : values.shape[1]] = values


def softplus(values):
    return jnp.maximum(values, 0.0) + jnp.log1p(jnp.exp(-jnp.abs(values)))


def scan_forward_kernel(
    place,
    piece_0,
    piece_1,
    piece_2,
    piece_3,
    dt_proj,
    dt_bias,
    decay_log,
    skip_gain,
    share,
    gate_in,
    masks,
    out_proj,
    out_0,
    out_1,
    out_2,
    out_3,
    mixed_out,
    share_out,
    y_out,
    held,
    rate,
    step_rows,
    drive_rows,
    y_rows,
    partial,
):
    rank = dt_proj.shape[0]
    states = decay_log.shape[0]
    length, chans = y_out.shape
    tiles = step_rows.shape[1] // 128
    mixed = sum_pieces(place, (piece_0, piece_1, piece_2, piece_3), held)
    padded_copy(mixed_out, mixed)
    dt_low = mixed[:, :rank].astype(BF16)
    step_size = softplus(dot_nn(dt_low, dt_proj[...]) + dt_bias[...])
    act = share[:, share.shape[1] - chans :].astype(F32)
    reset = NEVER * (1.0 - wide_masks(masks, 0, chans))
    padded_copy(rate, -LOG2E * jnp.exp(decay_log[...]))
    padded_copy(step_rows, step_size + reset)
    padded_copy(drive_rows, step_size * act)
    turned = mixed_out[...].T
    b_turned = turned[rank : rank + states]
    c_turned = turned[rank + states : rank + 2 * states]

    def block(index, state):
        start = pl.multiple_of(index * 8, 8)
        b_cols = block_columns(b_turned, index)
        c_cols = block_columns(c_turned, index)
        steps = step_rows[pl.ds(start, 8), :]
        drives = drive_rows[pl.ds(start, 8), :]
        rows = []
        for row in range(8):
            decay = jnp.exp2(rate[...] * steps[row : row + 1])
            state = decay * state + spread_column(b_cols, row, tiles) * drives[row : row + 1]
            rows.append(
                jnp.sum(spread_column(c_cols, row, tiles) * state, axis=0, keepdims=True)
            )
        y_rows[pl.ds(start, 8), :] = jnp.concatenate(rows, axis=0)
        return state

    lax.fori_loop(0, length // 8, block, jnp.zeros((states, 128 * tiles), F32))
    y = y_rows[:, :chans] + skip_gain[...] * act
    y_out[...] = y
    gate = gate_in[...]
    gated = (y * (gate * jax.nn.sigmoid(gate))).astype(BF16)
    share_out[...] = jnp.zeros(share_out.shape, BF16)
    share_out[:, :chans] = gated
    share_out[:, 128 * tiles : 128 * tiles + rank] = dt_low
    partial[...] = dot_nn(gated, out_proj[...])
    put_row_chunks(place, partial, (out_0, out_1, out_2, out_3))


def dispatch_kernel(
    place,
    piece_0,
    piece_1,
    piece_2,
    piece_3,
    rows_in,
    gain,
    choose,
    residual_out,
    columns_out,
    slots,
    held,
):
    take_row_pieces(place, (piece_0, piece_1, piece_2, piece_3), residual_out)
    residual = rows_in[...].astype(F32) + residual_out[...]
    residual_out[...] = residual
    width = columns_out.shape[1]
    for index in range(held.shape[0]):
        held[index] = residual[:, index * width : (index + 1) * width]
    columns_out[...] = held[place[0]]
    send = (residual * rms_rate(residual) * gain[...]).astype(BF16)
    slots[...] = dot_nn(choose[...], send).astype(BF16)


def hidden_back_kernel(grad_slots, second_w, d_hidden):
    d_hidden[...] = dot_nn(grad_slots[...], second_w[...])


def expert_kernel(arrived, first_w, d_hidden, hidden_out, d_pre_out, d_slots):
    value = dot_nn(arrived[...], first_w[...])
    square = value * value
    bend = jnp.tanh(GELU_SCALE * (value + GELU_CUBE * value * square))
    half = 0.5 * (1.0 + bend)
    hidden_out[...] = (value * half).astype(BF16)
    slope = half + 0.5 * value * (1.0 - bend * bend) * GELU_SCALE * (
        1.0 + 3.0 * GELU_CUBE * square
    )
    d_pre = (slope * d_hidden[...]).astype(BF16)
    d_pre_out[...] = d_pre
    d_slots[...] = dot_nt(d_pre, first_w[...]).astype(BF16)


def expert_grads_kernel(arrived, grad_slots, hidden, d_pre, second_w, first_out, second_out, moe):
    first_out[...] = dot_tn(arrived[...], d_pre[...]).astype(BF16)
    second_out[...] = dot_tn(grad_slots[...], hidden[...]).astype(BF16)
    moe[...] = dot_nt(hidden[...], second_w[...]).astype(BF16)


def back_rows_kernel(place, choose, slots, out_0, out_1, out_2, out_3, partial):
    partial[...] = dot_tn(choose[...], slots[...])
    put_row_chunks(place, partial, (out_0, out_1, out_2, out_3))


def back_columns_kernel(place, choose, slots, out_0, out_1, out_2, out_3, held):
    rows = dot_tn(choose[...], slots[...])
    put_column_chunks(place, rows, (out_0, out_1, out_2, out_3), held)


def put_column_chunks(place, rows, outs, held):
    count = len(outs)
    width = rows.shape[1] // count
    for index in range(count):
        held[index] = rows[:, index * width : (index + 1) * width]
    for step, out in enumerate(outs):
        out[:, :width] = held[lax.rem(place[0] + step, count)].astype(out.dtype)


def mixer_grad_kernel(
    place,
    piece_0,
    piece_1,
    piece_2,
    piece_3,
    residual_in,
    gain,
    cotangent,
    out_proj,
    columns_out,
    mix_out,
    d_gated,
    gain_grad,
    d_send,
    held,
):
    take_row_pieces(place, (piece_0, piece_1, piece_2, piece_3), d_send)
    residual = residual_in[...]
    inverse = rms_rate(residual)
    scaled = residual * inverse
    grad = d_send[...]
    gain_grad[...] = jnp.sum(grad * scaled, axis=0, keepdims=True)
    pulled = grad * gain[...]
    along = jnp.mean(pulled * scaled, axis=-1, keepdims=True)
    d_residual = cotangent[...].astype(F32) + inverse * (pulled - scaled * along)
    width = columns_out.shape[1]
    for index in range(held.shape[0]):
        held[index] = d_residual[:, index * width : (index + 1) * width]
    columns_out[...] = held[place[0]]
    d_mix = d_residual.astype(BF16)
    mix_out[...] = d_mix
    d_gated[...] = dot_nt(d_mix, out_proj[...])


def scan_backward_kernel(
    d_gated,
    y_in,
    gate_in,
    share,
    mixed_in,
    masks,
    dt_proj,
    dt_bias,
    decay_log,
    skip_gain,
    d_mixed_out,
    d_act_out,
    share_out,
    small_out,
    rate,
    step_rows,
    decay_rows,
    drive_rows,
    dy_rows,
    du_rows,
    dl_rows,
    decays,
    history,
):
    rank = dt_proj.shape[0]
    states = decay_log.shape[0]
    length, chans = y_in.shape
    tiles = step_rows.shape[1] // 128
    full = 128 * tiles
    dt_low = mixed_in[:, :rank].astype(BF16)
    raw_step = dot_nn(dt_low, dt_proj[...]) + dt_bias[...]
    step_size = softplus(raw_step)
    act = share[:, share.shape[1] - chans :].astype(F32)
    reset = NEVER * (1.0 - wide_masks(masks, 0, chans))
    padded_copy(rate, -jnp.exp(decay_log[...]))
    padded_copy(step_rows, step_size)
    padded_copy(decay_rows, LOG2E * (step_size + reset))
    padded_copy(drive_rows, step_size * act)
    gate = gate_in[...]
    gate_sig = jax.nn.sigmoid(gate)
    d_out = d_gated[...]
    d_y = d_out * (gate * gate_sig)
    padded_copy(dy_rows, d_y)
    d_gate = d_out * y_in[...] * gate_sig * (1.0 + gate * (1.0 - gate_sig))
    turned = mixed_in[...].T
    b_turned = turned[rank : rank + states]
    c_turned = turned[rank + states : rank + 2 * states]
    history[pl.ds(0, states), :] = jnp.zeros((states, full), F32)

    def forward_block(index, state):
        start = pl.multiple_of(index * 8, 8)
        b_cols = block_columns(b_turned, index)
        steps = decay_rows[pl.ds(start, 8), :]
        drives = drive_rows[pl.ds(start, 8), :]
        for row in range(8):
            decay = jnp.exp2(rate[...] * steps[row : row + 1])
            state = decay * state + spread_column(b_cols, row, tiles) * drives[row : row + 1]
            at = pl.multiple_of((start + row) * states, states)
            decays[pl.ds(at, states), :] = decay
            history[pl.ds(at + states, states), :] = state
        return state

    lax.fori_loop(0, length // 8, forward_block, jnp.zeros((states, full), F32))
    lanes = lax.broadcasted_iota(jnp.int32, (states, length), 1)

    def backward_block(count, carry):
        carried, d_rate, d_b, d_c = carry
        index = length // 8 - 1 - count
        start = pl.multiple_of(index * 8, 8)
        b_cols = block_columns(b_turned, index)
        c_cols = block_columns(c_turned, index)
        steps = step_rows[pl.ds(start, 8), :]
        drives = drive_rows[pl.ds(start, 8), :]
        dys = dy_rows[pl.ds(start, 8), :]
        du = [None] * 8
        dl = [None] * 8
        for row in reversed(range(8)):
            at = pl.multiple_of((start + row) * states, states)
            before = history[pl.ds(at, states), :]
            after = history[pl.ds(at + states, states), :]
            decay = decays[pl.ds(at, states), :]
            here = lanes == start + row
            dy_row = jnp.broadcast_to(dys[row : row + 1], (states, full))
            grad = spread_column(c_cols, row, tiles) * dy_row + carried
            c_part = jnp.sum(fold_tiles(dy_row * after), axis=1, keepdims=True)
            d_c = jnp.where(here, c_part, d_c)
            b_part = jnp.sum(fold_tiles(grad * drives[row : row + 1]), axis=1, keepdims=True)
            d_b = jnp.where(here, b_part, d_b)
            du[row] = jnp.sum(grad * spread_column(b_cols, row, tiles), axis=0, keepdims=True)
            carried = grad * decay
            d_log = carried * before
            dl[row] = jnp.sum(d_log * rate[...], axis=0, keepdims=True)
            d_rate = d_rate + d_log * steps[row : row + 1]
        du_rows[pl.ds(start, 8), :] = jnp.concatenate(du, axis=0)
        dl_rows[pl.ds(start, 8), :] = jnp.concatenate(dl, axis=0)
        return carried, d_rate, d_b, d_c

    nothing = jnp.zeros((states, full), F32)
    thin = jnp.zeros((states, length), F32)
    _, d_rate, d_b, d_c = lax.fori_loop(
        0, length // 8, backward_block, (nothing, nothing, thin, thin)
    )
    du = du_rows[:, :chans]
    d_act_out[...] = du * step_size + skip_gain[...] * d_y
    d_step = (dl_rows[:, :chans] + du * act) * jax.nn.sigmoid(raw_step)
    d_step_low = d_step.astype(BF16)
    share_out[:length] = d_gate.astype(BF16)
    share_out[length:] = d_step_low
    small_out[...] = jnp.zeros(small_out.shape, F32)
    small_out[:states] = (d_rate * rate[...])[:, :chans]
    small_out[states : states + 1] = jnp.sum(d_step, axis=0, keepdims=True)
    small_out[states + 1 : states + 2] = jnp.sum(d_y * act, axis=0, keepdims=True)
    low_turned = dot_nt(dt_proj[...], d_step_low)
    used = rank + 2 * states
    d_turned = jnp.concatenate(
        [low_turned, d_b, d_c, jnp.zeros((128 - used, length), F32)], axis=0
    )
    d_mixed_out[...] = d_turned.T[:, :used].astype(BF16)


def leave_kernel(
    place,
    piece_0,
    piece_1,
    piece_2,
    piece_3,
    d_act_scan,
    d_gate,
    conv_in,
    inner_in,
    masks,
    x_proj,
    conv_weight,
    in_proj,
    rows_in,
    gain,
    small_in,
    gain_two,
    out_0,
    out_1,
    out_2,
    out_3,
    message,
    held,
    held_columns,
):
    length, chans = inner_in.shape
    width = gain.shape[1]
    d_mixed = sum_pieces(place, (piece_0, piece_1, piece_2, piece_3), held).astype(BF16)
    d_act = d_act_scan[...] + dot_nt(d_mixed, x_proj[...])
    conv = conv_in[...]
    sig = jax.nn.sigmoid(conv)
    d_conv = d_act * sig * (1.0 + conv * (1.0 - sig))
    inner = inner_in[...]
    d_inner = conv_weight[3:4, :] * d_conv
    weight_grads = [jnp.sum(d_conv * inner, axis=0, keepdims=True)]
    for shift in (1, 2, 3):
        masked = d_conv * wide_masks(masks, shift, chans)
        weight_grads.append(
            jnp.sum(masked * pltpu.roll(inner, shift, 0), axis=0, keepdims=True)
        )
        d_inner = d_inner + conv_weight[3 - shift : 4 - shift, :] * pltpu.roll(
            masked, length - shift, 0
        )
    d_inner_low = d_inner.astype(BF16)
    message[...] = jnp.zeros(message.shape, BF16)
    message[:length, :chans] = d_inner_low
    lane = -(-chans // 128) * 128
    message[:length, lane : lane + d_mixed.shape[1]] = d_mixed
    d_normed = dot_nt(d_inner_low, in_proj[0]) + dot_nt(d_gate[:length], in_proj[1])
    rows = rows_in[...].astype(F32)
    scaled = rows * rms_rate(rows)
    norm_grad = jnp.sum(d_normed * scaled, axis=0, keepdims=True)
    along = jnp.mean(d_normed * gain[...] * scaled, axis=-1, keepdims=True)
    outs = (out_0, out_1, out_2, out_3)
    put_column_chunks(place, d_normed, outs, held_columns)
    column = width // len(outs)
    high = along.astype(BF16)
    for out in outs:
        out[:, column : column + 1] = high
        out[:, column + 1 : column + 2] = (along - high.astype(F32)).astype(BF16)
    small = small_in[...]
    states = 16
    sent = jnp.concatenate(
        [
            small[: states + 2],
            weight_grads[3],
            weight_grads[2],
            weight_grads[1],
            weight_grads[0],
            jnp.sum(d_conv, axis=0, keepdims=True),
            norm_grad[:, :chans],
            norm_grad[:, chans:],
            gain_two[:, :chans],
            gain_two[:, chans:],
            jnp.zeros((5, chans), F32),
        ],
        axis=0,
    )
    upper = sent.astype(BF16)
    message[length : length + 32, :chans] = upper
    message[length + 32 : length + 64, :chans] = (sent - upper.astype(F32)).astype(BF16)


def finish_rows_kernel(
    piece_0, piece_1, piece_2, piece_3, d_columns, tokens, scale, gain, grad_tokens
):
    width = tokens.shape[1]
    total = piece_0[...].astype(F32)
    for piece in (piece_1, piece_2, piece_3):
        total = total + piece[...].astype(F32)
    along = total[:, width : width + 1] + total[:, width + 1 : width + 2]
    inverse = scale[:, :1]
    pulled = total[:, :width] * gain[...]
    scaled = tokens[...].astype(F32) * inverse
    grad_tokens[...] = d_columns[...] + inverse * (pulled - scaled * along)


def send_chunks(chunks):
    count = len(chunks)
    pairs = [[(i, (i + s) % count) for i in range(count)] for s in range(count)]
    return [chunks[0]] + [lax.ppermute(chunks[s], "tensor", pairs[s]) for s in range(1, count)]


def share_rows(values, count):
    return send_chunks([values] * count)


def add_low(pieces):
    total = pieces[0].astype(F32)
    for piece in pieces[1:]:
        total = total + piece.astype(F32)
    return total.astype(BF16)


def near_gather(values, groups):
    def swap(array, bits):
        return lax.ppermute(array, "dp", [(i, i ^ bits) for i in range(groups)])

    far = [values] + [swap(values, bits) for bits in range(2, groups, 2)]
    near = [swap(piece, 1) for piece in far]
    order = [None] * groups
    for index, (piece, other) in enumerate(zip(far, near)):
        order[2 * index] = piece
        order[2 * index + 1] = other
    return order


def body(
    tokens,
    resets,
    routes,
    norm_one,
    in_proj,
    conv_weight,
    conv_bias,
    x_proj,
    dt_proj,
    dt_bias,
    decay_log,
    skip_gain,
    out_proj,
    norm_two,
    expert_in,
    expert_out,
    cotangent,
):
    groups = lax.axis_size("dp")
    parts = lax.axis_size("tensor")
    place = lax.axis_index("tensor").astype(jnp.int32).reshape(1)
    length, column = tokens.shape
    width = norm_one.shape[0]
    rank, chans = dt_proj.shape
    states = decay_log.shape[0]
    experts, share, hidden_units = expert_in.shape
    proj = x_proj.shape[1]
    tile_count = groups // experts
    block_rows = length * experts // groups
    capacity = max(2, block_rows // 4)
    slot_count = groups * capacity
    full = -(-chans // 128) * 128
    tiles = full // 128
    gain_one = norm_one.reshape(1, width)
    gain_two = norm_two.reshape(1, width)
    bias_row = conv_bias.reshape(1, chans)
    dt_row = dt_bias.reshape(1, chans)
    skip_row = skip_gain.reshape(1, chans)

    def exchange(values):
        return lax.all_to_all(values, "dp", split_axis=0, concat_axis=0, tiled=True)

    first_w = exchange(jnp.tile(expert_in, (tile_count, 1, 1))).reshape(width, hidden_units)
    second_w = exchange(jnp.tile(expert_out, (tile_count, 1, 1))).reshape(width, hidden_units)

    token_pieces = share_rows(tokens, parts)
    masks, choose, grad_send = run_kernel(
        functools.partial(prepare_kernel, experts, capacity, block_rows),
        [
            ((4, length, 128), F32),
            ((slot_count, length), BF16),
            ((slot_count, width), BF16),
        ],
        [resets.reshape(length, 1), routes, routes.reshape(1, length), cotangent],
    )
    grad_slots = exchange(grad_send.reshape(groups, capacity, width)).reshape(slot_count, width)

    rows, share_one, inner, conv, gate, mixed_part = run_kernel(
        enter_kernel,
        [
            ((length, width), BF16),
            ((length, width + chans), BF16),
            ((length, chans), F32),
            ((length, chans), F32),
            ((length, chans), F32),
            ((length, proj), BF16),
        ],
        [place, *token_pieces, gain_one, in_proj, conv_weight, bias_row, x_proj, masks],
        [((parts, length, column), F32)],
        scalars=1,
    )
    mixed_pieces = share_rows(mixed_part, parts)
    *mix_chunks, mixed, share_two, y = run_kernel(
        scan_forward_kernel,
        [((length // parts, width), BF16)] * parts
        + [
            ((length, 128), F32),
            ((length, full + 128), BF16),
            ((length, chans), F32),
        ],
        [
            place,
            *mixed_pieces,
            dt_proj,
            dt_row,
            decay_log,
            skip_row,
            share_one,
            gate,
            masks,
            out_proj,
        ],
        [
            ((parts, length, proj), BF16),
            ((states, full), F32),
            ((length, full), F32),
            ((length, full), F32),
            ((length, full), F32),
            ((length, width), F32),
        ],
        scalars=1,
    )
    mixer_pieces = share_rows(add_low(send_chunks(mix_chunks)), parts)
    residual, residual_columns, send_slots = run_kernel(
        dispatch_kernel,
        [
            ((length, width), F32),
            ((length, column), F32),
            ((slot_count, width), BF16),
        ],
        [place, *mixer_pieces, rows, gain_two, choose],
        [((parts, length, column), F32)],
        scalars=1,
    )
    arrived = exchange(send_slots.reshape(groups, capacity, width)).reshape(slot_count, width)
    (d_hidden,) = run_kernel(
        hidden_back_kernel, [((slot_count, hidden_units), F32)], [grad_slots, second_w]
    )
    hidden, d_pre, d_slots = run_kernel(
        expert_kernel,
        [
            ((slot_count, hidden_units), BF16),
            ((slot_count, hidden_units), BF16),
            ((slot_count, width), BF16),
        ],
        [arrived, first_w, d_hidden],
    )
    back_slots = exchange(d_slots.reshape(groups, capacity, width)).reshape(slot_count, width)
    grad_first, grad_second, moe_slots = run_kernel(
        expert_grads_kernel,
        [
            ((width, hidden_units), BF16),
            ((width, hidden_units), BF16),
            ((slot_count, width), BF16),
        ],
        [arrived, grad_slots, hidden, d_pre, second_w],
    )
    back_chunks = run_kernel(
        back_rows_kernel,
        [((length // parts, width), BF16)] * parts,
        [place, choose, back_slots],
        [((length, width), F32)],
        scalars=1,
    )
    send_pieces = share_rows(add_low(send_chunks(back_chunks)), parts)
    d_columns, d_mix, d_gated, gain_grad_two = run_kernel(
        mixer_grad_kernel,
        [
            ((length, column), F32),
            ((length, width), BF16),
            ((length, chans), F32),
            ((1, width), F32),
        ],
        [place, *send_pieces, residual, gain_two, cotangent, out_proj],
        [((length, width), F32), ((parts, length, column), F32)],
        scalars=1,
    )
    d_mixed_part, d_act_scan, share_three, small = run_kernel(
        scan_backward_kernel,
        [
            ((length, proj), BF16),
            ((length, chans), F32),
            ((2 * length, chans), BF16),
            ((24, chans), F32),
        ],
        [
            d_gated,
            y,
            gate,
            share_one,
            mixed,
            masks,
            dt_proj,
            dt_row,
            decay_log,
            skip_row,
        ],
        [
            ((states, full), F32),
            ((length, full), F32),
            ((length, full), F32),
            ((length, full), F32),
            ((length, full), F32),
            ((length, full), F32),
            ((length, full), F32),
            ((length * states, full), F32),
            (((length + 1) * states, full), F32),
        ],
    )
    d_mixed_pieces = share_rows(d_mixed_part, parts)
    *normed_chunks, message = run_kernel(
        leave_kernel,
        [((length, column + 2), BF16)] * parts + [((length + 64, full + 128), BF16)],
        [
            place,
            *d_mixed_pieces,
            d_act_scan,
            share_three,
            conv,
            inner,
            masks,
            x_proj,
            conv_weight,
            in_proj,
            rows,
            gain_one,
            small,
            gain_grad_two,
        ],
        [((parts, length, proj), BF16), ((parts, length, column), F32)],
        scalars=1,
    )
    normed_pieces = send_chunks(normed_chunks)
    row_scale = rms_rate(rows.astype(F32))
    gain_columns = lax.dynamic_slice_in_dim(gain_one, place[0] * column, column, 1)
    (grad_tokens,) = run_kernel(
        finish_rows_kernel,
        [((length, column), F32)],
        [*normed_pieces, d_columns, tokens, jnp.broadcast_to(row_scale, (length, 128)), gain_columns],
    )

    returned = exchange(moe_slots.reshape(groups, capacity, width)).reshape(slot_count, width)
    moe_chunks = run_kernel(
        back_columns_kernel,
        [((length, column), BF16)] * parts,
        [place, choose, returned],
        [((parts, length, column), F32)],
        scalars=1,
    )
    moe_pieces = send_chunks(moe_chunks)
    outcome = residual_columns
    for piece in moe_pieces:
        outcome = outcome + piece.astype(F32)
    outcome = outcome.astype(BF16)

    def owner_sum(values):
        got = exchange(values.reshape(groups, share, hidden_units)).astype(F32)
        return jnp.sum(got.reshape(tile_count, experts, share, hidden_units), axis=0)

    grad_expert_in = owner_sum(grad_first)
    grad_expert_out = owner_sum(grad_second)

    if groups <= WIDEST_GATHER:
        def gather(values):
            return lax.all_gather(values, "dp", axis=0, tiled=True)

        all_one = gather(share_one)
        all_two = gather(share_two)
        all_mix = gather(d_mix)
        all_three = lax.all_gather(share_three, "dp", axis=0, tiled=False)
        all_gate = all_three[:, :length].reshape(groups * length, chans)
        all_step = all_three[:, length:].reshape(groups * length, chans)
        grad_out_proj = dot_tn(all_two[:, :chans], all_mix)
        grad_dt_proj = dot_tn(all_two[:, full : full + rank], all_step)
        all_message = lax.all_gather(message, "dp", axis=0, tiled=False)
        all_inner = all_message[:, :length, :chans].reshape(groups * length, chans)
        all_mixed = all_message[:, :length, full : full + proj].reshape(groups * length, proj)
        grad_in_proj = jnp.stack(
            [dot_tn(all_one[:, :width], all_inner), dot_tn(all_one[:, :width], all_gate)]
        )
        grad_x_proj = dot_tn(all_one[:, width:], all_mixed)
        sent = jnp.sum(all_message[:, length:, :chans].astype(F32), axis=0)
        vectors = sent[:32] + sent[32:]
    else:
        d_inner = message[:length, :chans]
        d_mixed = message[:length, full : full + proj]
        sent = message[length:, :chans].astype(F32)
        grad_in_proj, grad_x_proj, grad_dt_proj, grad_out_proj, vectors = lax.psum(
            (
                jnp.stack(
                    [
                        dot_tn(share_one[:, :width], d_inner),
                        dot_tn(share_one[:, :width], share_three[:length]),
                    ]
                ),
                dot_tn(share_one[:, width:], d_mixed),
                dot_tn(share_two[:, full : full + rank], share_three[length:]),
                dot_tn(share_two[:, :chans], d_mix),
                sent[:32] + sent[32:],
            ),
            "dp",
        )
    first_vector = states + 2
    norm_part = vectors[first_vector + 5 : first_vector + 7].reshape(width)
    grad_norm_one = sum(share_rows(norm_part.reshape(1, width), parts)).reshape(width)
    grad_norm_two = vectors[first_vector + 7 : first_vector + 9].reshape(width)
    return (
        outcome,
        grad_tokens,
        grad_norm_one,
        grad_in_proj,
        vectors[first_vector : first_vector + 4],
        vectors[first_vector + 4],
        grad_x_proj,
        grad_dt_proj,
        vectors[states],
        vectors[:states],
        vectors[states + 1],
        grad_out_proj,
        grad_norm_two,
        grad_expert_in,
        grad_expert_out,
    )


def solution(mesh):
    placed = (
        P("dp", "tensor"),
        P("dp"),
        P("dp", None),
        P(),
        P(None, None, "tensor"),
        P(None, "tensor"),
        P("tensor"),
        P("tensor", None),
        P(None, "tensor"),
        P("tensor"),
        P(None, "tensor"),
        P("tensor"),
        P("tensor", None),
        P(),
        P(None, "dp", "tensor"),
        P(None, "dp", "tensor"),
        P("dp", None),
    )
    return jax.shard_map(
        body,
        mesh=mesh,
        in_specs=placed,
        out_specs=(
            P("dp", "tensor"),
            P("dp", "tensor"),
            P(),
            P(None, None, "tensor"),
            P(None, "tensor"),
            P("tensor"),
            P("tensor", None),
            P(None, "tensor"),
            P("tensor"),
            P(None, "tensor"),
            P("tensor"),
            P("tensor", None),
            P(),
            P(None, "dp", "tensor"),
            P(None, "dp", "tensor"),
        ),
        check_vma=False,
    )
```

```python
import functools
import math

import jax
import jax.numpy as jnp
from jax import lax
from jax.experimental import pallas as pl
from jax.experimental.pallas import tpu as pltpu
from jax.sharding import PartitionSpec as P

EPSILON = 1e-05
F32 = jnp.float32
BF16 = jnp.bfloat16
NEVER = 1e4
LOG2E = 1.4426950408889634
GELU_SCALE = math.sqrt(2.0 / math.pi)
GELU_CUBE = 0.044715
VMEM_BYTES = 56 * 1024 * 1024
NEAR_GROUPS = 8
VECTORS_ONE = 24
VECTORS_TWO = 8


def run_kernel(kernel, outs, args, scratch=(), scalars=0, far_args=(), far_outs=(), alias=None):
    def spec(index, far):
        return pl.BlockSpec(memory_space=pl.ANY if index in far else pltpu.VMEM)

    return pl.pallas_call(
        kernel,
        out_shape=[jax.ShapeDtypeStruct(shape, dtype) for shape, dtype in outs],
        in_specs=[
            pl.BlockSpec(memory_space=pltpu.SMEM) if index < scalars else spec(index, far_args)
            for index in range(len(args))
        ],
        out_specs=[spec(index, far_outs) for index in range(len(outs))],
        scratch_shapes=[
            shape if not isinstance(shape, tuple) else pltpu.VMEM(*shape) for shape in scratch
        ],
        input_output_aliases=alias or {},
        compiler_params=pltpu.CompilerParams(vmem_limit_bytes=VMEM_BYTES),
    )(*args)


def dot_nn(left, right):
    return lax.dot_general(left, right, (((1,), (0,)), ((), ())), preferred_element_type=F32)


def dot_nt(left, right):
    return lax.dot_general(left, right, (((1,), (1,)), ((), ())), preferred_element_type=F32)


def dot_tn(left, right):
    return lax.dot_general(left, right, (((0,), (0,)), ((), ())), preferred_element_type=F32)


def lane_tiles(column, tiles):
    return jnp.concatenate([column] * tiles, axis=1)


def fold_tiles(values):
    total = values[:, :128]
    for tile in range(1, values.shape[1] // 128):
        total = total + values[:, 128 * tile : 128 * (tile + 1)]
    return total


def wide_masks(masks, index, chans):
    return lane_tiles(masks[index], -(-chans // 128))[:, :chans]


def rms_rate(values):
    return lax.rsqrt(jnp.mean(values * values, axis=-1, keepdims=True) + EPSILON)


def as_row(ref):
    return ref[...].reshape(1, ref.shape[0])


def softplus(values):
    return jnp.maximum(values, 0.0) + jnp.log1p(jnp.exp(-jnp.abs(values)))


def padded_copy(target, values):
    target[...] = jnp.zeros(target.shape, target.dtype)
    target[:, : values.shape[1]] = values


def put_row_chunks(place, source, outs):
    count = len(outs)
    rows = source.shape[0] // count
    for step, out in enumerate(outs):
        start = pl.multiple_of(lax.rem(place[0] + step, count) * rows, rows)
        out[pl.ds(0, rows), :] = source[pl.ds(start, rows), :].astype(out.dtype)


def take_row_pieces(place, pieces, target):
    count = len(pieces)
    rows = target.shape[0] // count
    for step, piece in enumerate(pieces):
        start = pl.multiple_of(lax.rem(place[0] - step + count, count) * rows, rows)
        target[pl.ds(start, rows), :] = piece[...].astype(target.dtype)


def sum_pieces(place, pieces, held):
    count = len(pieces)
    for step, piece in enumerate(pieces):
        held[lax.rem(place[0] - step + count, count)] = piece[...]
    total = held[0].astype(F32)
    for index in range(1, count):
        total = total + held[index].astype(F32)
    return total


def run_copies(copies, semaphores):
    started = []
    for index, (source, target) in enumerate(copies):
        copy = pltpu.make_async_copy(source, target, semaphores.at[index])
        copy.start()
        started.append(copy)
    return started


def fill_masks(resets, masks):
    length = resets.shape[1]
    square = (length, length)
    earlier = lax.broadcasted_iota(jnp.int32, square, 0)
    reset = jnp.broadcast_to(resets[...].astype(F32), square).T
    keep = jnp.where(reset == 0.0, 1.0, 0.0)
    joined = jnp.where(earlier > 0, keep, 0.0)
    one_back = pltpu.roll(joined, 1, 0)
    two_back = pltpu.roll(joined, 2, 0)
    masks[0] = keep
    masks[1] = joined
    masks[2] = joined * one_back
    masks[3] = joined * one_back * two_back


def fill_choose(capacity, block_rows, experts, routes, choose):
    length = routes.shape[1]
    square = (length, length)
    earlier = lax.broadcasted_iota(jnp.int32, square, 0)
    later = lax.broadcasted_iota(jnp.int32, square, 1)
    route_of = jnp.broadcast_to(routes[...].astype(F32), square)
    same = (route_of.T == route_of) & (earlier < later)
    if block_rows < length:
        same = same & (earlier // block_rows == later // block_rows)
    rank = jnp.sum(jnp.where(same, 1.0, 0.0), axis=0, keepdims=True).astype(jnp.int32)
    group = routes[...]
    if block_rows < length:
        group = group + experts * (later[:1] // block_rows)
    slot = group * capacity + rank
    slot_count = choose.shape[0]
    slot_ids = lax.broadcasted_iota(jnp.int32, (slot_count, length), 0)
    hit = slot_ids == jnp.broadcast_to(slot, (slot_count, length))
    choose[...] = jnp.where(hit, 1.0, 0.0).astype(BF16)


def prepare_kernel(
    experts, capacity, block_rows, resets, routes, cotangent, masks, choose, slots
):
    fill_masks(resets, masks)
    fill_choose(capacity, block_rows, experts, routes, choose)
    slots[...] = dot_nn(choose[...], cotangent[...]).astype(BF16)


def put_folded(target, slots):
    rows, width = slots.shape
    units = target.shape[1]
    half = rows // 2
    rest = width - units
    target[:rows, :] = slots[:, :units]
    target[rows:, :rest] = slots[:half, units:]
    target[rows:, rest:] = slots[half:, units:]


def unfold_copies(source, target, top, rows):
    units = source.shape[1]
    half = rows // 2
    rest = target.shape[1] - units
    copies = [(source.at[pl.ds(0, rows)], target.at[pl.ds(top, rows), pl.ds(0, units)])]
    for part in range(2):
        copies.append(
            (
                source.at[pl.ds(rows, half), pl.ds(part * rest, rest)],
                target.at[pl.ds(top + part * half, half), pl.ds(units, rest)],
            )
        )
    return copies


def pack_kernel(
    capacity,
    resets,
    routes,
    cotangent,
    expert_in,
    expert_out,
    masks,
    choose,
    message,
    packed,
    semaphores,
):
    experts, share, units = expert_in.shape
    length, width = cotangent.shape
    copies = []
    for index in range(experts):
        target = message.at[index]
        copies.append((expert_in.at[index], target.at[pl.ds(0, share)]))
        copies.append((expert_out.at[index], target.at[pl.ds(share, share)]))
    started = run_copies(copies, semaphores)
    fill_choose(capacity, length, experts, routes, choose)
    slots = dot_nn(choose[...], cotangent[...]).astype(BF16)
    copies = []
    for index in range(experts):
        put_folded(packed.at[index], slots[index * capacity : (index + 1) * capacity])
        target = message.at[index]
        copies.append((packed.at[index], target.at[pl.ds(2 * share, packed.shape[1])]))
    started += run_copies(copies, semaphores.at[pl.ds(2 * experts, experts)])
    fill_masks(resets, masks)
    for copy in started:
        copy.wait()


def unpack_kernel(share, capacity, message, first_w, second_w, grad_slots, d_hidden, semaphores):
    folded = capacity + capacity // 2
    copies = []
    for index in range(message.shape[0]):
        piece = message.at[index]
        rows = pl.ds(index * share, share)
        copies.append((piece.at[pl.ds(share, share)], second_w.at[rows]))
        copies += unfold_copies(
            piece.at[pl.ds(2 * share, folded)], grad_slots, index * capacity, capacity
        )
        copies.append((piece.at[pl.ds(0, share)], first_w.at[rows]))
    for copy in run_copies(copies, semaphores):
        copy.wait()
    d_hidden[...] = dot_nn(grad_slots[...], second_w[...])


def put_blocks(target, values):
    length = values.shape[0]
    for start in range(0, values.shape[1], 128):
        target[start : start + length, :] = values[:, start : start + 128]


def enter_kernel(
    place,
    piece_0,
    piece_1,
    piece_2,
    piece_3,
    gain_ref,
    in_proj,
    conv_weight,
    conv_bias,
    x_proj,
    masks,
    rows_out,
    normed_out,
    act_out,
    inner_out,
    conv_out,
    gate_out,
    scale_out,
    gain_out,
    mixed_out,
    turned,
):
    take_row_pieces(place, (piece_0, piece_1, piece_2, piece_3), turned)
    rows = turned[...].T
    gain = as_row(gain_ref)
    rows_out[...] = rows.astype(BF16)
    normed = (rows * rms_rate(rows) * gain).astype(BF16)
    put_blocks(normed_out, normed)
    inner = dot_nt(normed, in_proj[0])
    chans = inner.shape[1]
    inner_out[...] = inner
    total = as_row(conv_bias) + conv_weight[3:4, :] * inner
    for shift in (1, 2, 3):
        moved = pltpu.roll(inner, shift, 0) * wide_masks(masks, shift, chans)
        total = total + conv_weight[3 - shift : 4 - shift, :] * moved
    conv_out[...] = total
    act = (total * jax.nn.sigmoid(total)).astype(BF16)
    act_out[...] = act
    mixed_out[...] = dot_nt(x_proj[...], act).astype(BF16)
    gate_out[...] = dot_nt(normed, in_proj[1])
    raw = turned[...]
    scale_out[...] = lax.rsqrt(jnp.mean(raw * raw, axis=0, keepdims=True) + EPSILON)
    turned[...] = jnp.broadcast_to(gain, rows.shape).T
    column = gain_out.shape[0]
    gain_out[...] = turned[pl.ds(pl.multiple_of(place[0] * column, column), column), :]


def block_columns(transposed, block):
    length = transposed.shape[1]
    return pltpu.roll(transposed, lax.rem(length - 8 * block, length), 1)


def spread_column(columns, row, tiles):
    return lane_tiles(jnp.broadcast_to(columns[:, row : row + 1], (columns.shape[0], 128)), tiles)


def scan_forward_kernel(
    place,
    piece_0,
    piece_1,
    piece_2,
    piece_3,
    dt_proj,
    dt_bias,
    decay_log,
    skip_gain,
    act_in,
    gate_in,
    masks,
    out_proj,
    normed,
    out_0,
    out_1,
    out_2,
    out_3,
    mixed_out,
    share_out,
    y_out,
    held,
    rate,
    step_rows,
    drive_rows,
    y_rows,
    partial,
):
    rank = dt_proj.shape[0]
    states = decay_log.shape[0]
    length, chans = y_out.shape
    tiles = step_rows.shape[1] // 128
    mixed = sum_pieces(place, (piece_0, piece_1, piece_2, piece_3), held)
    mixed_out[...] = mixed
    step_size = softplus(dot_tn(mixed[:rank].astype(BF16), dt_proj[...]) + as_row(dt_bias))
    act = act_in[...].astype(F32)
    reset = NEVER * (1.0 - wide_masks(masks, 0, chans))
    padded_copy(rate, -LOG2E * jnp.exp(decay_log[...]))
    padded_copy(step_rows, step_size + reset)
    padded_copy(drive_rows, step_size * act)
    b_turned = mixed[rank : rank + states]
    c_turned = mixed[rank + states : rank + 2 * states]

    def block(index, state):
        start = pl.multiple_of(index * 8, 8)
        b_cols = block_columns(b_turned, index)
        c_cols = block_columns(c_turned, index)
        steps = step_rows[pl.ds(start, 8), :]
        drives = drive_rows[pl.ds(start, 8), :]
        rows = []
        for row in range(8):
            decay = jnp.exp2(rate[...] * steps[row : row + 1])
            state = decay * state + spread_column(b_cols, row, tiles) * drives[row : row + 1]
            rows.append(
                jnp.sum(spread_column(c_cols, row, tiles) * state, axis=0, keepdims=True)
            )
        y_rows[pl.ds(start, 8), :] = jnp.concatenate(rows, axis=0)
        return state

    lax.fori_loop(0, length // 8, block, jnp.zeros((states, 128 * tiles), F32))
    y = y_rows[:, :chans] + as_row(skip_gain) * act
    y_out[...] = y
    gate = gate_in[...]
    gated = (y * (gate * jax.nn.sigmoid(gate))).astype(BF16)
    partial[...] = dot_nn(gated, out_proj[...])
    put_row_chunks(place, partial, (out_0, out_1, out_2, out_3))
    width = normed.shape[0]
    share_out[:width] = normed[...]
    padded_copy(step_rows, gated.astype(F32))
    share_out[width : width + chans] = step_rows[...].T[:chans].astype(BF16)
    padded_copy(step_rows, act)
    share_out[width + chans :] = step_rows[...].T[:chans].astype(BF16)


def dispatch_kernel(
    place,
    piece_0,
    piece_1,
    piece_2,
    piece_3,
    rows_in,
    gain,
    choose,
    residual_out,
    columns_out,
    slots,
    turned,
):
    take_row_pieces(place, (piece_0, piece_1, piece_2, piece_3), residual_out)
    residual = rows_in[...].astype(F32) + residual_out[...]
    residual_out[...] = residual
    send = (residual * rms_rate(residual) * as_row(gain)).astype(BF16)
    slots[...] = dot_nn(choose[...], send).astype(BF16)
    turned[...] = residual.T
    column = columns_out.shape[0]
    columns_out[...] = turned[pl.ds(pl.multiple_of(place[0] * column, column), column), :]


def hidden_back_kernel(grad_slots, second_w, d_hidden):
    d_hidden[...] = dot_nn(grad_slots[...], second_w[...])


def expert_kernel(arrived, first_w, d_hidden, hidden_out, d_pre_out, d_slots):
    value = dot_nn(arrived[...], first_w[...])
    square = value * value
    bend = jnp.tanh(GELU_SCALE * (value + GELU_CUBE * value * square))
    half = 0.5 * (1.0 + bend)
    slope = half + 0.5 * value * (1.0 - bend * bend) * GELU_SCALE * (
        1.0 + 3.0 * GELU_CUBE * square
    )
    d_pre = (slope * d_hidden[...]).astype(BF16)
    d_pre_out[...] = d_pre
    d_slots[...] = dot_nt(d_pre, first_w[...]).astype(BF16)
    hidden_out[...] = (value * half).astype(BF16)


def expert_grads_kernel(arrived, grad_slots, hidden, d_pre, second_w, first_out, second_out, moe):
    first_out[...] = dot_tn(arrived[...], d_pre[...]).astype(BF16)
    second_out[...] = dot_tn(grad_slots[...], hidden[...]).astype(BF16)
    moe[...] = dot_nt(hidden[...], second_w[...]).astype(BF16)


def expert_grads_pack_kernel(
    share, capacity, arrived, grad_slots, hidden, d_pre, second_w, message, grads, packed, semaphores
):
    experts = message.shape[0]
    started = []
    for which, (left, right) in enumerate(((arrived, d_pre), (grad_slots, hidden))):
        grads[which] = dot_tn(left[...], right[...]).astype(BF16)
        copies = [
            (
                grads.at[which, pl.ds(index * share, share)],
                message.at[index, pl.ds(which * share, share)],
            )
            for index in range(experts)
        ]
        started += run_copies(copies, semaphores.at[pl.ds(which * experts, experts)])
    moe = dot_nt(hidden[...], second_w[...]).astype(BF16)
    copies = []
    for index in range(experts):
        put_folded(packed.at[index], moe[index * capacity : (index + 1) * capacity])
        copies.append(
            (packed.at[index], message.at[index, pl.ds(2 * share, packed.shape[1])])
        )
    started += run_copies(copies, semaphores.at[pl.ds(2 * experts, experts)])
    for copy in started:
        copy.wait()


def owner_kernel(share, message, first_out, second_out, low, wide, arrivals, semaphores):
    count = message.shape[0]
    arriving = run_copies(
        [(message.at[index, pl.ds(0, 2 * share)], low.at[index]) for index in range(count)],
        arrivals,
    )
    started = []
    for index in range(count):
        arriving[index].wait()
        wide[index] = low[index].astype(F32)
        copies = [
            (wide.at[index, pl.ds(0, share)], first_out.at[index]),
            (wide.at[index, pl.ds(share, share)], second_out.at[index]),
        ]
        started += run_copies(copies, semaphores.at[pl.ds(2 * index, 2)])
    for copy in started:
        copy.wait()


def back_rows_kernel(place, choose, slots, out_0, out_1, out_2, out_3, partial):
    partial[...] = dot_tn(choose[...], slots[...])
    put_row_chunks(place, partial, (out_0, out_1, out_2, out_3))


def back_columns_kernel(place, choose, slots, out_0, out_1, out_2, out_3, turned):
    turned[...] = dot_tn(slots[...], choose[...])
    put_row_chunks(place, turned, (out_0, out_1, out_2, out_3))


def back_folded_kernel(
    share, place, choose, message, out_0, out_1, out_2, out_3, slots, turned, semaphores
):
    count = message.shape[0]
    capacity = slots.shape[0] // count
    folded = message.shape[1] - 2 * share
    copies = []
    for index in range(count):
        copies += unfold_copies(
            message.at[index, pl.ds(2 * share, folded)], slots, index * capacity, capacity
        )
    for copy in run_copies(copies, semaphores):
        copy.wait()
    back_columns_kernel(place, choose, slots, out_0, out_1, out_2, out_3, turned)


def mixer_grad_kernel(
    place,
    piece_0,
    piece_1,
    piece_2,
    piece_3,
    residual_in,
    gain_ref,
    cotangent,
    out_proj,
    columns_out,
    mix_out,
    d_gated,
    gain_grad,
    d_send,
    turned,
):
    take_row_pieces(place, (piece_0, piece_1, piece_2, piece_3), d_send)
    residual = residual_in[...]
    inverse = rms_rate(residual)
    scaled = residual * inverse
    grad = d_send[...]
    pulled = grad * as_row(gain_ref)
    along = jnp.mean(pulled * scaled, axis=-1, keepdims=True)
    d_residual = cotangent[...].astype(F32) + inverse * (pulled - scaled * along)
    d_mix = d_residual.astype(BF16)
    put_blocks(mix_out, d_mix)
    d_gated[...] = dot_nt(d_mix, out_proj[...])
    gain_grad[...] = jnp.sum(grad * scaled, axis=0, keepdims=True)
    turned[...] = d_residual.T
    column = columns_out.shape[0]
    columns_out[...] = turned[pl.ds(pl.multiple_of(place[0] * column, column), column), :]


def split_vectors(vectors):
    upper = vectors.astype(BF16).astype(F32)
    return upper, vectors - upper


def scan_backward_kernel(
    d_gated,
    y_in,
    gate_in,
    act_in,
    mixed_in,
    masks,
    dt_proj,
    dt_bias,
    decay_log,
    skip_gain,
    gain_grad,
    d_mix,
    d_mixed_out,
    d_act_out,
    d_gate_out,
    share_out,
    rate,
    step_rows,
    decay_rows,
    drive_rows,
    dy_rows,
    du_rows,
    dl_rows,
    decays,
    history,
):
    rank = dt_proj.shape[0]
    states = decay_log.shape[0]
    length, chans = y_in.shape
    tiles = step_rows.shape[1] // 128
    full = 128 * tiles
    mixed = mixed_in[...]
    dt_low = mixed[:rank].astype(BF16)
    raw_step = dot_tn(dt_low, dt_proj[...]) + as_row(dt_bias)
    step_size = softplus(raw_step)
    act = act_in[...].astype(F32)
    reset = NEVER * (1.0 - wide_masks(masks, 0, chans))
    padded_copy(rate, -jnp.exp(decay_log[...]))
    padded_copy(step_rows, step_size)
    padded_copy(decay_rows, LOG2E * (step_size + reset))
    padded_copy(drive_rows, step_size * act)
    gate = gate_in[...]
    gate_sig = jax.nn.sigmoid(gate)
    d_out = d_gated[...]
    d_y = d_out * (gate * gate_sig)
    padded_copy(dy_rows, d_y)
    d_gate = d_out * y_in[...] * gate_sig * (1.0 + gate * (1.0 - gate_sig))
    b_turned = mixed[rank : rank + states]
    c_turned = mixed[rank + states : rank + 2 * states]
    history[pl.ds(0, states), :] = jnp.zeros((states, full), F32)

    def forward_block(index, state):
        start = pl.multiple_of(index * 8, 8)
        b_cols = block_columns(b_turned, index)
        steps = decay_rows[pl.ds(start, 8), :]
        drives = drive_rows[pl.ds(start, 8), :]
        for row in range(8):
            decay = jnp.exp2(rate[...] * steps[row : row + 1])
            state = decay * state + spread_column(b_cols, row, tiles) * drives[row : row + 1]
            at = pl.multiple_of((start + row) * states, states)
            decays[pl.ds(at, states), :] = decay
            history[pl.ds(at + states, states), :] = state
        return state

    lax.fori_loop(0, length // 8, forward_block, jnp.zeros((states, full), F32))
    lanes = lax.broadcasted_iota(jnp.int32, (states, length), 1)

    def backward_block(count, carry):
        carried, d_rate, d_b, d_c = carry
        index = length // 8 - 1 - count
        start = pl.multiple_of(index * 8, 8)
        b_cols = block_columns(b_turned, index)
        c_cols = block_columns(c_turned, index)
        steps = step_rows[pl.ds(start, 8), :]
        drives = drive_rows[pl.ds(start, 8), :]
        dys = dy_rows[pl.ds(start, 8), :]
        du = [None] * 8
        dl = [None] * 8
        for row in reversed(range(8)):
            at = pl.multiple_of((start + row) * states, states)
            before = history[pl.ds(at, states), :]
            after = history[pl.ds(at + states, states), :]
            decay = decays[pl.ds(at, states), :]
            here = lanes == start + row
            dy_row = jnp.broadcast_to(dys[row : row + 1], (states, full))
            grad = spread_column(c_cols, row, tiles) * dy_row + carried
            c_part = jnp.sum(fold_tiles(dy_row * after), axis=1, keepdims=True)
            d_c = jnp.where(here, c_part, d_c)
            b_part = jnp.sum(fold_tiles(grad * drives[row : row + 1]), axis=1, keepdims=True)
            d_b = jnp.where(here, b_part, d_b)
            du[row] = jnp.sum(grad * spread_column(b_cols, row, tiles), axis=0, keepdims=True)
            carried = grad * decay
            d_log = carried * before
            dl[row] = jnp.sum(d_log * rate[...], axis=0, keepdims=True)
            d_rate = d_rate + d_log * steps[row : row + 1]
        du_rows[pl.ds(start, 8), :] = jnp.concatenate(du, axis=0)
        dl_rows[pl.ds(start, 8), :] = jnp.concatenate(dl, axis=0)
        return carried, d_rate, d_b, d_c

    nothing = jnp.zeros((states, full), F32)
    thin = jnp.zeros((states, length), F32)
    _, d_rate, d_b, d_c = lax.fori_loop(
        0, length // 8, backward_block, (nothing, nothing, thin, thin)
    )
    du = du_rows[:, :chans]
    d_step = (dl_rows[:, :chans] + du * act) * jax.nn.sigmoid(raw_step)
    d_step_low = d_step.astype(BF16)
    low_turned = dot_nt(dt_proj[...], d_step_low)
    d_mixed_out[...] = jnp.concatenate([low_turned, d_b, d_c], axis=0).astype(BF16)
    d_act_out[...] = du * step_size + as_row(skip_gain) * d_y
    d_gate_low = d_gate.astype(BF16)
    d_gate_out[...] = d_gate_low
    width = d_mix.shape[0]
    share_out[:width] = d_mix[...]
    padded_copy(du_rows, d_gate_low.astype(F32))
    share_out[width : width + chans] = du_rows[...].T[:chans].astype(BF16)
    gain_rows = gain_grad[...]
    upper, lower = split_vectors(
        jnp.concatenate(
            [
                (d_rate * rate[...])[:, :chans],
                jnp.sum(d_step, axis=0, keepdims=True),
                jnp.sum(d_y * act, axis=0, keepdims=True),
                gain_rows[:, :chans],
                gain_rows[:, chans:],
                jnp.zeros((VECTORS_ONE - states - 4, chans), F32),
            ],
            axis=0,
        )
    )
    dl_rows[...] = jnp.zeros(dl_rows.shape, F32)
    dl_rows[:rank, :chans] = dot_nn(dt_low, d_step_low)
    dl_rows[rank : rank + VECTORS_ONE, :chans] = upper
    dl_rows[rank + VECTORS_ONE : rank + 2 * VECTORS_ONE, :chans] = lower
    share_out[width + chans :] = dl_rows[...].T[:chans].astype(BF16)


def leave_kernel(
    place,
    piece_0,
    piece_1,
    piece_2,
    piece_3,
    d_act_scan,
    d_gate,
    conv_in,
    inner_in,
    masks,
    x_proj,
    conv_weight,
    in_proj,
    rows_in,
    gain,
    out_0,
    out_1,
    out_2,
    out_3,
    message,
    held,
    turned,
    padded,
):
    length, chans = inner_in.shape
    width = rows_in.shape[1]
    full = padded.shape[1]
    d_mixed = sum_pieces(place, (piece_0, piece_1, piece_2, piece_3), held).astype(BF16)
    d_act = d_act_scan[...] + dot_tn(d_mixed, x_proj[...])
    conv = conv_in[...]
    sig = jax.nn.sigmoid(conv)
    d_conv = d_act * sig * (1.0 + conv * (1.0 - sig))
    inner = inner_in[...]
    d_inner = conv_weight[3:4, :] * d_conv
    weight_grads = [jnp.sum(d_conv * inner, axis=0, keepdims=True)]
    for shift in (1, 2, 3):
        masked = d_conv * wide_masks(masks, shift, chans)
        weight_grads.append(
            jnp.sum(masked * pltpu.roll(inner, shift, 0), axis=0, keepdims=True)
        )
        d_inner = d_inner + conv_weight[3 - shift : 4 - shift, :] * pltpu.roll(
            masked, length - shift, 0
        )
    d_inner_low = d_inner.astype(BF16)
    padded_copy(padded, d_inner_low.astype(F32))
    message[:chans] = padded[...].T[:chans].astype(BF16)
    proj = d_mixed.shape[0]
    top = message.shape[0] - full // 128 * 2 * VECTORS_TWO
    message[chans:top] = jnp.concatenate(
        [d_mixed.astype(F32), jnp.zeros((top - chans - proj, length), F32)], axis=0
    ).astype(BF16)
    d_normed = dot_nn(d_inner_low, in_proj[0]) + dot_nn(d_gate[...], in_proj[1])
    rows = rows_in[...].astype(F32)
    scaled = rows * rms_rate(rows)
    norm_grad = jnp.sum(d_normed * scaled, axis=0, keepdims=True)
    upper, lower = split_vectors(
        jnp.concatenate(
            [
                weight_grads[3],
                weight_grads[2],
                weight_grads[1],
                weight_grads[0],
                jnp.sum(d_conv, axis=0, keepdims=True),
                norm_grad[:, :chans],
                norm_grad[:, chans:],
                jnp.zeros((VECTORS_TWO - 7, chans), F32),
            ],
            axis=0,
        )
    )
    padded_copy(padded, jnp.zeros((length, chans), F32))
    padded[:VECTORS_TWO, :chans] = upper
    padded[VECTORS_TWO : 2 * VECTORS_TWO, :chans] = lower
    for tile in range(full // 128):
        message[top + tile * 2 * VECTORS_TWO : top + (tile + 1) * 2 * VECTORS_TWO] = padded[
            : 2 * VECTORS_TWO, tile * 128 : (tile + 1) * 128
        ].astype(BF16)
    along = jnp.mean(d_normed * as_row(gain) * scaled, axis=-1, keepdims=True)
    along = jnp.broadcast_to(along, (length, length)).T[:8]
    high = along.astype(BF16)
    low = (along - high.astype(F32)).astype(BF16)
    turned[...] = d_normed.T
    outs = (out_0, out_1, out_2, out_3)
    put_row_chunks(place, turned, outs)
    column = width // len(outs)
    for out in outs:
        out[column:, :] = jnp.concatenate([high, low], axis=0)


def finish_rows_kernel(
    piece_0, piece_1, piece_2, piece_3, d_columns, tokens, scale, gain, grad_tokens
):
    column = tokens.shape[0]
    total = piece_0[...].astype(F32)
    for piece in (piece_1, piece_2, piece_3):
        total = total + piece[...].astype(F32)
    along = total[column : column + 1] + total[column + 8 : column + 9]
    inverse = scale[...]
    pulled = total[:column] * gain[...]
    scaled = tokens[...].astype(F32) * inverse
    grad_tokens[...] = d_columns[...] + inverse * (pulled - scaled * along)


def take_blocks(target, pieces):
    for index, piece in enumerate(pieces):
        for start in range(0, target.shape[1], 128):
            target[index * 128 : (index + 1) * 128, start : start + 128] = piece[
                start : start + 128
            ]


def take_turned(target, pieces, start):
    rows = target.shape[0]
    for index, piece in enumerate(pieces):
        target[:, index * 128 : (index + 1) * 128] = piece[start : start + rows]


def first_sets_kernel(firsts, normed, gated, acts):
    chans = gated.shape[0]
    width = normed.shape[1]
    take_blocks(normed, firsts)
    take_turned(gated, firsts, width)
    take_turned(acts, firsts, width + chans)


def wide_grads_kernel(
    sizes,
    seconds,
    normed,
    gated,
    out_grad,
    in_grad,
    dt_grad,
    bias_grad,
    decay_grad,
    skip_grad,
    norm_grad,
    mixed,
    d_gate,
    total,
    gate_grad,
    semaphore,
):
    rank, states = sizes
    chans, width = out_grad.shape
    take_turned(d_gate, seconds, width)
    gate_grad[...] = dot_nn(d_gate[...], normed[...])
    last = pltpu.make_async_copy(gate_grad, in_grad.at[1], semaphore)
    last.start()
    take_blocks(mixed, seconds)
    out_grad[...] = dot_nn(gated[...], mixed[...])
    vectors = seconds[0][width + chans :].astype(F32)
    for piece in seconds[1:]:
        vectors = vectors + piece[width + chans :].astype(F32)
    total[...] = jnp.zeros(total.shape, F32)
    total[:chans] = vectors
    rows = total[...].T[:, :chans]
    dt_grad[...] = rows[:rank]
    rows = rows[rank : rank + VECTORS_ONE] + rows[rank + VECTORS_ONE : rank + 2 * VECTORS_ONE]
    decay_grad[...] = rows[:states]
    bias_grad[...] = rows[states].reshape(chans)
    skip_grad[...] = rows[states + 1].reshape(chans)
    norm_grad[...] = jnp.concatenate(
        [rows[states + 2 : states + 3], rows[states + 3 : states + 4]], axis=1
    )
    last.wait()


def late_grads_kernel(
    widths,
    lasts,
    normed,
    acts,
    kept_grad,
    in_grad,
    x_grad,
    weight_grad,
    bias_grad,
    norm_grad,
    d_inner,
    d_mixed,
    inner_grad,
    semaphore,
):
    chans, proj = widths
    rows = d_mixed.shape[0]
    take_turned(d_inner, lasts, 0)
    inner_grad[...] = dot_nn(d_inner[...], normed[...])
    last = pltpu.make_async_copy(inner_grad, in_grad.at[0], semaphore)
    last.start()
    take_turned(d_mixed, lasts, chans)
    x_grad[...] = dot_nt(d_mixed[...], acts[...])[:proj]
    total = lasts[0][chans + rows :].astype(F32)
    for piece in lasts[1:]:
        total = total + piece[chans + rows :].astype(F32)
    deep = 2 * VECTORS_TWO
    vectors = jnp.concatenate(
        [total[start : start + deep] for start in range(0, total.shape[0], deep)], axis=1
    )[:, :chans]
    vectors = vectors[:VECTORS_TWO] + vectors[VECTORS_TWO:]
    weight_grad[...] = vectors[:4]
    bias_grad[...] = vectors[4].reshape(chans)
    norm_grad[...] = jnp.concatenate([vectors[5:6], vectors[6:7]], axis=1)
    last.wait()


def send_chunks(chunks):
    count = len(chunks)
    pairs = [[(i, (i + s) % count) for i in range(count)] for s in range(count)]
    return [chunks[0]] + [lax.ppermute(chunks[s], "tensor", pairs[s]) for s in range(1, count)]


def share_rows(values, count):
    return send_chunks([values] * count)


def add_low(pieces):
    total = pieces[0].astype(F32)
    for piece in pieces[1:]:
        total = total + piece.astype(F32)
    return total.astype(BF16)


def after(values, *events):
    return list(lax.optimization_barrier((tuple(values), events))[0])


def swap(values, bits):
    return lax.ppermute(values, "dp", [(i, i ^ bits) for i in range(NEAR_GROUPS)])


def swap_near(fars):
    return [*fars, *[swap(far, 1) for far in fars]]


def body(
    tokens,
    resets,
    routes,
    norm_one,
    in_proj,
    conv_weight,
    conv_bias,
    x_proj,
    dt_proj,
    dt_bias,
    decay_log,
    skip_gain,
    out_proj,
    norm_two,
    expert_in,
    expert_out,
    cotangent,
):
    groups = lax.axis_size("dp")
    parts = lax.axis_size("tensor")
    place = lax.axis_index("tensor").astype(jnp.int32).reshape(1)
    length, column = tokens.shape
    width = norm_one.shape[0]
    rank, chans = dt_proj.shape
    states = decay_log.shape[0]
    experts, share, hidden_units = expert_in.shape
    proj = x_proj.shape[1]
    tile_count = groups // experts
    block_rows = length * experts // groups
    capacity = max(2, block_rows // 4)
    slot_count = groups * capacity
    tiles = -(-chans // 128)
    full = 128 * tiles
    near = groups == NEAR_GROUPS and experts == groups
    tokens_turned = tokens.T
    in_turned = jnp.swapaxes(in_proj, 1, 2)
    x_turned = x_proj.T
    resets_row = resets.reshape(1, length)
    routes_row = routes.reshape(1, length)

    def exchange(values):
        return lax.all_to_all(values, "dp", split_axis=0, concat_axis=0, tiled=True)

    def exchange_slots(slots):
        return exchange(slots.reshape(groups, capacity, width)).reshape(slot_count, width)

    token_pieces = share_rows(tokens_turned, parts)
    mask_out = ((4, length, 128), F32)
    choose_out = ((slot_count, length), BF16)
    weight_outs = [((width, hidden_units), BF16)] * 2
    slots_out = ((slot_count, width), BF16)
    hidden_out = ((slot_count, hidden_units), BF16)
    folded = capacity + capacity // 2
    message_out = ((groups, 2 * share + folded, hidden_units), BF16)
    if near:
        masks, choose, packed = run_kernel(
            functools.partial(pack_kernel, capacity),
            [mask_out, choose_out, message_out],
            [resets_row, routes_row, cotangent, expert_in, expert_out],
            [
                ((groups, folded, hidden_units), BF16),
                pltpu.SemaphoreType.DMA((3 * experts,)),
            ],
            far_outs=(2,),
        )
        first_w, second_w, grad_slots, d_hidden = run_kernel(
            functools.partial(unpack_kernel, share, capacity),
            weight_outs + [slots_out, ((slot_count, hidden_units), F32)],
            [exchange(packed)],
            [pltpu.SemaphoreType.DMA((5 * groups,))],
            far_args=(0,),
        )
    else:
        masks, choose, grad_send = run_kernel(
            functools.partial(prepare_kernel, experts, capacity, block_rows),
            [mask_out, choose_out, slots_out],
            [resets_row, routes_row, cotangent],
        )
        first_w = exchange(jnp.tile(expert_in, (tile_count, 1, 1))).reshape(weight_outs[0][0])
        second_w = exchange(jnp.tile(expert_out, (tile_count, 1, 1))).reshape(weight_outs[0][0])
        grad_slots = exchange_slots(grad_send)
        (d_hidden,) = run_kernel(
            hidden_back_kernel, [((slot_count, hidden_units), F32)], [grad_slots, second_w]
        )

    rows, normed, act, inner, conv, gate, scale, gain_columns, mixed_part = run_kernel(
        enter_kernel,
        [
            ((length, width), BF16),
            ((width, length), BF16),
            ((length, chans), BF16),
            ((length, chans), F32),
            ((length, chans), F32),
            ((length, chans), F32),
            ((1, length), F32),
            ((column, length), F32),
            ((proj, length), BF16),
        ],
        [place, *token_pieces, norm_one, in_turned, conv_weight, conv_bias, x_turned, masks],
        [((width, length), F32)],
        scalars=1,
    )
    mixed_pieces = share_rows(mixed_part, parts)
    *mix_chunks, mixed, first, y = run_kernel(
        scan_forward_kernel,
        [((length // parts, width), BF16)] * parts
        + [
            ((proj, length), F32),
            ((width + 2 * chans, length), BF16),
            ((length, chans), F32),
        ],
        [
            place,
            *mixed_pieces,
            dt_proj,
            dt_bias,
            decay_log,
            skip_gain,
            act,
            gate,
            masks,
            out_proj,
            normed,
        ],
        [
            ((parts, proj, length), BF16),
            ((states, full), F32),
            ((length, full), F32),
            ((length, full), F32),
            ((length, full), F32),
            ((length, width), F32),
        ],
        scalars=1,
    )
    mixer_pieces = share_rows(add_low(send_chunks(mix_chunks)), parts)
    residual, residual_columns, send_slots = run_kernel(
        dispatch_kernel,
        [((length, width), F32), ((column, length), F32), slots_out],
        [place, *mixer_pieces, rows, norm_two, choose],
        [((width, length), F32)],
        scalars=1,
    )
    arrived = exchange_slots(send_slots)
    if near:
        first_x = swap(after([first], d_hidden)[0], 2)
        arrived = after([arrived], first_x)[0]
    hidden, d_pre, d_slots = run_kernel(
        expert_kernel, [hidden_out, hidden_out, slots_out], [arrived, first_w, d_hidden]
    )
    back_slots = exchange_slots(d_slots)
    grad_args = [arrived, grad_slots, hidden, d_pre, second_w]
    grad_out = ((experts, share, hidden_units), F32)
    if near:
        (packed,) = run_kernel(
            functools.partial(expert_grads_pack_kernel, share, capacity),
            [message_out],
            grad_args,
            [
                ((2, width, hidden_units), BF16),
                ((groups, folded, hidden_units), BF16),
                pltpu.SemaphoreType.DMA((3 * groups,)),
            ],
            far_outs=(0,),
        )
        first_y = swap(after([first], hidden)[0], 4)
        packed, back_slots = after([packed, back_slots], first_y)
        back_slots = after([back_slots], packed)[0]
        owned = exchange(packed)
    else:
        grad_first, grad_second, moe_slots = run_kernel(
            expert_grads_kernel, weight_outs + [slots_out], grad_args
        )
    back_chunks = run_kernel(
        back_rows_kernel,
        [((length // parts, width), BF16)] * parts,
        [place, choose, back_slots],
        [((length, width), F32)],
        scalars=1,
    )
    send_pieces = share_rows(add_low(send_chunks(back_chunks)), parts)
    d_columns, d_mix, d_gated, gain_grad_two = run_kernel(
        mixer_grad_kernel,
        [
            ((column, length), F32),
            ((width, length), BF16),
            ((length, chans), F32),
            ((1, width), F32),
        ],
        [place, *send_pieces, residual, norm_two, cotangent, out_proj],
        [((length, width), F32), ((width, length), F32)],
        scalars=1,
    )
    d_mixed_part, d_act_scan, d_gate, second = run_kernel(
        scan_backward_kernel,
        [
            ((proj, length), BF16),
            ((length, chans), F32),
            ((length, chans), BF16),
            ((width + 2 * chans, length), BF16),
        ],
        [
            d_gated,
            y,
            gate,
            act,
            mixed,
            masks,
            dt_proj,
            dt_bias,
            decay_log,
            skip_gain,
            gain_grad_two,
            d_mix,
        ],
        [
            ((states, full), F32),
            ((length, full), F32),
            ((length, full), F32),
            ((length, full), F32),
            ((length, full), F32),
            ((length, full), F32),
            ((length, full), F32),
            ((length * states, full), F32),
            (((length + 1) * states, full), F32),
        ],
    )
    d_mixed_pieces = share_rows(d_mixed_part, parts)
    if near:
        second_x, second_y = swap(second, 2), swap(second, 4)
    last_rows = chans + -(-proj // 16) * 16 + tiles * 2 * VECTORS_TWO
    *normed_chunks, message = run_kernel(
        leave_kernel,
        [((column + 16, length), BF16)] * parts
        + [((last_rows, length), BF16)],
        [
            place,
            *d_mixed_pieces,
            d_act_scan,
            d_gate,
            conv,
            inner,
            masks,
            x_turned,
            conv_weight,
            in_turned,
            rows,
            norm_one,
        ],
        [((parts, proj, length), BF16), ((width, length), F32), ((length, full), F32)],
        scalars=1,
    )
    normed_pieces = send_chunks(normed_chunks)
    (grad_tokens,) = run_kernel(
        finish_rows_kernel,
        [((column, length), F32)],
        [*normed_pieces, d_columns, tokens_turned, scale, gain_columns],
    )

    chunk_outs = [((column, length), BF16)] * parts
    if near:
        moe_chunks = run_kernel(
            functools.partial(back_folded_kernel, share),
            chunk_outs,
            [place, choose, owned],
            [slots_out, ((width, length), F32), pltpu.SemaphoreType.DMA((3 * groups,))],
            scalars=1,
            far_args=(2,),
        )
        grad_expert_in, grad_expert_out = run_kernel(
            functools.partial(owner_kernel, share),
            [grad_out] * 2,
            [owned],
            [
                ((groups, 2 * share, hidden_units), BF16),
                ((groups, 2 * share, hidden_units), F32),
                pltpu.SemaphoreType.DMA((groups,)),
                pltpu.SemaphoreType.DMA((2 * groups,)),
            ],
            far_args=(0,),
            far_outs=(0, 1),
        )
    else:
        moe_chunks = run_kernel(
            back_columns_kernel,
            chunk_outs,
            [place, choose, exchange_slots(moe_slots)],
            [((width, length), F32)],
            scalars=1,
        )

        def owner_sum(values):
            got = exchange(values.reshape(groups, share, hidden_units)).astype(F32)
            return jnp.sum(got.reshape(tile_count, experts, share, hidden_units), axis=0)

        grad_expert_in = owner_sum(grad_first)
        grad_expert_out = owner_sum(grad_second)
    outcome = residual_columns
    for piece in send_chunks(moe_chunks):
        outcome = outcome + piece.astype(F32)
    outcome = outcome.astype(BF16)

    if near:
        first_y, second_x, second_y = after([first_y, second_x, second_y], message)
        firsts = swap_near([first, first_x, first_y, swap(first_y, 2)])
        seconds = swap_near([second, second_x, second_y, swap(second_x, 4)])

        def first_sets(*refs):
            first_sets_kernel(refs[:groups], *refs[groups:])

        all_normed, all_gated, all_act = run_kernel(
            first_sets,
            [
                ((groups * length, width), BF16),
                ((chans, groups * length), BF16),
                ((chans, groups * length), BF16),
            ],
            firsts,
        )

        def wide_grads(*refs):
            wide_grads_kernel((rank, states), refs[:groups], *refs[groups:])

        (
            grad_out_proj,
            grad_in_turned,
            grad_dt_proj,
            grad_dt_bias,
            grad_decay_log,
            grad_skip_gain,
            grad_norm_two,
        ) = run_kernel(
            wide_grads,
            [
                ((chans, width), F32),
                ((2, chans, width), F32),
                ((rank, chans), F32),
                ((chans,), F32),
                ((states, chans), F32),
                ((chans,), F32),
                ((1, width), F32),
            ],
            [*seconds, all_normed, all_gated],
            [
                ((groups * length, width), BF16),
                ((chans, groups * length), BF16),
                ((full, length), F32),
                ((chans, width), F32),
                pltpu.SemaphoreType.DMA,
            ],
            far_outs=(1,),
        )
        message = after([message], second_x, second_y)[0]
        lasts = swap_near([message, swap(message, 2), swap(message, 4), swap(message, 6)])

        def late_grads(*refs):
            late_grads_kernel((chans, proj), refs[:groups], *refs[groups:])

        grad_in_turned, grad_x_turned, grad_conv_weight, grad_conv_bias, norm_part = run_kernel(
            late_grads,
            [
                ((2, chans, width), F32),
                ((proj, chans), F32),
                ((4, chans), F32),
                ((chans,), F32),
                ((1, width), F32),
            ],
            [*lasts, all_normed, all_act, grad_in_turned],
            [
                ((chans, groups * length), BF16),
                ((-(-proj // 16) * 16, groups * length), BF16),
                ((chans, width), F32),
                pltpu.SemaphoreType.DMA,
            ],
            far_args=(groups + 2,),
            far_outs=(0,),
            alias={groups + 2: 0},
        )
    else:
        top = last_rows - tiles * 2 * VECTORS_TWO
        ones = second[width + chans :].astype(F32).T
        twos = message[top:].astype(F32).reshape(tiles, 2 * VECTORS_TWO, length)
        twos = jnp.swapaxes(twos, 0, 1).reshape(2 * VECTORS_TWO, full)[:, :chans]
        plain_normed = jnp.swapaxes(normed.reshape(-1, length, 128), 0, 1).reshape(length, width)
        plain_mix = jnp.swapaxes(d_mix.reshape(-1, length, 128), 0, 1).reshape(length, width)
        grad_in_turned, grad_x_turned, grad_dt_proj, grad_out_proj, ones, twos = lax.psum(
            (
                jnp.stack(
                    [
                        dot_nn(message[:chans], plain_normed),
                        dot_nn(second[width : width + chans], plain_normed),
                    ]
                ),
                dot_nn(message[chans : chans + proj], act),
                ones[:rank],
                dot_nn(first[width : width + chans], plain_mix),
                ones[rank : rank + VECTORS_ONE]
                + ones[rank + VECTORS_ONE : rank + 2 * VECTORS_ONE],
                twos[:VECTORS_TWO] + twos[VECTORS_TWO:],
            ),
            "dp",
        )
        grad_decay_log = ones[:states]
        grad_dt_bias = ones[states]
        grad_skip_gain = ones[states + 1]
        grad_norm_two = ones[states + 2 : states + 4]
        grad_conv_weight = twos[:4]
        grad_conv_bias = twos[4]
        norm_part = twos[5:7].reshape(1, width)
    grad_norm_one = sum(share_rows(norm_part, parts))
    return (
        outcome.T,
        grad_tokens.T,
        grad_norm_one.reshape(width),
        jnp.swapaxes(grad_in_turned, 1, 2),
        grad_conv_weight,
        grad_conv_bias,
        grad_x_turned.T,
        grad_dt_proj,
        grad_dt_bias,
        grad_decay_log,
        grad_skip_gain,
        grad_out_proj,
        grad_norm_two.reshape(width),
        grad_expert_in,
        grad_expert_out,
    )


def solution(mesh):
    placed = (
        P("dp", "tensor"),
        P("dp"),
        P("dp", None),
        P(),
        P(None, None, "tensor"),
        P(None, "tensor"),
        P("tensor"),
        P("tensor", None),
        P(None, "tensor"),
        P("tensor"),
        P(None, "tensor"),
        P("tensor"),
        P("tensor", None),
        P(),
        P(None, "dp", "tensor"),
        P(None, "dp", "tensor"),
        P("dp", None),
    )
    return jax.shard_map(
        body,
        mesh=mesh,
        in_specs=placed,
        out_specs=(
            P("dp", "tensor"),
            P("dp", "tensor"),
            P(),
            P(None, None, "tensor"),
            P(None, "tensor"),
            P("tensor"),
            P("tensor", None),
            P(None, "tensor"),
            P("tensor"),
            P(None, "tensor"),
            P("tensor"),
            P("tensor", None),
            P(),
            P(None, "dp", "tensor"),
            P(None, "dp", "tensor"),
        ),
        check_vma=False,
    )
```

```python
import functools
import math

import jax
import jax.numpy as jnp
from jax import lax
from jax.experimental import pallas as pl
from jax.experimental.pallas import tpu as pltpu
from jax.sharding import PartitionSpec as P

EPSILON = 1e-05
F32 = jnp.float32
BF16 = jnp.bfloat16
NEVER = 1e4
LOG2E = 1.4426950408889634
GELU_SCALE = math.sqrt(2.0 / math.pi)
GELU_CUBE = 0.044715
VMEM_SPARE = 6 * 1024 * 1024
NEAR_GROUPS = 8
VECTORS_ONE = 24
VECTORS_TWO = 8


def run_kernel(
    kernel,
    outs,
    args,
    scratch=(),
    scalars=0,
    far_args=(),
    staged=(),
    far_outs=(),
    loose_outs=(),
    held_outs=(),
    alias=None,
):
    staged = tuple(staged)
    outside = {*far_args, *staged}

    def spec(index, far):
        return pl.BlockSpec(memory_space=pltpu.HBM if index in far else pltpu.VMEM)

    def held(index, shape, dtype):
        if index in loose_outs:
            return jax.ShapeDtypeStruct(shape, dtype)
        return (pltpu.VMEM if index in held_outs else pltpu.HBM)(shape, dtype)

    def body(*refs):
        refs = list(refs)
        if staged:
            *refs, semaphores = refs
            places = refs[len(refs) - len(staged) :]
            refs = refs[: len(refs) - len(staged)]
            copies = run_copies(list(zip([refs[index] for index in staged], places)), semaphores)
            for index, place in zip(staged, places):
                refs[index] = place
            for copy in copies:
                copy.wait()
        kernel(*refs)

    sizes = [(arg.shape, arg.dtype) for index, arg in enumerate(args) if index not in far_args]
    sizes += [out for index, out in enumerate(outs) if index not in far_outs]
    sizes += [shape for shape in scratch if isinstance(shape, tuple)]
    scratch = [pltpu.VMEM(*shape) if isinstance(shape, tuple) else shape for shape in scratch]
    if staged:
        scratch += [pltpu.VMEM(args[index].shape, args[index].dtype) for index in staged]
        scratch += [pltpu.SemaphoreType.DMA((len(staged),))]
    needed = sum(math.prod(shape) * jnp.dtype(dtype).itemsize for shape, dtype in sizes)
    return pl.pallas_call(
        body,
        out_shape=[held(index, shape, dtype) for index, (shape, dtype) in enumerate(outs)],
        in_specs=[
            pl.BlockSpec(memory_space=pltpu.SMEM) if index < scalars else spec(index, outside)
            for index in range(len(args))
        ],
        out_specs=[spec(index, far_outs) for index in range(len(outs))],
        scratch_shapes=scratch,
        input_output_aliases=alias or {},
        compiler_params=pltpu.CompilerParams(vmem_limit_bytes=VMEM_SPARE + needed * 5 // 4),
    )(
        *[
            pltpu.with_memory_space_constraint(arg, pltpu.HBM) if index in outside else arg
            for index, arg in enumerate(args)
        ]
    )


def dot_nn(left, right):
    return lax.dot_general(left, right, (((1,), (0,)), ((), ())), preferred_element_type=F32)


def dot_nt(left, right):
    return lax.dot_general(left, right, (((1,), (1,)), ((), ())), preferred_element_type=F32)


def dot_tn(left, right):
    return lax.dot_general(left, right, (((0,), (0,)), ((), ())), preferred_element_type=F32)


def lane_tiles(column, tiles):
    return jnp.concatenate([column] * tiles, axis=1)


def fold_tiles(values):
    total = values[:, :128]
    for tile in range(1, values.shape[1] // 128):
        total = total + values[:, 128 * tile : 128 * (tile + 1)]
    return total


def wide_masks(masks, index, chans):
    return lane_tiles(masks[index], -(-chans // 128))[:, :chans]


def rms_rate(values):
    return lax.rsqrt(jnp.mean(values * values, axis=-1, keepdims=True) + EPSILON)


def as_row(ref):
    return ref[...].reshape(1, ref.shape[0])


def softplus(values):
    return jnp.maximum(values, 0.0) + jnp.log1p(jnp.exp(-jnp.abs(values)))


def padded_copy(target, values):
    target[...] = jnp.zeros(target.shape, target.dtype)
    target[:, : values.shape[1]] = values


def put_row_chunks(place, source, outs):
    count = len(outs)
    rows = source.shape[0] // count
    for step, out in enumerate(outs):
        start = pl.multiple_of(lax.rem(place[0] + step, count) * rows, rows)
        out[pl.ds(0, rows), :] = source[pl.ds(start, rows), :].astype(out.dtype)


def take_row_pieces(place, pieces, target):
    count = len(pieces)
    rows = target.shape[0] // count
    for step, piece in enumerate(pieces):
        start = pl.multiple_of(lax.rem(place[0] - step + count, count) * rows, rows)
        target[pl.ds(start, rows), :] = piece[...].astype(target.dtype)


def sum_pieces(place, pieces, held):
    count = len(pieces)
    for step, piece in enumerate(pieces):
        held[lax.rem(place[0] - step + count, count)] = piece[...]
    total = held[0].astype(F32)
    for index in range(1, count):
        total = total + held[index].astype(F32)
    return total


def run_copies(copies, semaphores):
    started = []
    for index, (source, target) in enumerate(copies):
        copy = pltpu.make_async_copy(source, target, semaphores.at[index])
        copy.start()
        started.append(copy)
    return started


def fill_masks(resets, masks):
    length = resets.shape[1]
    square = (length, length)
    earlier = lax.broadcasted_iota(jnp.int32, square, 0)
    reset = jnp.broadcast_to(resets[...].astype(F32), square).T
    keep = jnp.where(reset == 0.0, 1.0, 0.0)
    joined = jnp.where(earlier > 0, keep, 0.0)
    one_back = pltpu.roll(joined, 1, 0)
    two_back = pltpu.roll(joined, 2, 0)
    masks[0] = keep
    masks[1] = joined
    masks[2] = joined * one_back
    masks[3] = joined * one_back * two_back


def fill_choose(capacity, block_rows, experts, routes, choose):
    length = routes.shape[1]
    square = (length, length)
    earlier = lax.broadcasted_iota(jnp.int32, square, 0)
    later = lax.broadcasted_iota(jnp.int32, square, 1)
    route_of = jnp.broadcast_to(routes[...].astype(F32), square)
    same = (route_of.T == route_of) & (earlier < later)
    if block_rows < length:
        same = same & (earlier // block_rows == later // block_rows)
    rank = jnp.sum(jnp.where(same, 1.0, 0.0), axis=0, keepdims=True).astype(jnp.int32)
    group = routes[...]
    if block_rows < length:
        group = group + experts * (later[:1] // block_rows)
    slot = group * capacity + rank
    slot_count = choose.shape[0]
    slot_ids = lax.broadcasted_iota(jnp.int32, (slot_count, length), 0)
    hit = slot_ids == jnp.broadcast_to(slot, (slot_count, length))
    choose[...] = jnp.where(hit, 1.0, 0.0).astype(BF16)


def prepare_kernel(
    experts, capacity, block_rows, resets, routes, cotangent, masks, choose, slots
):
    fill_masks(resets, masks)
    fill_choose(capacity, block_rows, experts, routes, choose)
    slots[...] = dot_nn(choose[...], cotangent[...]).astype(BF16)


def put_folded(target, slots):
    rows, width = slots.shape
    units = target.shape[1]
    half = rows // 2
    rest = width - units
    target[:rows, :] = slots[:, :units]
    target[rows:, :rest] = slots[:half, units:]
    target[rows:, rest:] = slots[half:, units:]


def unfold_copies(source, target, top, rows):
    units = source.shape[1]
    half = rows // 2
    rest = target.shape[1] - units
    copies = [(source.at[pl.ds(0, rows)], target.at[pl.ds(top, rows), pl.ds(0, units)])]
    for part in range(2):
        copies.append(
            (
                source.at[pl.ds(rows, half), pl.ds(part * rest, rest)],
                target.at[pl.ds(top + part * half, half), pl.ds(units, rest)],
            )
        )
    return copies


def pack_kernel(
    capacity,
    resets,
    routes,
    cotangent,
    expert_in,
    expert_out,
    masks,
    choose,
    message,
    packed,
    staged,
    arrivals,
    semaphores,
):
    experts, share, units = expert_in.shape
    length, width = cotangent.shape
    copies = []
    for index in range(experts):
        copies.append((expert_in.at[index], staged.at[index, 0]))
        copies.append((expert_out.at[index], staged.at[index, 1]))
    arriving = run_copies(copies, arrivals)
    fill_choose(capacity, length, experts, routes, choose)
    slots = dot_nn(choose[...], cotangent[...]).astype(BF16)
    started = []
    for index in range(experts):
        copies = []
        for which in range(2):
            arriving[2 * index + which].wait()
            target = message.at[index, pl.ds(which * share, share)]
            copies.append((staged.at[index, which], target))
        started += run_copies(copies, semaphores.at[pl.ds(2 * index, 2)])
    copies = []
    for index in range(experts):
        put_folded(packed.at[index], slots[index * capacity : (index + 1) * capacity])
        target = message.at[index]
        copies.append((packed.at[index], target.at[pl.ds(2 * share, packed.shape[1])]))
    started += run_copies(copies, semaphores.at[pl.ds(2 * experts, experts)])
    fill_masks(resets, masks)
    for copy in started:
        copy.wait()


def unpack_kernel(
    share,
    capacity,
    message,
    first_out,
    second_out,
    slots_out,
    d_hidden,
    first_w,
    second_w,
    grad_slots,
    semaphores,
):
    folded = capacity + capacity // 2
    copies = []
    for index in range(message.shape[0]):
        piece = message.at[index]
        rows = pl.ds(index * share, share)
        copies.append((piece.at[pl.ds(share, share)], second_w.at[rows]))
        copies += unfold_copies(
            piece.at[pl.ds(2 * share, folded)], grad_slots, index * capacity, capacity
        )
        copies.append((piece.at[pl.ds(0, share)], first_w.at[rows]))
    for copy in run_copies(copies, semaphores):
        copy.wait()
    copies = [(first_w, first_out), (second_w, second_out), (grad_slots, slots_out)]
    started = run_copies(copies, semaphores)
    d_hidden[...] = dot_nn(grad_slots[...], second_w[...])
    for copy in started:
        copy.wait()


def put_blocks(target, values):
    length = values.shape[0]
    for start in range(0, values.shape[1], 128):
        target[start : start + length, :] = values[:, start : start + 128]


def enter_kernel(
    place,
    piece_0,
    piece_1,
    piece_2,
    piece_3,
    gain_ref,
    in_proj,
    conv_weight,
    conv_bias,
    x_proj,
    masks,
    rows_out,
    normed_out,
    act_out,
    inner_out,
    conv_out,
    gate_out,
    scale_out,
    gain_out,
    mixed_out,
    turned,
):
    take_row_pieces(place, (piece_0, piece_1, piece_2, piece_3), turned)
    rows = turned[...].T
    gain = as_row(gain_ref)
    rows_out[...] = rows.astype(BF16)
    normed = (rows * rms_rate(rows) * gain).astype(BF16)
    put_blocks(normed_out, normed)
    inner = dot_nt(normed, in_proj[0])
    chans = inner.shape[1]
    inner_out[...] = inner
    total = as_row(conv_bias) + conv_weight[3:4, :] * inner
    for shift in (1, 2, 3):
        moved = pltpu.roll(inner, shift, 0) * wide_masks(masks, shift, chans)
        total = total + conv_weight[3 - shift : 4 - shift, :] * moved
    conv_out[...] = total
    act = (total * jax.nn.sigmoid(total)).astype(BF16)
    act_out[...] = act
    mixed_out[...] = dot_nt(x_proj[...], act).astype(BF16)
    gate_out[...] = dot_nt(normed, in_proj[1])
    raw = turned[...]
    scale_out[...] = lax.rsqrt(jnp.mean(raw * raw, axis=0, keepdims=True) + EPSILON)
    turned[...] = jnp.broadcast_to(gain, rows.shape).T
    column = gain_out.shape[0]
    gain_out[...] = turned[pl.ds(pl.multiple_of(place[0] * column, column), column), :]


def block_columns(transposed, block):
    length = transposed.shape[1]
    return pltpu.roll(transposed, lax.rem(length - 8 * block, length), 1)


def spread_column(columns, row, tiles):
    return lane_tiles(jnp.broadcast_to(columns[:, row : row + 1], (columns.shape[0], 128)), tiles)


def scan_forward_kernel(
    place,
    piece_0,
    piece_1,
    piece_2,
    piece_3,
    dt_proj,
    dt_bias,
    decay_log,
    skip_gain,
    act_in,
    gate_in,
    masks,
    out_proj,
    normed,
    out_0,
    out_1,
    out_2,
    out_3,
    mixed_out,
    share_out,
    y_out,
    held,
    rate,
    step_rows,
    drive_rows,
    y_rows,
    partial,
):
    rank = dt_proj.shape[0]
    states = decay_log.shape[0]
    length, chans = y_out.shape
    tiles = step_rows.shape[1] // 128
    mixed = sum_pieces(place, (piece_0, piece_1, piece_2, piece_3), held)
    mixed_out[...] = mixed
    step_size = softplus(dot_tn(mixed[:rank].astype(BF16), dt_proj[...]) + as_row(dt_bias))
    act = act_in[...].astype(F32)
    reset = NEVER * (1.0 - wide_masks(masks, 0, chans))
    padded_copy(rate, -LOG2E * jnp.exp(decay_log[...]))
    padded_copy(step_rows, step_size + reset)
    padded_copy(drive_rows, step_size * act)
    b_turned = mixed[rank : rank + states]
    c_turned = mixed[rank + states : rank + 2 * states]

    def block(index, state):
        start = pl.multiple_of(index * 8, 8)
        b_cols = block_columns(b_turned, index)
        c_cols = block_columns(c_turned, index)
        steps = step_rows[pl.ds(start, 8), :]
        drives = drive_rows[pl.ds(start, 8), :]
        rows = []
        for row in range(8):
            decay = jnp.exp2(rate[...] * steps[row : row + 1])
            state = decay * state + spread_column(b_cols, row, tiles) * drives[row : row + 1]
            rows.append(
                jnp.sum(spread_column(c_cols, row, tiles) * state, axis=0, keepdims=True)
            )
        y_rows[pl.ds(start, 8), :] = jnp.concatenate(rows, axis=0)
        return state

    lax.fori_loop(0, length // 8, block, jnp.zeros((states, 128 * tiles), F32))
    y = y_rows[:, :chans] + as_row(skip_gain) * act
    y_out[...] = y
    gate = gate_in[...]
    gated = (y * (gate * jax.nn.sigmoid(gate))).astype(BF16)
    partial[...] = dot_nn(gated, out_proj[...])
    put_row_chunks(place, partial, (out_0, out_1, out_2, out_3))
    width = normed.shape[0]
    share_out[:width] = normed[...]
    padded_copy(step_rows, gated.astype(F32))
    share_out[width : width + chans] = step_rows[...].T[:chans].astype(BF16)
    padded_copy(step_rows, act)
    share_out[width + chans :] = step_rows[...].T[:chans].astype(BF16)


def dispatch_kernel(
    place,
    piece_0,
    piece_1,
    piece_2,
    piece_3,
    rows_in,
    gain,
    choose,
    residual_out,
    columns_out,
    slots,
    turned,
):
    take_row_pieces(place, (piece_0, piece_1, piece_2, piece_3), residual_out)
    residual = rows_in[...].astype(F32) + residual_out[...]
    residual_out[...] = residual
    send = (residual * rms_rate(residual) * as_row(gain)).astype(BF16)
    slots[...] = dot_nn(choose[...], send).astype(BF16)
    turned[...] = residual.T
    column = columns_out.shape[0]
    columns_out[...] = turned[pl.ds(pl.multiple_of(place[0] * column, column), column), :]


def hidden_back_kernel(grad_slots, second_w, d_hidden):
    d_hidden[...] = dot_nn(grad_slots[...], second_w[...])


def expert_kernel(arrived, first_w, d_hidden, hidden_out, d_pre_out, d_slots):
    value = dot_nn(arrived[...], first_w[...])
    square = value * value
    bend = jnp.tanh(GELU_SCALE * (value + GELU_CUBE * value * square))
    half = 0.5 * (1.0 + bend)
    slope = half + 0.5 * value * (1.0 - bend * bend) * GELU_SCALE * (
        1.0 + 3.0 * GELU_CUBE * square
    )
    d_pre = (slope * d_hidden[...]).astype(BF16)
    d_pre_out[...] = d_pre
    d_slots[...] = dot_nt(d_pre, first_w[...]).astype(BF16)
    hidden_out[...] = (value * half).astype(BF16)


def expert_grads_kernel(arrived, grad_slots, hidden, d_pre, second_w, first_out, second_out, moe):
    first_out[...] = dot_tn(arrived[...], d_pre[...]).astype(BF16)
    second_out[...] = dot_tn(grad_slots[...], hidden[...]).astype(BF16)
    moe[...] = dot_nt(hidden[...], second_w[...]).astype(BF16)


def expert_grads_pack_kernel(
    share, capacity, arrived, grad_slots, hidden, d_pre, second_w, message, grads, packed, semaphores
):
    experts = message.shape[0]
    started = []
    for which, (left, right) in enumerate(((arrived, d_pre), (grad_slots, hidden))):
        grads[which] = dot_tn(left[...], right[...]).astype(BF16)
        copies = [
            (
                grads.at[which, pl.ds(index * share, share)],
                message.at[index, pl.ds(which * share, share)],
            )
            for index in range(experts)
        ]
        started += run_copies(copies, semaphores.at[pl.ds(which * experts, experts)])
    moe = dot_nt(hidden[...], second_w[...]).astype(BF16)
    copies = []
    for index in range(experts):
        put_folded(packed.at[index], moe[index * capacity : (index + 1) * capacity])
        copies.append(
            (packed.at[index], message.at[index, pl.ds(2 * share, packed.shape[1])])
        )
    started += run_copies(copies, semaphores.at[pl.ds(2 * experts, experts)])
    for copy in started:
        copy.wait()


def owner_kernel(share, message, first_out, second_out, low, wide, arrivals, semaphores):
    count = message.shape[0]
    arriving = run_copies(
        [(message.at[index, pl.ds(0, 2 * share)], low.at[index]) for index in range(count)],
        arrivals,
    )
    started = []
    for index in range(count):
        arriving[index].wait()
        wide[index] = low[index].astype(F32)
        copies = [
            (wide.at[index, pl.ds(0, share)], first_out.at[index]),
            (wide.at[index, pl.ds(share, share)], second_out.at[index]),
        ]
        started += run_copies(copies, semaphores.at[pl.ds(2 * index, 2)])
    for copy in started:
        copy.wait()


def back_rows_kernel(place, choose, slots, out_0, out_1, out_2, out_3, partial):
    partial[...] = dot_tn(choose[...], slots[...])
    put_row_chunks(place, partial, (out_0, out_1, out_2, out_3))


def back_columns_kernel(choose, shares, slots, out):
    rows = dot_tn(slots[...], choose[...]).astype(BF16)
    count, top, _ = shares.shape
    column = rows.shape[0] // count
    for index in range(count):
        out[index, :top, :] = shares[index]
        out[index, top:, :] = rows[index * column : (index + 1) * column]


def back_folded_kernel(share, choose, shares, message, out, slots, semaphores):
    count = message.shape[0]
    capacity = slots.shape[0] // count
    folded = message.shape[1] - 2 * share
    copies = []
    for index in range(count):
        copies += unfold_copies(
            message.at[index, pl.ds(2 * share, folded)], slots, index * capacity, capacity
        )
    for copy in run_copies(copies, semaphores):
        copy.wait()
    back_columns_kernel(choose, shares, slots, out)


def late_vectors_kernel(refs, weight_grad, bias_grad, norm_out, staged, semaphores):
    deep = 2 * VECTORS_TWO
    rows = staged.shape[1]
    top = refs[0].shape[0] - rows
    copies = [(ref.at[pl.ds(top, rows)], staged.at[index]) for index, ref in enumerate(refs)]
    for copy in run_copies(copies, semaphores):
        copy.wait()
    total = staged[0].astype(F32)
    for index in range(1, staged.shape[0]):
        total = total + staged[index].astype(F32)
    chans = weight_grad.shape[1]
    vectors = jnp.concatenate(
        [total[start : start + deep] for start in range(0, rows, deep)], axis=1
    )[:, :chans]
    vectors = vectors[:VECTORS_TWO] + vectors[VECTORS_TWO:]
    weight_grad[...] = vectors[:4]
    bias_grad[...] = vectors[4].reshape(chans)
    norm_grad = jnp.concatenate([vectors[5:6], vectors[6:7]], axis=1)
    norm_out[...] = norm_grad


def mixer_grad_kernel(
    place,
    piece_0,
    piece_1,
    piece_2,
    piece_3,
    residual_in,
    gain_ref,
    cotangent,
    out_proj,
    columns_out,
    mix_out,
    d_gated,
    gain_grad,
    d_send,
    turned,
):
    take_row_pieces(place, (piece_0, piece_1, piece_2, piece_3), d_send)
    residual = residual_in[...]
    inverse = rms_rate(residual)
    scaled = residual * inverse
    grad = d_send[...]
    pulled = grad * as_row(gain_ref)
    along = jnp.mean(pulled * scaled, axis=-1, keepdims=True)
    d_residual = cotangent[...].astype(F32) + inverse * (pulled - scaled * along)
    d_mix = d_residual.astype(BF16)
    put_blocks(mix_out, d_mix)
    d_gated[...] = dot_nt(d_mix, out_proj[...])
    gain_grad[...] = jnp.sum(grad * scaled, axis=0, keepdims=True)
    turned[...] = d_residual.T
    column = columns_out.shape[0]
    columns_out[...] = turned[pl.ds(pl.multiple_of(place[0] * column, column), column), :]


def split_vectors(vectors):
    upper = vectors.astype(BF16).astype(F32)
    return upper, vectors - upper


def scan_backward_kernel(
    d_gated,
    y_in,
    gate_in,
    act_in,
    mixed_in,
    masks,
    dt_proj,
    dt_bias,
    decay_log,
    skip_gain,
    gain_grad,
    d_mix,
    d_mixed_out,
    d_act_out,
    d_gate_out,
    share_out,
    rate,
    step_rows,
    decay_rows,
    drive_rows,
    dy_rows,
    du_rows,
    dl_rows,
    decays,
    history,
):
    rank = dt_proj.shape[0]
    states = decay_log.shape[0]
    length, chans = y_in.shape
    tiles = step_rows.shape[1] // 128
    full = 128 * tiles
    mixed = mixed_in[...]
    dt_low = mixed[:rank].astype(BF16)
    raw_step = dot_tn(dt_low, dt_proj[...]) + as_row(dt_bias)
    step_size = softplus(raw_step)
    act = act_in[...].astype(F32)
    reset = NEVER * (1.0 - wide_masks(masks, 0, chans))
    padded_copy(rate, -jnp.exp(decay_log[...]))
    padded_copy(step_rows, step_size)
    padded_copy(decay_rows, LOG2E * (step_size + reset))
    padded_copy(drive_rows, step_size * act)
    gate = gate_in[...]
    gate_sig = jax.nn.sigmoid(gate)
    d_out = d_gated[...]
    d_y = d_out * (gate * gate_sig)
    padded_copy(dy_rows, d_y)
    d_gate = d_out * y_in[...] * gate_sig * (1.0 + gate * (1.0 - gate_sig))
    b_turned = mixed[rank : rank + states]
    c_turned = mixed[rank + states : rank + 2 * states]
    history[pl.ds(0, states), :] = jnp.zeros((states, full), F32)

    def forward_block(index, state):
        start = pl.multiple_of(index * 8, 8)
        b_cols = block_columns(b_turned, index)
        steps = decay_rows[pl.ds(start, 8), :]
        drives = drive_rows[pl.ds(start, 8), :]
        for row in range(8):
            decay = jnp.exp2(rate[...] * steps[row : row + 1])
            state = decay * state + spread_column(b_cols, row, tiles) * drives[row : row + 1]
            at = pl.multiple_of((start + row) * states, states)
            decays[pl.ds(at, states), :] = decay
            history[pl.ds(at + states, states), :] = state
        return state

    lax.fori_loop(0, length // 8, forward_block, jnp.zeros((states, full), F32))
    lanes = lax.broadcasted_iota(jnp.int32, (states, length), 1)

    def backward_block(count, carry):
        carried, d_rate, d_b, d_c = carry
        index = length // 8 - 1 - count
        start = pl.multiple_of(index * 8, 8)
        b_cols = block_columns(b_turned, index)
        c_cols = block_columns(c_turned, index)
        steps = step_rows[pl.ds(start, 8), :]
        drives = drive_rows[pl.ds(start, 8), :]
        dys = dy_rows[pl.ds(start, 8), :]
        du = [None] * 8
        dl = [None] * 8
        for row in reversed(range(8)):
            at = pl.multiple_of((start + row) * states, states)
            before = history[pl.ds(at, states), :]
            after = history[pl.ds(at + states, states), :]
            decay = decays[pl.ds(at, states), :]
            here = lanes == start + row
            dy_row = jnp.broadcast_to(dys[row : row + 1], (states, full))
            grad = spread_column(c_cols, row, tiles) * dy_row + carried
            c_part = jnp.sum(fold_tiles(dy_row * after), axis=1, keepdims=True)
            d_c = jnp.where(here, c_part, d_c)
            b_part = jnp.sum(fold_tiles(grad * drives[row : row + 1]), axis=1, keepdims=True)
            d_b = jnp.where(here, b_part, d_b)
            du[row] = jnp.sum(grad * spread_column(b_cols, row, tiles), axis=0, keepdims=True)
            carried = grad * decay
            d_log = carried * before
            dl[row] = jnp.sum(d_log * rate[...], axis=0, keepdims=True)
            d_rate = d_rate + d_log * steps[row : row + 1]
        du_rows[pl.ds(start, 8), :] = jnp.concatenate(du, axis=0)
        dl_rows[pl.ds(start, 8), :] = jnp.concatenate(dl, axis=0)
        return carried, d_rate, d_b, d_c

    nothing = jnp.zeros((states, full), F32)
    thin = jnp.zeros((states, length), F32)
    _, d_rate, d_b, d_c = lax.fori_loop(
        0, length // 8, backward_block, (nothing, nothing, thin, thin)
    )
    du = du_rows[:, :chans]
    d_step = (dl_rows[:, :chans] + du * act) * jax.nn.sigmoid(raw_step)
    d_step_low = d_step.astype(BF16)
    low_turned = dot_nt(dt_proj[...], d_step_low)
    d_mixed_out[...] = jnp.concatenate([low_turned, d_b, d_c], axis=0).astype(BF16)
    d_act_out[...] = du * step_size + as_row(skip_gain) * d_y
    d_gate_low = d_gate.astype(BF16)
    d_gate_out[...] = d_gate_low
    width = d_mix.shape[0]
    share_out[:width] = d_mix[...]
    padded_copy(du_rows, d_gate_low.astype(F32))
    share_out[width : width + chans] = du_rows[...].T[:chans].astype(BF16)
    gain_rows = gain_grad[...]
    upper, lower = split_vectors(
        jnp.concatenate(
            [
                (d_rate * rate[...])[:, :chans],
                jnp.sum(d_step, axis=0, keepdims=True),
                jnp.sum(d_y * act, axis=0, keepdims=True),
                gain_rows[:, :chans],
                gain_rows[:, chans:],
                jnp.zeros((VECTORS_ONE - states - 4, chans), F32),
            ],
            axis=0,
        )
    )
    dl_rows[...] = jnp.zeros(dl_rows.shape, F32)
    dl_rows[:rank, :chans] = dot_nn(dt_low, d_step_low)
    dl_rows[rank : rank + VECTORS_ONE, :chans] = upper
    dl_rows[rank + VECTORS_ONE : rank + 2 * VECTORS_ONE, :chans] = lower
    share_out[width + chans :] = dl_rows[...].T[:chans].astype(BF16)


def leave_kernel(
    place,
    piece_0,
    piece_1,
    piece_2,
    piece_3,
    d_act_scan,
    d_gate,
    conv_in,
    inner_in,
    masks,
    x_proj,
    conv_weight,
    in_proj,
    rows_in,
    gain,
    shares,
    message,
    held,
    turned,
    padded,
):
    length, chans = inner_in.shape
    width = rows_in.shape[1]
    full = padded.shape[1]
    d_mixed = sum_pieces(place, (piece_0, piece_1, piece_2, piece_3), held).astype(BF16)
    d_act = d_act_scan[...] + dot_tn(d_mixed, x_proj[...])
    conv = conv_in[...]
    sig = jax.nn.sigmoid(conv)
    d_conv = d_act * sig * (1.0 + conv * (1.0 - sig))
    inner = inner_in[...]
    d_inner = conv_weight[3:4, :] * d_conv
    weight_grads = [jnp.sum(d_conv * inner, axis=0, keepdims=True)]
    for shift in (1, 2, 3):
        masked = d_conv * wide_masks(masks, shift, chans)
        weight_grads.append(
            jnp.sum(masked * pltpu.roll(inner, shift, 0), axis=0, keepdims=True)
        )
        d_inner = d_inner + conv_weight[3 - shift : 4 - shift, :] * pltpu.roll(
            masked, length - shift, 0
        )
    d_inner_low = d_inner.astype(BF16)
    padded_copy(padded, d_inner_low.astype(F32))
    message[:chans] = padded[...].T[:chans].astype(BF16)
    proj = d_mixed.shape[0]
    top = message.shape[0] - full // 128 * 2 * VECTORS_TWO
    message[chans:top] = jnp.concatenate(
        [d_mixed.astype(F32), jnp.zeros((top - chans - proj, length), F32)], axis=0
    ).astype(BF16)
    d_normed = dot_nn(d_inner_low, in_proj[0]) + dot_nn(d_gate[...], in_proj[1])
    rows = rows_in[...].astype(F32)
    scaled = rows * rms_rate(rows)
    norm_grad = jnp.sum(d_normed * scaled, axis=0, keepdims=True)
    upper, lower = split_vectors(
        jnp.concatenate(
            [
                weight_grads[3],
                weight_grads[2],
                weight_grads[1],
                weight_grads[0],
                jnp.sum(d_conv, axis=0, keepdims=True),
                norm_grad[:, :chans],
                norm_grad[:, chans:],
                jnp.zeros((VECTORS_TWO - 7, chans), F32),
            ],
            axis=0,
        )
    )
    padded_copy(padded, jnp.zeros((length, chans), F32))
    padded[:VECTORS_TWO, :chans] = upper
    padded[VECTORS_TWO : 2 * VECTORS_TWO, :chans] = lower
    for tile in range(full // 128):
        message[top + tile * 2 * VECTORS_TWO : top + (tile + 1) * 2 * VECTORS_TWO] = padded[
            : 2 * VECTORS_TWO, tile * 128 : (tile + 1) * 128
        ].astype(BF16)
    along = jnp.mean(d_normed * as_row(gain) * scaled, axis=-1, keepdims=True)
    along = jnp.broadcast_to(along, (length, length)).T[:8]
    high = along.astype(BF16)
    low = (along - high.astype(F32)).astype(BF16)
    turned[...] = d_normed.T
    count, rows, _ = shares.shape
    column = width // count
    ends = jnp.concatenate([high, low], axis=0)
    for index in range(count):
        shares[index, :column, :] = turned[index * column : (index + 1) * column].astype(BF16)
        shares[index, column:, :] = ends


def finish_rows_kernel(pieces, residual, d_columns, tokens, scale, gain, outcome, grad_tokens):
    column = tokens.shape[0]
    total = pieces[0].astype(F32)
    for index in range(1, pieces.shape[0]):
        total = total + pieces[index].astype(F32)
    along = total[column : column + 1] + total[column + 8 : column + 9]
    inverse = scale[...]
    pulled = total[:column] * gain[...]
    scaled = tokens[...].astype(F32) * inverse
    grad_tokens[...] = d_columns[...] + inverse * (pulled - scaled * along)
    outcome[...] = (residual[...] + total[column + 16 :]).astype(BF16)


def take_blocks(target, pieces):
    for index, piece in enumerate(pieces):
        for start in range(0, target.shape[1], 128):
            target[index * 128 : (index + 1) * 128, start : start + 128] = piece[
                start : start + 128
            ]


def take_turned(target, pieces, start):
    rows = target.shape[0]
    for index, piece in enumerate(pieces):
        target[:, index * 128 : (index + 1) * 128] = piece[start : start + rows]


def stage_pieces(refs, staged, semaphores, rows=None):
    copies = []
    parts = len(refs) // 2
    for index, ref in enumerate(refs):
        side, part = divmod(index, parts)
        target = staged.at[4 * side + min(part, 3)]
        if part >= 3 and parts > 4:
            height = staged.shape[1] // (parts - 3)
            target = target.at[pl.ds((part - 3) * height, height)]
        copies.append((ref if rows is None else ref.at[pl.ds(*rows)], target))
    return run_copies(copies, semaphores), [staged.at[index] for index in range(8)]


def first_sets_kernel(refs, normed, gated, acts, staged, semaphores):
    chans = gated.shape[0]
    width = normed.shape[1]
    arriving, firsts = stage_pieces(refs, staged, semaphores)
    for copy in arriving:
        copy.wait()
    take_blocks(normed, firsts)
    take_turned(gated, firsts, width)
    take_turned(acts, firsts, width + chans)


def wide_grads_kernel(
    sizes,
    second_refs,
    last_refs,
    normed,
    gated,
    acts,
    out_grad,
    in_grad,
    x_grad,
    dt_grad,
    bias_grad,
    decay_grad,
    skip_grad,
    norm_grad,
    staged,
    staged_last,
    mixed,
    d_gate,
    d_mixed,
    total,
    wide_grad,
    second_arrivals,
    last_arrivals,
    semaphores,
):
    rank, states, proj = sizes
    chans, width = out_grad.shape
    arriving_last, lasts = stage_pieces(last_refs, staged_last, last_arrivals)
    arriving, seconds = stage_pieces(second_refs, staged, second_arrivals)
    for copy in arriving_last:
        copy.wait()
    take_turned(d_gate, lasts, 0)
    wide_grad[0] = dot_nn(d_gate[...], normed[...])
    started = run_copies([(wide_grad.at[0], in_grad.at[0])], semaphores)
    take_turned(d_mixed, lasts, chans)
    x_grad[...] = dot_nt(d_mixed[...], acts[...])[:proj]
    for copy in arriving:
        copy.wait()
    take_turned(d_gate, seconds, width)
    wide_grad[1] = dot_nn(d_gate[...], normed[...])
    started += run_copies([(wide_grad.at[1], in_grad.at[1])], semaphores.at[pl.ds(1, 1)])
    take_blocks(mixed, seconds)
    half = chans // 2
    for index in range(2):
        rows = pl.ds(index * half, half)
        wide_grad[2, rows] = dot_nn(gated[rows], mixed[...])
        started += run_copies(
            [(wide_grad.at[2, rows], out_grad.at[rows])], semaphores.at[pl.ds(2 + index, 1)]
        )
    vectors = seconds[0][width + chans :].astype(F32)
    for piece in seconds[1:]:
        vectors = vectors + piece[width + chans :].astype(F32)
    total[...] = jnp.zeros(total.shape, F32)
    total[:chans] = vectors
    rows = total[...].T[:, :chans]
    dt_grad[...] = rows[:rank]
    rows = rows[rank : rank + VECTORS_ONE] + rows[rank + VECTORS_ONE : rank + 2 * VECTORS_ONE]
    decay_grad[...] = rows[:states]
    bias_grad[...] = rows[states].reshape(chans)
    skip_grad[...] = rows[states + 1].reshape(chans)
    norm_grad[...] = jnp.concatenate(
        [rows[states + 2 : states + 3], rows[states + 3 : states + 4]], axis=1
    )
    for copy in started:
        copy.wait()


def send_chunks(chunks):
    count = len(chunks)
    pairs = [[(i, (i + s) % count) for i in range(count)] for s in range(count)]
    return [chunks[0]] + [lax.ppermute(chunks[s], "tensor", pairs[s]) for s in range(1, count)]


def share_rows(values, count):
    return send_chunks([values] * count)


def add_low(pieces):
    total = pieces[0].astype(F32)
    for piece in pieces[1:]:
        total = total + piece.astype(F32)
    return total.astype(BF16)


def after(values, *events):
    return list(lax.optimization_barrier((tuple(values), events))[0])


def swap(values, bits):
    return lax.ppermute(values, "dp", [(i, i ^ bits) for i in range(NEAR_GROUPS)])


def split_beside(along_x, along_y):
    half = along_x.shape[0] // 2
    return along_y[:half], along_x[half:]


def swap_across(halves):
    return [swap(halves[0], 2), swap(halves[1], 4)]


def swap_near(values):
    return [*values, *[swap(part, 1) for part in values]]


def body(
    tokens,
    resets,
    routes,
    norm_one,
    in_proj,
    conv_weight,
    conv_bias,
    x_proj,
    dt_proj,
    dt_bias,
    decay_log,
    skip_gain,
    out_proj,
    norm_two,
    expert_in,
    expert_out,
    cotangent,
):
    groups = lax.axis_size("dp")
    parts = lax.axis_size("tensor")
    place = lax.axis_index("tensor").astype(jnp.int32).reshape(1)
    length, column = tokens.shape
    width = norm_one.shape[0]
    rank, chans = dt_proj.shape
    states = decay_log.shape[0]
    experts, share, hidden_units = expert_in.shape
    proj = x_proj.shape[1]
    tile_count = groups // experts
    block_rows = length * experts // groups
    capacity = max(2, block_rows // 4)
    slot_count = groups * capacity
    tiles = -(-chans // 128)
    full = 128 * tiles
    near = groups == NEAR_GROUPS and experts == groups
    tokens_turned = tokens.T
    in_turned = jnp.swapaxes(in_proj, 1, 2)
    x_turned = x_proj.T
    resets_row = resets.reshape(1, length)
    routes_row = routes.reshape(1, length)

    def exchange(values):
        return lax.all_to_all(values, "dp", split_axis=0, concat_axis=0, tiled=True)

    def exchange_slots(slots):
        return exchange(slots.reshape(groups, capacity, width)).reshape(slot_count, width)

    token_pieces = share_rows(tokens_turned, parts)
    mask_out = ((4, length, 128), F32)
    choose_out = ((slot_count, length), BF16)
    weight_outs = [((width, hidden_units), BF16)] * 2
    slots_out = ((slot_count, width), BF16)
    hidden_out = ((slot_count, hidden_units), BF16)
    folded = capacity + capacity // 2
    message_out = ((groups, 2 * share + folded, hidden_units), BF16)
    if near:
        masks, choose, packed = run_kernel(
            functools.partial(pack_kernel, capacity),
            [mask_out, choose_out, message_out],
            [resets_row, routes_row, cotangent, expert_in, expert_out],
            [
                ((groups, folded, hidden_units), BF16),
                ((experts, 2, share, hidden_units), BF16),
                pltpu.SemaphoreType.DMA((2 * experts,)),
                pltpu.SemaphoreType.DMA((3 * experts,)),
            ],
            far_args=(3, 4),
            far_outs=(2,), staged=(0, 1, 2))
        weights = exchange(packed)
    else:
        masks, choose, grad_send = run_kernel(
            functools.partial(prepare_kernel, experts, capacity, block_rows),
            [mask_out, choose_out, slots_out],
            [resets_row, routes_row, cotangent], loose_outs=(2,))
        first_w = exchange(jnp.tile(expert_in, (tile_count, 1, 1))).reshape(weight_outs[0][0])
        second_w = exchange(jnp.tile(expert_out, (tile_count, 1, 1))).reshape(weight_outs[0][0])
        grad_slots = exchange_slots(grad_send)
        (d_hidden,) = run_kernel(
            hidden_back_kernel, [((slot_count, hidden_units), F32)], [grad_slots, second_w]
        )

    rows, normed, act, inner, conv, gate, scale, gain_columns, mixed_part = run_kernel(
        enter_kernel,
        [
            ((length, width), BF16),
            ((width, length), BF16),
            ((length, chans), BF16),
            ((length, chans), F32),
            ((length, chans), F32),
            ((length, chans), F32),
            ((1, length), F32),
            ((column, length), F32),
            ((proj, length), BF16),
        ],
        [place, *token_pieces, norm_one, in_turned, conv_weight, conv_bias, x_turned, masks],
        [((width, length), F32)],
        scalars=1, loose_outs=(8,), staged=(1, 2, 3, 4, 10))
    mixed_pieces = share_rows(mixed_part, parts)
    *mix_chunks, mixed, first, y = run_kernel(
        scan_forward_kernel,
        [((length // parts, width), BF16)] * parts
        + [
            ((proj, length), F32),
            ((width + 2 * chans, length), BF16),
            ((length, chans), F32),
        ],
        [
            place,
            *mixed_pieces,
            dt_proj,
            dt_bias,
            decay_log,
            skip_gain,
            act,
            gate,
            masks,
            out_proj,
            normed,
        ],
        [
            ((parts, proj, length), BF16),
            ((states, full), F32),
            ((length, full), F32),
            ((length, full), F32),
            ((length, full), F32),
            ((length, width), F32),
        ],
        scalars=1, loose_outs=(0, 1, 2, 3, 5), staged=(1, 2, 3, 4, 9, 10, 11, 13))
    mixer_pieces = share_rows(add_low(send_chunks(mix_chunks)), parts)
    if near:
        first_x, first_y = swap(first, 2), swap(first, 4)
    residual, residual_columns, send_slots = run_kernel(
        dispatch_kernel,
        [((length, width), F32), ((column, length), F32), slots_out],
        [place, *mixer_pieces, rows, norm_two, choose],
        [((width, length), F32)],
        scalars=1, loose_outs=(2,), staged=(1, 2, 3, 4, 5, 7))
    if near:
        first_w, second_w, grad_slots, d_hidden = run_kernel(
            functools.partial(unpack_kernel, share, capacity),
            weight_outs + [slots_out, ((slot_count, hidden_units), F32)],
            after([weights], send_slots, first_x, first_y),
            [*weight_outs, slots_out, pltpu.SemaphoreType.DMA((5 * groups,))],
            far_args=(0,),
            far_outs=(0, 1, 2),
        )
    arrived = exchange_slots(send_slots)
    hidden, d_pre, d_slots = run_kernel(
        expert_kernel, [hidden_out, hidden_out, slots_out], [arrived, first_w, d_hidden], loose_outs=(2,), staged=(0, 1, 2))
    back_slots = exchange_slots(d_slots)
    grad_args = [arrived, grad_slots, hidden, d_pre, second_w]
    grad_out = ((experts, share, hidden_units), F32)
    if near:
        (packed,) = run_kernel(
            functools.partial(expert_grads_pack_kernel, share, capacity),
            [message_out],
            grad_args,
            [
                ((2, width, hidden_units), BF16),
                ((groups, folded, hidden_units), BF16),
                pltpu.SemaphoreType.DMA((3 * groups,)),
            ],
            far_outs=(0,), staged=range(5))
        first_d = swap_across(split_beside(*after([first_x, first_y], arrived)))
        back_slots = after([back_slots], packed, first_d)[0]
        packed = after([packed], back_slots)[0]
        owned = exchange(packed)
    else:
        grad_first, grad_second, moe_slots = run_kernel(
            expert_grads_kernel, weight_outs + [slots_out], grad_args, loose_outs=(0, 1, 2))
    back_chunks = run_kernel(
        back_rows_kernel,
        [((length // parts, width), BF16)] * parts,
        [place, choose, back_slots],
        [((length, width), F32)],
        scalars=1, loose_outs=(0, 1, 2, 3), staged=(1, 2))
    send_pieces = share_rows(add_low(send_chunks(back_chunks)), parts)
    if near:
        firsts = swap_near([first, first_x, first_y, *first_d])

        send_pieces = after(send_pieces, firsts)
    d_columns, d_mix, d_gated, gain_grad_two = run_kernel(
        mixer_grad_kernel,
        [
            ((column, length), F32),
            ((width, length), BF16),
            ((length, chans), F32),
            ((1, width), F32),
        ],
        [place, *send_pieces, residual, norm_two, cotangent, out_proj],
        [((length, width), F32), ((width, length), F32)],
        scalars=1, staged=(1, 2, 3, 4, 5, 7, 8), held_outs=(1, 2, 3))
    d_mixed_part, d_act_scan, d_gate, second = run_kernel(
        scan_backward_kernel,
        [
            ((proj, length), BF16),
            ((length, chans), F32),
            ((length, chans), BF16),
            ((width + 2 * chans, length), BF16),
        ],
        [
            d_gated,
            y,
            gate,
            act,
            mixed,
            masks,
            dt_proj,
            dt_bias,
            decay_log,
            skip_gain,
            gain_grad_two,
            d_mix,
        ],
        [
            ((states, full), F32),
            ((length, full), F32),
            ((length, full), F32),
            ((length, full), F32),
            ((length, full), F32),
            ((length, full), F32),
            ((length, full), F32),
            ((length * states, full), F32),
            (((length + 1) * states, full), F32),
        ], loose_outs=(0, 3), staged=(1, 2, 3, 4, 5, 6), held_outs=(1, 2))
    d_mixed_pieces = share_rows(d_mixed_part, parts)
    if near:
        second_x, second_y = swap(second, 2), swap(second, 4)
    last_rows = chans + -(-proj // 16) * 16 + tiles * 2 * VECTORS_TWO
    normed_shares, message = run_kernel(
        leave_kernel,
        [((parts, column + 16, length), BF16), ((last_rows, length), BF16)],
        [
            place,
            *d_mixed_pieces,
            d_act_scan,
            d_gate,
            conv,
            inner,
            masks,
            x_turned,
            conv_weight,
            in_turned,
            rows,
            norm_one,
        ],
        [((parts, proj, length), BF16), ((width, length), F32), ((length, full), F32)],
        scalars=1, loose_outs=(0, 1), staged=(1, 2, 3, 4, 7, 8, 9, 13))
    shares_out = ((parts, 2 * column + 16, length), BF16)
    if near:
        (shares,) = run_kernel(
            functools.partial(back_folded_kernel, share),
            [shares_out],
            [choose, normed_shares, owned],
            [slots_out, pltpu.SemaphoreType.DMA((3 * groups,))],
            staged=(0,),
            far_args=(2,),
            loose_outs=(0,),
        )
        grad_expert_in, grad_expert_out = run_kernel(
            functools.partial(owner_kernel, share),
            [grad_out] * 2,
            after([owned], shares),
            [
                ((groups, 2 * share, hidden_units), BF16),
                ((groups, 2 * share, hidden_units), F32),
                pltpu.SemaphoreType.DMA((groups,)),
                pltpu.SemaphoreType.DMA((2 * groups,)),
            ],
            far_args=(0,),
            far_outs=(0, 1),
        )
        second, second_x, second_y = after([second, second_x, second_y], grad_expert_in)
        halves = split_beside(second_x, second_y)
        last = after([message], second_x, second_y)[0]
        lasts = [last, swap(last, 2), swap(last, 4), swap(last, 6)]
        second_d = swap_across(halves)
        *seconds, near_own, near_x, near_y = swap_near([second, second_x, second_y])
        firsts = after(firsts, halves, near_own, near_x, near_y)

        def first_sets(*refs):
            first_sets_kernel(refs[:10], *refs[10:])

        all_normed, all_gated, all_act = run_kernel(
            first_sets,
            [
                ((groups * length, width), BF16),
                ((chans, groups * length), BF16),
                ((chans, groups * length), BF16),
            ],
            firsts,
            [((groups, width + 2 * chans, length), BF16), pltpu.SemaphoreType.DMA((10,))],
            far_args=range(10),
        )
    else:
        (shares,) = run_kernel(
            back_columns_kernel,
            [shares_out],
            [choose, normed_shares, exchange_slots(moe_slots)],
            loose_outs=(0,),
        )

        def owner_sum(values):
            got = exchange(values.reshape(groups, share, hidden_units)).astype(F32)
            return jnp.sum(got.reshape(tile_count, experts, share, hidden_units), axis=0)

        grad_expert_in = owner_sum(grad_first)
        grad_expert_out = owner_sum(grad_second)
    shares_made = shares
    shares = lax.all_to_all(shares, "tensor", split_axis=0, concat_axis=0, tiled=True)
    outcome, grad_tokens = run_kernel(
        finish_rows_kernel,
        [((column, length), BF16), ((column, length), F32)],
        [shares, residual_columns, d_columns, tokens_turned, scale, gain_columns],
        staged=range(6),
        loose_outs=(0, 1),
    )

    if near:
        lasts, second_d = after([lasts, second_d], all_normed, grad_tokens)
        lasts = swap_near(lasts)
        near_d = [swap(part, 1) for part in second_d]
        seconds = [*seconds, *second_d, near_own, near_x, near_y, *near_d]

        def late_vectors(*refs):
            late_vectors_kernel(refs[:groups], *refs[groups:])

        grad_conv_weight, grad_conv_bias, norm_shares = run_kernel(
            late_vectors,
            [((4, chans), F32), ((chans,), F32), ((1, width), F32)],
            lasts,
            [
                ((groups, tiles * 2 * VECTORS_TWO, length), BF16),
                pltpu.SemaphoreType.DMA((groups,)),
            ],
            far_args=range(groups),
            loose_outs=(0, 1, 2),
        )
        norm_parts = share_rows(after([norm_shares], near_d)[0], parts)

        def wide_grads(*refs):
            wide_grads_kernel(
                (rank, states, proj), refs[:10], refs[10 : 10 + groups], *refs[10 + groups :]
            )

        (
            grad_out_proj,
            grad_in_turned,
            grad_x_turned,
            grad_dt_proj,
            grad_dt_bias,
            grad_decay_log,
            grad_skip_gain,
            grad_norm_two,
        ) = run_kernel(
            wide_grads,
            [
                ((chans, width), F32),
                ((2, chans, width), F32),
                ((proj, chans), F32),
                ((rank, chans), F32),
                ((chans,), F32),
                ((states, chans), F32),
                ((chans,), F32),
                ((1, width), F32),
            ],
            [*after(seconds, norm_shares), *lasts, all_normed, all_gated, all_act],
            [
                ((groups, width + 2 * chans, length), BF16),
                ((groups, last_rows, length), BF16),
                ((groups * length, width), BF16),
                ((chans, groups * length), BF16),
                ((-(-proj // 16) * 16, groups * length), BF16),
                ((full, length), F32),
                ((3, chans, width), F32),
                pltpu.SemaphoreType.DMA((10,)),
                pltpu.SemaphoreType.DMA((groups,)),
                pltpu.SemaphoreType.DMA((4,)),
            ],
            far_args=range(10 + groups),
            far_outs=(0, 1),
            loose_outs=range(8),
        )
        grad_norm_one = sum(norm_parts).reshape(width)
    else:
        top = last_rows - tiles * 2 * VECTORS_TWO
        ones = second[width + chans :].astype(F32).T
        twos = message[top:].astype(F32).reshape(tiles, 2 * VECTORS_TWO, length)
        twos = jnp.swapaxes(twos, 0, 1).reshape(2 * VECTORS_TWO, full)[:, :chans]
        plain_normed = jnp.swapaxes(normed.reshape(-1, length, 128), 0, 1).reshape(length, width)
        plain_mix = jnp.swapaxes(d_mix.reshape(-1, length, 128), 0, 1).reshape(length, width)
        grad_in_turned, grad_x_turned, grad_dt_proj, grad_out_proj, ones, twos = lax.psum(
            (
                jnp.stack(
                    [
                        dot_nn(message[:chans], plain_normed),
                        dot_nn(second[width : width + chans], plain_normed),
                    ]
                ),
                dot_nn(message[chans : chans + proj], act),
                ones[:rank],
                dot_nn(first[width : width + chans], plain_mix),
                ones[rank : rank + VECTORS_ONE]
                + ones[rank + VECTORS_ONE : rank + 2 * VECTORS_ONE],
                twos[:VECTORS_TWO] + twos[VECTORS_TWO:],
            ),
            "dp",
        )
        grad_decay_log = ones[:states]
        grad_dt_bias = ones[states]
        grad_skip_gain = ones[states + 1]
        grad_norm_two = ones[states + 2 : states + 4]
        grad_conv_weight = twos[:4]
        grad_conv_bias = twos[4]
        grad_norm_one = sum(share_rows(twos[5:7].reshape(1, width), parts)).reshape(width)
    return (
        outcome.T,
        grad_tokens.T,
        grad_norm_one,
        jnp.swapaxes(grad_in_turned, 1, 2),
        grad_conv_weight,
        grad_conv_bias,
        grad_x_turned.T,
        grad_dt_proj,
        grad_dt_bias,
        grad_decay_log,
        grad_skip_gain,
        grad_out_proj,
        grad_norm_two.reshape(width),
        grad_expert_in,
        grad_expert_out,
    )


def solution(mesh):
    placed = (
        P("dp", "tensor"),
        P("dp"),
        P("dp", None),
        P(),
        P(None, None, "tensor"),
        P(None, "tensor"),
        P("tensor"),
        P("tensor", None),
        P(None, "tensor"),
        P("tensor"),
        P(None, "tensor"),
        P("tensor"),
        P("tensor", None),
        P(),
        P(None, "dp", "tensor"),
        P(None, "dp", "tensor"),
        P("dp", None),
    )
    return jax.shard_map(
        body,
        mesh=mesh,
        in_specs=placed,
        out_specs=(
            P("dp", "tensor"),
            P("dp", "tensor"),
            P(),
            P(None, None, "tensor"),
            P(None, "tensor"),
            P("tensor"),
            P("tensor", None),
            P(None, "tensor"),
            P("tensor"),
            P(None, "tensor"),
            P("tensor"),
            P("tensor", None),
            P(),
            P(None, "dp", "tensor"),
            P(None, "dp", "tensor"),
        ),
        check_vma=False,
    )
```

```python
import functools
import math

import jax
import jax.numpy as jnp
from jax import lax
from jax.experimental import pallas as pl
from jax.experimental.pallas import tpu as pltpu
from jax.sharding import PartitionSpec as P

EPSILON = 1e-05
F32 = jnp.float32
BF16 = jnp.bfloat16
NEVER = 1e4
LOG2E = 1.4426950408889634
GELU_SCALE = math.sqrt(2.0 / math.pi)
GELU_CUBE = 0.044715
VMEM_SPARE = 6 * 1024 * 1024
NEAR_GROUPS = 8
VECTORS_ONE = 24
VECTORS_TWO = 8
NORM_ROWS = 16


def run_kernel(
    kernel,
    outs,
    args,
    scratch=(),
    scalars=0,
    far_args=(),
    staged=(),
    far_outs=(),
    loose_outs=(),
    held_outs=(),
    alias=None,
):
    staged = tuple(staged)
    outside = {*far_args, *staged}

    def spec(index, far):
        return pl.BlockSpec(memory_space=pltpu.HBM if index in far else pltpu.VMEM)

    def held(index, shape, dtype):
        if index in loose_outs:
            return jax.ShapeDtypeStruct(shape, dtype)
        return (pltpu.VMEM if index in held_outs else pltpu.HBM)(shape, dtype)

    def body(*refs):
        refs = list(refs)
        if staged:
            *refs, semaphores = refs
            places = refs[len(refs) - len(staged) :]
            refs = refs[: len(refs) - len(staged)]
            copies = run_copies(list(zip([refs[index] for index in staged], places)), semaphores)
            for index, place in zip(staged, places):
                refs[index] = place
            for copy in copies:
                copy.wait()
        kernel(*refs)

    sizes = [(arg.shape, arg.dtype) for index, arg in enumerate(args) if index not in far_args]
    sizes += [out for index, out in enumerate(outs) if index not in far_outs]
    sizes += [shape for shape in scratch if isinstance(shape, tuple)]
    scratch = [pltpu.VMEM(*shape) if isinstance(shape, tuple) else shape for shape in scratch]
    if staged:
        scratch += [pltpu.VMEM(args[index].shape, args[index].dtype) for index in staged]
        scratch += [pltpu.SemaphoreType.DMA((len(staged),))]
    needed = sum(math.prod(shape) * jnp.dtype(dtype).itemsize for shape, dtype in sizes)
    return pl.pallas_call(
        body,
        out_shape=[held(index, shape, dtype) for index, (shape, dtype) in enumerate(outs)],
        in_specs=[
            pl.BlockSpec(memory_space=pltpu.SMEM) if index < scalars else spec(index, outside)
            for index in range(len(args))
        ],
        out_specs=[spec(index, far_outs) for index in range(len(outs))],
        scratch_shapes=scratch,
        input_output_aliases=alias or {},
        compiler_params=pltpu.CompilerParams(vmem_limit_bytes=VMEM_SPARE + needed * 5 // 4),
    )(
        *[
            pltpu.with_memory_space_constraint(arg, pltpu.HBM) if index in outside else arg
            for index, arg in enumerate(args)
        ]
    )


def dot_nn(left, right):
    return lax.dot_general(left, right, (((1,), (0,)), ((), ())), preferred_element_type=F32)


def dot_nt(left, right):
    return lax.dot_general(left, right, (((1,), (1,)), ((), ())), preferred_element_type=F32)


def dot_tn(left, right):
    return lax.dot_general(left, right, (((0,), (0,)), ((), ())), preferred_element_type=F32)


def lane_tiles(column, tiles):
    return jnp.concatenate([column] * tiles, axis=1)


def fold_tiles(values):
    total = values[:, :128]
    for tile in range(1, values.shape[1] // 128):
        total = total + values[:, 128 * tile : 128 * (tile + 1)]
    return total


def wide_masks(masks, index, chans):
    return lane_tiles(masks[index], -(-chans // 128))[:, :chans]


def rms_rate(values):
    return lax.rsqrt(jnp.mean(values * values, axis=-1, keepdims=True) + EPSILON)


def as_row(ref):
    return ref[...].reshape(1, ref.shape[0])


def softplus(values):
    return jnp.maximum(values, 0.0) + jnp.log1p(jnp.exp(-jnp.abs(values)))


def padded_copy(target, values):
    target[...] = jnp.zeros(target.shape, target.dtype)
    target[:, : values.shape[1]] = values


def put_row_chunks(place, source, outs):
    count = len(outs)
    rows = source.shape[0] // count
    for step, out in enumerate(outs):
        start = pl.multiple_of(lax.rem(place[0] + step, count) * rows, rows)
        out[pl.ds(0, rows), :] = source[pl.ds(start, rows), :].astype(out.dtype)


def take_row_pieces(place, pieces, target):
    count = len(pieces)
    rows = target.shape[0] // count
    for step, piece in enumerate(pieces):
        start = pl.multiple_of(lax.rem(place[0] - step + count, count) * rows, rows)
        target[pl.ds(start, rows), :] = piece[...].astype(target.dtype)


def sum_pieces(place, pieces, held):
    count = len(pieces)
    for step, piece in enumerate(pieces):
        held[lax.rem(place[0] - step + count, count)] = piece[...]
    total = held[0].astype(F32)
    for index in range(1, count):
        total = total + held[index].astype(F32)
    return total


def run_copies(copies, semaphores):
    started = []
    for index, (source, target) in enumerate(copies):
        copy = pltpu.make_async_copy(source, target, semaphores.at[index])
        copy.start()
        started.append(copy)
    return started


def fill_masks(resets, masks):
    length = resets.shape[1]
    square = (length, length)
    earlier = lax.broadcasted_iota(jnp.int32, square, 0)
    reset = jnp.broadcast_to(resets[...].astype(F32), square).T
    keep = jnp.where(reset == 0.0, 1.0, 0.0)
    joined = jnp.where(earlier > 0, keep, 0.0)
    one_back = pltpu.roll(joined, 1, 0)
    two_back = pltpu.roll(joined, 2, 0)
    masks[0] = keep
    masks[1] = joined
    masks[2] = joined * one_back
    masks[3] = joined * one_back * two_back


def fill_choose(capacity, block_rows, experts, routes, choose):
    length = routes.shape[1]
    square = (length, length)
    earlier = lax.broadcasted_iota(jnp.int32, square, 0)
    later = lax.broadcasted_iota(jnp.int32, square, 1)
    route_of = jnp.broadcast_to(routes[...].astype(F32), square)
    same = (route_of.T == route_of) & (earlier < later)
    if block_rows < length:
        same = same & (earlier // block_rows == later // block_rows)
    rank = jnp.sum(jnp.where(same, 1.0, 0.0), axis=0, keepdims=True).astype(jnp.int32)
    group = routes[...]
    if block_rows < length:
        group = group + experts * (later[:1] // block_rows)
    slot = group * capacity + rank
    slot_count = choose.shape[0]
    slot_ids = lax.broadcasted_iota(jnp.int32, (slot_count, length), 0)
    hit = slot_ids == jnp.broadcast_to(slot, (slot_count, length))
    choose[...] = jnp.where(hit, 1.0, 0.0).astype(BF16)


def prepare_kernel(
    experts, capacity, block_rows, resets, routes, cotangent, masks, choose, slots
):
    fill_masks(resets, masks)
    fill_choose(capacity, block_rows, experts, routes, choose)
    slots[...] = dot_nn(choose[...], cotangent[...]).astype(BF16)


def put_folded(target, slots):
    rows, width = slots.shape
    units = target.shape[1]
    half = rows // 2
    rest = width - units
    target[:rows, :] = slots[:, :units]
    target[rows:, :rest] = slots[:half, units:]
    target[rows:, rest:] = slots[half:, units:]


def unfold_copies(source, target, top, rows):
    units = source.shape[1]
    half = rows // 2
    rest = target.shape[1] - units
    copies = [(source.at[pl.ds(0, rows)], target.at[pl.ds(top, rows), pl.ds(0, units)])]
    for part in range(2):
        copies.append(
            (
                source.at[pl.ds(rows, half), pl.ds(part * rest, rest)],
                target.at[pl.ds(top + part * half, half), pl.ds(units, rest)],
            )
        )
    return copies


def pack_kernel(
    capacity,
    resets,
    routes,
    cotangent,
    expert_in,
    expert_out,
    masks,
    choose,
    message,
    packed,
    staged,
    arrivals,
    semaphores,
):
    experts, share, units = expert_in.shape
    length, width = cotangent.shape
    copies = []
    for index in range(experts):
        copies.append((expert_in.at[index], staged.at[index, 0]))
        copies.append((expert_out.at[index], staged.at[index, 1]))
    arriving = run_copies(copies, arrivals)
    fill_choose(capacity, length, experts, routes, choose)
    slots = dot_nn(choose[...], cotangent[...]).astype(BF16)
    started = []
    for index in range(experts):
        copies = []
        for which in range(2):
            arriving[2 * index + which].wait()
            target = message.at[index, pl.ds(which * share, share)]
            copies.append((staged.at[index, which], target))
        started += run_copies(copies, semaphores.at[pl.ds(2 * index, 2)])
    copies = []
    for index in range(experts):
        put_folded(packed.at[index], slots[index * capacity : (index + 1) * capacity])
        target = message.at[index]
        copies.append((packed.at[index], target.at[pl.ds(2 * share, packed.shape[1])]))
    started += run_copies(copies, semaphores.at[pl.ds(2 * experts, experts)])
    fill_masks(resets, masks)
    for copy in started:
        copy.wait()


def pass_on(along_x, along_y, pass_y, pass_x, passed, arrivals, semaphores):
    half = passed.shape[1]
    copies = [
        (along_y.at[pl.ds(0, half)], passed.at[0]),
        (along_x.at[pl.ds(half, half)], passed.at[1]),
    ]
    for copy in run_copies(copies, arrivals):
        copy.wait()
    return run_copies([(passed.at[0], pass_y), (passed.at[1], pass_x)], semaphores)


def unpack_kernel(
    share,
    capacity,
    message,
    along_x,
    along_y,
    first_out,
    second_out,
    slots_out,
    pass_y,
    pass_x,
    d_hidden,
    first_w,
    second_w,
    grad_slots,
    passed,
    pass_semaphores,
    semaphores,
):
    started = pass_on(
        along_x,
        along_y,
        pass_y,
        pass_x,
        passed,
        pass_semaphores.at[pl.ds(0, 2)],
        pass_semaphores.at[pl.ds(2, 2)],
    )
    folded = capacity + capacity // 2
    copies = []
    for index in range(message.shape[0]):
        piece = message.at[index]
        rows = pl.ds(index * share, share)
        copies.append((piece.at[pl.ds(share, share)], second_w.at[rows]))
        copies += unfold_copies(
            piece.at[pl.ds(2 * share, folded)], grad_slots, index * capacity, capacity
        )
        copies.append((piece.at[pl.ds(0, share)], first_w.at[rows]))
    for copy in run_copies(copies, semaphores):
        copy.wait()
    copies = [(first_w, first_out), (second_w, second_out), (grad_slots, slots_out)]
    started += run_copies(copies, semaphores)
    d_hidden[...] = dot_nn(grad_slots[...], second_w[...])
    for copy in started:
        copy.wait()


def put_blocks(target, values):
    length = values.shape[0]
    for start in range(0, values.shape[1], 128):
        target[start : start + length, :] = values[:, start : start + 128]


def enter_kernel(
    place,
    piece_0,
    piece_1,
    piece_2,
    piece_3,
    gain_ref,
    in_proj,
    conv_weight,
    conv_bias,
    x_proj,
    masks,
    rows_out,
    normed_out,
    act_out,
    inner_out,
    conv_out,
    gate_out,
    scale_out,
    gain_out,
    mixed_out,
    turned,
):
    take_row_pieces(place, (piece_0, piece_1, piece_2, piece_3), turned)
    rows = turned[...].T
    gain = as_row(gain_ref)
    rows_out[...] = rows.astype(BF16)
    normed = (rows * rms_rate(rows) * gain).astype(BF16)
    put_blocks(normed_out, normed)
    inner = dot_nt(normed, in_proj[0])
    chans = inner.shape[1]
    inner_out[...] = inner
    total = as_row(conv_bias) + conv_weight[3:4, :] * inner
    for shift in (1, 2, 3):
        moved = pltpu.roll(inner, shift, 0) * wide_masks(masks, shift, chans)
        total = total + conv_weight[3 - shift : 4 - shift, :] * moved
    conv_out[...] = total
    act = (total * jax.nn.sigmoid(total)).astype(BF16)
    act_out[...] = act
    mixed_out[...] = dot_nt(x_proj[...], act).astype(BF16)
    gate_out[...] = dot_nt(normed, in_proj[1])
    raw = turned[...]
    scale_out[...] = lax.rsqrt(jnp.mean(raw * raw, axis=0, keepdims=True) + EPSILON)
    turned[...] = jnp.broadcast_to(gain, rows.shape).T
    column = gain_out.shape[0]
    gain_out[...] = turned[pl.ds(pl.multiple_of(place[0] * column, column), column), :]


def block_columns(transposed, block):
    length = transposed.shape[1]
    return pltpu.roll(transposed, lax.rem(length - 8 * block, length), 1)


def spread_column(columns, row, tiles):
    return lane_tiles(jnp.broadcast_to(columns[:, row : row + 1], (columns.shape[0], 128)), tiles)


def scan_forward_kernel(
    place,
    piece_0,
    piece_1,
    piece_2,
    piece_3,
    dt_proj,
    dt_bias,
    decay_log,
    skip_gain,
    act_in,
    gate_in,
    masks,
    out_proj,
    normed,
    out_0,
    out_1,
    out_2,
    out_3,
    mixed_out,
    share_out,
    y_out,
    held,
    rate,
    step_rows,
    drive_rows,
    y_rows,
    partial,
):
    rank = dt_proj.shape[0]
    states = decay_log.shape[0]
    length, chans = y_out.shape
    tiles = step_rows.shape[1] // 128
    mixed = sum_pieces(place, (piece_0, piece_1, piece_2, piece_3), held)
    mixed_out[...] = mixed
    step_size = softplus(dot_tn(mixed[:rank].astype(BF16), dt_proj[...]) + as_row(dt_bias))
    act = act_in[...].astype(F32)
    reset = NEVER * (1.0 - wide_masks(masks, 0, chans))
    padded_copy(rate, -LOG2E * jnp.exp(decay_log[...]))
    padded_copy(step_rows, step_size + reset)
    padded_copy(drive_rows, step_size * act)
    b_turned = mixed[rank : rank + states]
    c_turned = mixed[rank + states : rank + 2 * states]

    def block(index, state):
        start = pl.multiple_of(index * 8, 8)
        b_cols = block_columns(b_turned, index)
        c_cols = block_columns(c_turned, index)
        steps = step_rows[pl.ds(start, 8), :]
        drives = drive_rows[pl.ds(start, 8), :]
        rows = []
        for row in range(8):
            decay = jnp.exp2(rate[...] * steps[row : row + 1])
            state = decay * state + spread_column(b_cols, row, tiles) * drives[row : row + 1]
            rows.append(
                jnp.sum(spread_column(c_cols, row, tiles) * state, axis=0, keepdims=True)
            )
        y_rows[pl.ds(start, 8), :] = jnp.concatenate(rows, axis=0)
        return state

    lax.fori_loop(0, length // 8, block, jnp.zeros((states, 128 * tiles), F32))
    y = y_rows[:, :chans] + as_row(skip_gain) * act
    y_out[...] = y
    gate = gate_in[...]
    gated = (y * (gate * jax.nn.sigmoid(gate))).astype(BF16)
    partial[...] = dot_nn(gated, out_proj[...])
    put_row_chunks(place, partial, (out_0, out_1, out_2, out_3))
    width = normed.shape[0]
    share_out[:width] = normed[...]
    padded_copy(step_rows, gated.astype(F32))
    share_out[width : width + chans] = step_rows[...].T[:chans].astype(BF16)
    padded_copy(step_rows, act)
    share_out[width + chans :] = step_rows[...].T[:chans].astype(BF16)


def dispatch_kernel(
    place,
    piece_0,
    piece_1,
    piece_2,
    piece_3,
    rows_in,
    gain,
    choose,
    residual_out,
    columns_out,
    slots,
    turned,
):
    take_row_pieces(place, (piece_0, piece_1, piece_2, piece_3), residual_out)
    residual = rows_in[...].astype(F32) + residual_out[...]
    residual_out[...] = residual
    send = (residual * rms_rate(residual) * as_row(gain)).astype(BF16)
    slots[...] = dot_nn(choose[...], send).astype(BF16)
    turned[...] = residual.T
    column = columns_out.shape[0]
    columns_out[...] = turned[pl.ds(pl.multiple_of(place[0] * column, column), column), :]


def hidden_back_kernel(grad_slots, second_w, d_hidden):
    d_hidden[...] = dot_nn(grad_slots[...], second_w[...])


def expert_kernel(arrived, first_w, d_hidden, hidden_out, d_pre_out, d_slots):
    value = dot_nn(arrived[...], first_w[...])
    square = value * value
    bend = jnp.tanh(GELU_SCALE * (value + GELU_CUBE * value * square))
    half = 0.5 * (1.0 + bend)
    slope = half + 0.5 * value * (1.0 - bend * bend) * GELU_SCALE * (
        1.0 + 3.0 * GELU_CUBE * square
    )
    d_pre = (slope * d_hidden[...]).astype(BF16)
    d_pre_out[...] = d_pre
    d_slots[...] = dot_nt(d_pre, first_w[...]).astype(BF16)
    hidden_out[...] = (value * half).astype(BF16)


def expert_grads_kernel(arrived, grad_slots, hidden, d_pre, second_w, first_out, second_out, moe):
    first_out[...] = dot_tn(arrived[...], d_pre[...]).astype(BF16)
    second_out[...] = dot_tn(grad_slots[...], hidden[...]).astype(BF16)
    moe[...] = dot_nt(hidden[...], second_w[...]).astype(BF16)


def expert_grads_pack_kernel(
    share, capacity, arrived, grad_slots, hidden, d_pre, second_w, message, grads, packed, semaphores
):
    experts = message.shape[0]
    started = []
    for which, (left, right) in enumerate(((arrived, d_pre), (grad_slots, hidden))):
        grads[which] = dot_tn(left[...], right[...]).astype(BF16)
        copies = [
            (
                grads.at[which, pl.ds(index * share, share)],
                message.at[index, pl.ds(which * share, share)],
            )
            for index in range(experts)
        ]
        started += run_copies(copies, semaphores.at[pl.ds(which * experts, experts)])
    moe = dot_nt(hidden[...], second_w[...]).astype(BF16)
    copies = []
    for index in range(experts):
        put_folded(packed.at[index], moe[index * capacity : (index + 1) * capacity])
        copies.append(
            (packed.at[index], message.at[index, pl.ds(2 * share, packed.shape[1])])
        )
    started += run_copies(copies, semaphores.at[pl.ds(2 * experts, experts)])
    for copy in started:
        copy.wait()


def owner_kernel(
    share,
    message,
    along_x,
    along_y,
    first_out,
    second_out,
    pass_y,
    pass_x,
    low,
    wide,
    passed,
    arrivals,
    semaphores,
):
    count = message.shape[0]
    arriving = run_copies(
        [(message.at[index, pl.ds(0, 2 * share)], low.at[index]) for index in range(count)],
        arrivals.at[pl.ds(2, count)],
    )
    started = pass_on(
        along_x,
        along_y,
        pass_y,
        pass_x,
        passed,
        arrivals.at[pl.ds(0, 2)],
        semaphores.at[pl.ds(0, 2)],
    )
    for index in range(count):
        arriving[index].wait()
        wide[index] = low[index].astype(F32)
        copies = [
            (wide.at[index, pl.ds(0, share)], first_out.at[index]),
            (wide.at[index, pl.ds(share, share)], second_out.at[index]),
        ]
        started += run_copies(copies, semaphores.at[pl.ds(2 + 2 * index, 2)])
    for copy in started:
        copy.wait()


def back_rows_kernel(place, choose, slots, out_0, out_1, out_2, out_3, partial):
    partial[...] = dot_tn(choose[...], slots[...])
    put_row_chunks(place, partial, (out_0, out_1, out_2, out_3))


def back_columns_kernel(place, choose, shares, slots, out_0, out_1, out_2, out_3, rows):
    rows[...] = dot_tn(slots[...], choose[...]).astype(BF16)
    outs = (out_0, out_1, out_2, out_3)
    count, top, _ = shares.shape
    column = rows.shape[0] // count
    for step, out in enumerate(outs):
        whose = lax.rem(place[0] + step, count)
        out[:top, :] = shares[whose]
        out[top:, :] = rows[pl.ds(pl.multiple_of(whose * column, column), column), :]


def back_folded_kernel(
    share,
    place,
    choose,
    shares,
    message,
    refs,
    out_0,
    out_1,
    out_2,
    out_3,
    weight_grad,
    bias_grad,
    slots,
    rows,
    staged,
    semaphores,
):
    count = message.shape[0]
    capacity = slots.shape[0] // count
    folded = message.shape[1] - 2 * share
    copies = []
    for index in range(count):
        copies += unfold_copies(
            message.at[index, pl.ds(2 * share, folded)], slots, index * capacity, capacity
        )
    deep = 2 * VECTORS_TWO
    height = staged.shape[1]
    top = refs[0].shape[0] - height
    copies += [(ref.at[pl.ds(top, height)], staged.at[index]) for index, ref in enumerate(refs)]
    for copy in run_copies(copies, semaphores):
        copy.wait()
    total = staged[0].astype(F32)
    for index in range(1, staged.shape[0]):
        total = total + staged[index].astype(F32)
    chans = weight_grad.shape[1]
    vectors = jnp.concatenate(
        [total[start : start + deep] for start in range(0, height, deep)], axis=1
    )[:, :chans]
    vectors = vectors[:VECTORS_TWO] + vectors[VECTORS_TWO:]
    weight_grad[...] = vectors[:4]
    bias_grad[...] = vectors[4].reshape(chans)
    norm_grad = jnp.concatenate([vectors[5:6], vectors[6:7]], axis=1)
    norm_rows = [norm_grad[:, start : start + 128] for start in range(0, norm_grad.shape[1], 128)]
    spare = jnp.zeros((NORM_ROWS - len(norm_rows), 128), F32)
    upper, lower = split_vectors(jnp.concatenate([*norm_rows, spare], axis=0))
    norm_low = jnp.concatenate([upper, lower], axis=0).astype(BF16)
    outs = (out_0, out_1, out_2, out_3)
    plain = out_0.shape[0] - 2 * NORM_ROWS
    back_columns_kernel(
        place, choose, shares, slots, *[out.at[pl.ds(0, plain)] for out in outs], rows
    )
    for out in outs:
        out[plain:, :] = norm_low


def mixer_grad_kernel(
    place,
    piece_0,
    piece_1,
    piece_2,
    piece_3,
    residual_in,
    gain_ref,
    cotangent,
    out_proj,
    columns_out,
    mix_out,
    d_gated,
    gain_grad,
    d_send,
    turned,
):
    take_row_pieces(place, (piece_0, piece_1, piece_2, piece_3), d_send)
    residual = residual_in[...]
    inverse = rms_rate(residual)
    scaled = residual * inverse
    grad = d_send[...]
    pulled = grad * as_row(gain_ref)
    along = jnp.mean(pulled * scaled, axis=-1, keepdims=True)
    d_residual = cotangent[...].astype(F32) + inverse * (pulled - scaled * along)
    d_mix = d_residual.astype(BF16)
    put_blocks(mix_out, d_mix)
    d_gated[...] = dot_nt(d_mix, out_proj[...])
    gain_grad[...] = jnp.sum(grad * scaled, axis=0, keepdims=True)
    turned[...] = d_residual.T
    column = columns_out.shape[0]
    columns_out[...] = turned[pl.ds(pl.multiple_of(place[0] * column, column), column), :]


def split_vectors(vectors):
    upper = vectors.astype(BF16).astype(F32)
    return upper, vectors - upper


def scan_states_kernel(
    y_in,
    gate_in,
    act_in,
    mixed_in,
    masks,
    dt_proj,
    dt_bias,
    decay_log,
    decays,
    history,
    step_rows,
    drive_rows,
    step_slope,
    y_slope,
    gate_slope,
    rate,
    decay_rows,
):
    rank = dt_proj.shape[0]
    states = decay_log.shape[0]
    length, chans = y_in.shape
    tiles = step_rows.shape[1] // 128
    full = 128 * tiles
    mixed = mixed_in[...]
    raw_step = dot_tn(mixed[:rank].astype(BF16), dt_proj[...]) + as_row(dt_bias)
    step_size = softplus(raw_step)
    step_slope[...] = jax.nn.sigmoid(raw_step)
    reset = NEVER * (1.0 - wide_masks(masks, 0, chans))
    padded_copy(rate, -LOG2E * jnp.exp(decay_log[...]))
    padded_copy(step_rows, step_size)
    padded_copy(decay_rows, step_size + reset)
    padded_copy(drive_rows, step_size * act_in[...].astype(F32))
    gate = gate_in[...]
    gate_sig = jax.nn.sigmoid(gate)
    y_slope[...] = gate * gate_sig
    gate_slope[...] = y_in[...] * gate_sig * (1.0 + gate * (1.0 - gate_sig))
    b_turned = mixed[rank : rank + states]
    history[pl.ds(0, states), :] = jnp.zeros((states, full), F32)

    def forward_block(index, state):
        start = pl.multiple_of(index * 8, 8)
        b_cols = block_columns(b_turned, index)
        steps = decay_rows[pl.ds(start, 8), :]
        drives = drive_rows[pl.ds(start, 8), :]
        for row in range(8):
            decay = jnp.exp2(rate[...] * steps[row : row + 1])
            state = decay * state + spread_column(b_cols, row, tiles) * drives[row : row + 1]
            at = pl.multiple_of((start + row) * states, states)
            decays[pl.ds(at, states), :] = decay
            history[pl.ds(at + states, states), :] = state
        return state

    lax.fori_loop(0, length // 8, forward_block, jnp.zeros((states, full), F32))


def scan_backward_kernel(
    d_gated,
    y_slope,
    gate_slope,
    act_in,
    mixed_in,
    dt_proj,
    decay_log,
    skip_gain,
    gain_grad,
    d_mix,
    decays,
    history,
    step_rows,
    drive_rows,
    step_slope,
    d_mixed_out,
    d_act_out,
    d_gate_out,
    share_out,
    rate,
    dy_rows,
    du_rows,
    dl_rows,
):
    rank = dt_proj.shape[0]
    states = decay_log.shape[0]
    length, chans = y_slope.shape
    tiles = step_rows.shape[1] // 128
    full = 128 * tiles
    mixed = mixed_in[...]
    dt_low = mixed[:rank].astype(BF16)
    act = act_in[...].astype(F32)
    padded_copy(rate, -jnp.exp(decay_log[...]))
    d_out = d_gated[...]
    d_y = d_out * y_slope[...]
    padded_copy(dy_rows, d_y)
    d_gate = d_out * gate_slope[...]
    b_turned = mixed[rank : rank + states]
    c_turned = mixed[rank + states : rank + 2 * states]
    lanes = lax.broadcasted_iota(jnp.int32, (states, length), 1)

    def backward_block(count, carry):
        carried, d_rate, d_b, d_c = carry
        index = length // 8 - 1 - count
        start = pl.multiple_of(index * 8, 8)
        b_cols = block_columns(b_turned, index)
        c_cols = block_columns(c_turned, index)
        steps = step_rows[pl.ds(start, 8), :]
        drives = drive_rows[pl.ds(start, 8), :]
        dys = dy_rows[pl.ds(start, 8), :]
        du = [None] * 8
        dl = [None] * 8
        for row in reversed(range(8)):
            at = pl.multiple_of((start + row) * states, states)
            before = history[pl.ds(at, states), :]
            after = history[pl.ds(at + states, states), :]
            decay = decays[pl.ds(at, states), :]
            here = lanes == start + row
            dy_row = jnp.broadcast_to(dys[row : row + 1], (states, full))
            grad = spread_column(c_cols, row, tiles) * dy_row + carried
            c_part = jnp.sum(fold_tiles(dy_row * after), axis=1, keepdims=True)
            d_c = jnp.where(here, c_part, d_c)
            b_part = jnp.sum(fold_tiles(grad * drives[row : row + 1]), axis=1, keepdims=True)
            d_b = jnp.where(here, b_part, d_b)
            du[row] = jnp.sum(grad * spread_column(b_cols, row, tiles), axis=0, keepdims=True)
            carried = grad * decay
            d_log = carried * before
            dl[row] = jnp.sum(d_log * rate[...], axis=0, keepdims=True)
            d_rate = d_rate + d_log * steps[row : row + 1]
        du_rows[pl.ds(start, 8), :] = jnp.concatenate(du, axis=0)
        dl_rows[pl.ds(start, 8), :] = jnp.concatenate(dl, axis=0)
        return carried, d_rate, d_b, d_c

    nothing = jnp.zeros((states, full), F32)
    thin = jnp.zeros((states, length), F32)
    _, d_rate, d_b, d_c = lax.fori_loop(
        0, length // 8, backward_block, (nothing, nothing, thin, thin)
    )
    du = du_rows[:, :chans]
    d_step = (dl_rows[:, :chans] + du * act) * step_slope[...]
    d_step_low = d_step.astype(BF16)
    low_turned = dot_nt(dt_proj[...], d_step_low)
    d_mixed_out[...] = jnp.concatenate([low_turned, d_b, d_c], axis=0).astype(BF16)
    d_act_out[...] = du * step_rows[:, :chans] + as_row(skip_gain) * d_y
    d_gate_low = d_gate.astype(BF16)
    d_gate_out[...] = d_gate_low
    width = d_mix.shape[0]
    share_out[:width] = d_mix[...]
    padded_copy(du_rows, d_gate_low.astype(F32))
    share_out[width : width + chans] = du_rows[...].T[:chans].astype(BF16)
    gain_rows = gain_grad[...]
    upper, lower = split_vectors(
        jnp.concatenate(
            [
                (d_rate * rate[...])[:, :chans],
                jnp.sum(d_step, axis=0, keepdims=True),
                jnp.sum(d_y * act, axis=0, keepdims=True),
                gain_rows[:, :chans],
                gain_rows[:, chans:],
                jnp.zeros((VECTORS_ONE - states - 4, chans), F32),
            ],
            axis=0,
        )
    )
    dl_rows[...] = jnp.zeros(dl_rows.shape, F32)
    dl_rows[:rank, :chans] = dot_nn(dt_low, d_step_low)
    dl_rows[rank : rank + VECTORS_ONE, :chans] = upper
    dl_rows[rank + VECTORS_ONE : rank + 2 * VECTORS_ONE, :chans] = lower
    share_out[width + chans :] = dl_rows[...].T[:chans].astype(BF16)


def leave_kernel(
    place,
    piece_0,
    piece_1,
    piece_2,
    piece_3,
    d_act_scan,
    d_gate,
    conv_in,
    inner_in,
    masks,
    x_proj,
    conv_weight,
    in_proj,
    rows_in,
    gain,
    shares,
    message,
    held,
    turned,
    padded,
):
    length, chans = inner_in.shape
    width = rows_in.shape[1]
    full = padded.shape[1]
    d_mixed = sum_pieces(place, (piece_0, piece_1, piece_2, piece_3), held).astype(BF16)
    d_act = d_act_scan[...] + dot_tn(d_mixed, x_proj[...])
    conv = conv_in[...]
    sig = jax.nn.sigmoid(conv)
    d_conv = d_act * sig * (1.0 + conv * (1.0 - sig))
    inner = inner_in[...]
    d_inner = conv_weight[3:4, :] * d_conv
    weight_grads = [jnp.sum(d_conv * inner, axis=0, keepdims=True)]
    for shift in (1, 2, 3):
        masked = d_conv * wide_masks(masks, shift, chans)
        weight_grads.append(
            jnp.sum(masked * pltpu.roll(inner, shift, 0), axis=0, keepdims=True)
        )
        d_inner = d_inner + conv_weight[3 - shift : 4 - shift, :] * pltpu.roll(
            masked, length - shift, 0
        )
    d_inner_low = d_inner.astype(BF16)
    padded_copy(padded, d_inner_low.astype(F32))
    message[:chans] = padded[...].T[:chans].astype(BF16)
    proj = d_mixed.shape[0]
    top = message.shape[0] - full // 128 * 2 * VECTORS_TWO
    message[chans:top] = jnp.concatenate(
        [d_mixed.astype(F32), jnp.zeros((top - chans - proj, length), F32)], axis=0
    ).astype(BF16)
    d_normed = dot_nn(d_inner_low, in_proj[0]) + dot_nn(d_gate[...], in_proj[1])
    rows = rows_in[...].astype(F32)
    scaled = rows * rms_rate(rows)
    norm_grad = jnp.sum(d_normed * scaled, axis=0, keepdims=True)
    upper, lower = split_vectors(
        jnp.concatenate(
            [
                weight_grads[3],
                weight_grads[2],
                weight_grads[1],
                weight_grads[0],
                jnp.sum(d_conv, axis=0, keepdims=True),
                norm_grad[:, :chans],
                norm_grad[:, chans:],
                jnp.zeros((VECTORS_TWO - 7, chans), F32),
            ],
            axis=0,
        )
    )
    padded_copy(padded, jnp.zeros((length, chans), F32))
    padded[:VECTORS_TWO, :chans] = upper
    padded[VECTORS_TWO : 2 * VECTORS_TWO, :chans] = lower
    for tile in range(full // 128):
        message[top + tile * 2 * VECTORS_TWO : top + (tile + 1) * 2 * VECTORS_TWO] = padded[
            : 2 * VECTORS_TWO, tile * 128 : (tile + 1) * 128
        ].astype(BF16)
    along = jnp.mean(d_normed * as_row(gain) * scaled, axis=-1, keepdims=True)
    along = jnp.broadcast_to(along, (length, length)).T[:8]
    high = along.astype(BF16)
    low = (along - high.astype(F32)).astype(BF16)
    turned[...] = d_normed.T
    count, rows, _ = shares.shape
    column = width // count
    ends = jnp.concatenate([high, low], axis=0)
    for index in range(count):
        shares[index, :column, :] = turned[index * column : (index + 1) * column].astype(BF16)
        shares[index, column:, :] = ends


def finish_rows_kernel(
    piece_0,
    piece_1,
    piece_2,
    piece_3,
    residual,
    d_columns,
    tokens,
    scale,
    gain,
    outcome,
    grad_tokens,
    *norm_out,
):
    column = tokens.shape[0]
    total = piece_0[...].astype(F32)
    for piece in (piece_1, piece_2, piece_3):
        total = total + piece[...].astype(F32)
    along = total[column : column + 1] + total[column + 8 : column + 9]
    inverse = scale[...]
    pulled = total[:column] * gain[...]
    scaled = tokens[...].astype(F32) * inverse
    grad_tokens[...] = d_columns[...] + inverse * (pulled - scaled * along)
    plain = 2 * column + 16
    outcome[...] = (residual[...] + total[column + 16 : plain]).astype(BF16)
    for out in norm_out:
        norm = total[plain : plain + NORM_ROWS] + total[plain + NORM_ROWS :]
        width = out.shape[0]
        out[...] = jnp.concatenate(
            [norm[row : row + 1] for row in range(width // 128)], axis=1
        ).reshape(width)


def take_blocks(target, pieces):
    for index, piece in enumerate(pieces):
        for start in range(0, target.shape[1], 128):
            target[index * 128 : (index + 1) * 128, start : start + 128] = piece[
                start : start + 128
            ]


def take_turned(target, pieces, start):
    rows = target.shape[0]
    for index, piece in enumerate(pieces):
        target[:, index * 128 : (index + 1) * 128] = piece[start : start + rows]


def stage_pieces(refs, staged, semaphores, rows=None):
    copies = []
    parts = len(refs) // 2
    for index, ref in enumerate(refs):
        side, part = divmod(index, parts)
        target = staged.at[4 * side + min(part, 3)]
        if part >= 3 and parts > 4:
            height = staged.shape[1] // (parts - 3)
            target = target.at[pl.ds((part - 3) * height, height)]
        copies.append((ref if rows is None else ref.at[pl.ds(*rows)], target))
    return run_copies(copies, semaphores), [staged.at[index] for index in range(8)]


def first_sets_kernel(refs, normed, gated, acts, staged, semaphores):
    chans = gated.shape[0]
    width = normed.shape[1]
    arriving, firsts = stage_pieces(refs, staged, semaphores)
    for copy in arriving:
        copy.wait()
    take_blocks(normed, firsts)
    take_turned(gated, firsts, width)
    take_turned(acts, firsts, width + chans)


def wide_grads_kernel(
    sizes,
    second_refs,
    last_refs,
    normed,
    gated,
    acts,
    out_grad,
    in_grad,
    x_grad,
    dt_grad,
    bias_grad,
    decay_grad,
    skip_grad,
    norm_grad,
    staged,
    staged_last,
    mixed,
    d_gate,
    d_mixed,
    total,
    wide_grad,
    second_arrivals,
    last_arrivals,
    semaphores,
):
    rank, states, proj = sizes
    chans, width = out_grad.shape
    arriving_last, lasts = stage_pieces(last_refs, staged_last, last_arrivals)
    arriving, seconds = stage_pieces(second_refs, staged, second_arrivals)
    for copy in arriving_last:
        copy.wait()
    take_turned(d_gate, lasts, 0)
    wide_grad[0] = dot_nn(d_gate[...], normed[...])
    started = run_copies([(wide_grad.at[0], in_grad.at[0])], semaphores)
    for copy in arriving:
        copy.wait()
    take_turned(d_gate, seconds, width)
    wide_grad[1] = dot_nn(d_gate[...], normed[...])
    started += run_copies([(wide_grad.at[1], in_grad.at[1])], semaphores.at[pl.ds(1, 1)])
    take_blocks(mixed, seconds)
    half = chans // 2
    for index in range(2):
        rows = pl.ds(index * half, half)
        wide_grad[2, rows] = dot_nn(gated[rows], mixed[...])
        started += run_copies(
            [(wide_grad.at[2, rows], out_grad.at[rows])], semaphores.at[pl.ds(2 + index, 1)]
        )
    take_turned(d_mixed, lasts, chans)
    x_grad[...] = dot_nt(d_mixed[...], acts[...])[:proj]
    vectors = seconds[0][width + chans :].astype(F32)
    for piece in seconds[1:]:
        vectors = vectors + piece[width + chans :].astype(F32)
    total[...] = jnp.zeros(total.shape, F32)
    total[:chans] = vectors
    rows = total[...].T[:, :chans]
    dt_grad[...] = rows[:rank]
    rows = rows[rank : rank + VECTORS_ONE] + rows[rank + VECTORS_ONE : rank + 2 * VECTORS_ONE]
    decay_grad[...] = rows[:states]
    bias_grad[...] = rows[states].reshape(chans)
    skip_grad[...] = rows[states + 1].reshape(chans)
    norm_grad[...] = jnp.concatenate(
        [rows[states + 2 : states + 3], rows[states + 3 : states + 4]], axis=1
    ).reshape(width)
    for copy in started:
        copy.wait()


def send_chunks(chunks):
    count = len(chunks)
    pairs = [[(i, (i + s) % count) for i in range(count)] for s in range(count)]
    return [chunks[0]] + [lax.ppermute(chunks[s], "tensor", pairs[s]) for s in range(1, count)]


def share_rows(values, count):
    return send_chunks([values] * count)


def add_low(pieces):
    total = pieces[0].astype(F32)
    for piece in pieces[1:]:
        total = total + piece.astype(F32)
    return total.astype(BF16)


def after(values, *events):
    return list(lax.optimization_barrier((tuple(values), events))[0])


def swap(values, bits):
    return lax.ppermute(values, "dp", [(i, i ^ bits) for i in range(NEAR_GROUPS)])


def swap_across(halves):
    return [swap(halves[0], 2), swap(halves[1], 4)]


def swap_near(values):
    return [*values, *[swap(part, 1) for part in values]]


def body(
    tokens,
    resets,
    routes,
    norm_one,
    in_proj,
    conv_weight,
    conv_bias,
    x_proj,
    dt_proj,
    dt_bias,
    decay_log,
    skip_gain,
    out_proj,
    norm_two,
    expert_in,
    expert_out,
    cotangent,
):
    groups = lax.axis_size("dp")
    parts = lax.axis_size("tensor")
    place = lax.axis_index("tensor").astype(jnp.int32).reshape(1)
    length, column = tokens.shape
    width = norm_one.shape[0]
    rank, chans = dt_proj.shape
    states = decay_log.shape[0]
    experts, share, hidden_units = expert_in.shape
    proj = x_proj.shape[1]
    tile_count = groups // experts
    block_rows = length * experts // groups
    capacity = max(2, block_rows // 4)
    slot_count = groups * capacity
    tiles = -(-chans // 128)
    full = 128 * tiles
    near = groups == NEAR_GROUPS and experts == groups
    tokens_turned = tokens.T
    in_turned = jnp.swapaxes(in_proj, 1, 2)
    x_turned = x_proj.T
    resets_row = resets.reshape(1, length)
    routes_row = routes.reshape(1, length)

    def exchange(values):
        return lax.all_to_all(values, "dp", split_axis=0, concat_axis=0, tiled=True)

    def exchange_slots(slots):
        return exchange(slots.reshape(groups, capacity, width)).reshape(slot_count, width)

    token_pieces = share_rows(tokens_turned, parts)
    mask_out = ((4, length, 128), F32)
    choose_out = ((slot_count, length), BF16)
    weight_outs = [((width, hidden_units), BF16)] * 2
    slots_out = ((slot_count, width), BF16)
    hidden_out = ((slot_count, hidden_units), BF16)
    folded = capacity + capacity // 2
    message_out = ((groups, 2 * share + folded, hidden_units), BF16)
    if near:
        masks, choose, packed = run_kernel(
            functools.partial(pack_kernel, capacity),
            [mask_out, choose_out, message_out],
            [resets_row, routes_row, cotangent, expert_in, expert_out],
            [
                ((groups, folded, hidden_units), BF16),
                ((experts, 2, share, hidden_units), BF16),
                pltpu.SemaphoreType.DMA((2 * experts,)),
                pltpu.SemaphoreType.DMA((3 * experts,)),
            ],
            far_args=(3, 4),
            far_outs=(2,), staged=(0, 1, 2))
        weights = exchange(packed)
    else:
        masks, choose, grad_send = run_kernel(
            functools.partial(prepare_kernel, experts, capacity, block_rows),
            [mask_out, choose_out, slots_out],
            [resets_row, routes_row, cotangent], loose_outs=(2,))
        first_w = exchange(jnp.tile(expert_in, (tile_count, 1, 1))).reshape(weight_outs[0][0])
        second_w = exchange(jnp.tile(expert_out, (tile_count, 1, 1))).reshape(weight_outs[0][0])
        grad_slots = exchange_slots(grad_send)
        (d_hidden,) = run_kernel(
            hidden_back_kernel, [((slot_count, hidden_units), F32)], [grad_slots, second_w]
        )

    rows, normed, act, inner, conv, gate, scale, gain_columns, mixed_part = run_kernel(
        enter_kernel,
        [
            ((length, width), BF16),
            ((width, length), BF16),
            ((length, chans), BF16),
            ((length, chans), F32),
            ((length, chans), F32),
            ((length, chans), F32),
            ((1, length), F32),
            ((column, length), F32),
            ((proj, length), BF16),
        ],
        [place, *token_pieces, norm_one, in_turned, conv_weight, conv_bias, x_turned, masks],
        [((width, length), F32)],
        scalars=1, loose_outs=(8,), staged=(1, 2, 3, 4, 10))
    mixed_pieces = share_rows(mixed_part, parts)
    *mix_chunks, mixed, first, y = run_kernel(
        scan_forward_kernel,
        [((length // parts, width), BF16)] * parts
        + [
            ((proj, length), F32),
            ((width + 2 * chans, length), BF16),
            ((length, chans), F32),
        ],
        [
            place,
            *mixed_pieces,
            dt_proj,
            dt_bias,
            decay_log,
            skip_gain,
            act,
            gate,
            masks,
            out_proj,
            normed,
        ],
        [
            ((parts, proj, length), BF16),
            ((states, full), F32),
            ((length, full), F32),
            ((length, full), F32),
            ((length, full), F32),
            ((length, width), F32),
        ],
        scalars=1, loose_outs=(0, 1, 2, 3, 5), staged=(1, 2, 3, 4, 9, 10, 11, 13))
    mixer_pieces = share_rows(add_low(send_chunks(mix_chunks)), parts)
    if near:
        first_x, first_y = swap(first, 2), swap(first, 4)
    residual, residual_columns, send_slots = run_kernel(
        dispatch_kernel,
        [((length, width), F32), ((column, length), F32), slots_out],
        [place, *mixer_pieces, rows, norm_two, choose],
        [((width, length), F32)],
        scalars=1, loose_outs=(2,), staged=(1, 2, 3, 4, 5, 7))
    if near:
        half_out = (((width + 2 * chans) // 2, length), BF16)
        first_w, second_w, grad_slots, *halves, d_hidden = run_kernel(
            functools.partial(unpack_kernel, share, capacity),
            weight_outs
            + [slots_out, half_out, half_out, ((slot_count, hidden_units), F32)],
            [*after([weights], send_slots), first_x, first_y],
            [
                *weight_outs,
                slots_out,
                ((2, *half_out[0]), BF16),
                pltpu.SemaphoreType.DMA((4,)),
                pltpu.SemaphoreType.DMA((5 * groups,)),
            ],
            far_args=(0, 1, 2),
            far_outs=(0, 1, 2, 3, 4),
        )
        first_d = swap_across(halves)
    arrived = exchange_slots(send_slots)
    hidden, d_pre, d_slots = run_kernel(
        expert_kernel, [hidden_out, hidden_out, slots_out], [arrived, first_w, d_hidden], loose_outs=(2,), staged=(0, 1, 2))
    if near:
        d_slots = after([d_slots], first_d)[0]
    back_slots = exchange_slots(d_slots)
    grad_args = [arrived, grad_slots, hidden, d_pre, second_w]
    grad_out = ((experts, share, hidden_units), F32)
    if near:
        (packed,) = run_kernel(
            functools.partial(expert_grads_pack_kernel, share, capacity),
            [message_out],
            grad_args,
            [
                ((2, width, hidden_units), BF16),
                ((groups, folded, hidden_units), BF16),
                pltpu.SemaphoreType.DMA((3 * groups,)),
            ],
            far_outs=(0,), staged=range(5))
        back_slots = after([back_slots], packed)[0]
        packed = after([packed], back_slots)[0]
        owned = exchange(packed)
    else:
        grad_first, grad_second, moe_slots = run_kernel(
            expert_grads_kernel, weight_outs + [slots_out], grad_args, loose_outs=(0, 1, 2))
    back_chunks = run_kernel(
        back_rows_kernel,
        [((length // parts, width), BF16)] * parts,
        [place, choose, back_slots],
        [((length, width), F32)],
        scalars=1, loose_outs=(0, 1, 2, 3), staged=(1, 2))
    send_pieces = share_rows(add_low(send_chunks(back_chunks)), parts)
    if near:
        firsts = swap_near([first, first_x, first_y, *first_d])

        send_pieces = after(send_pieces, firsts)
    decays, history, step_rows, drive_rows, step_slope, y_slope, gate_slope = run_kernel(
        scan_states_kernel,
        [
            ((length * states, full), F32),
            (((length + 1) * states, full), F32),
            ((length, full), F32),
            ((length, full), F32),
            ((length, chans), F32),
            ((length, chans), F32),
            ((length, chans), F32),
        ],
        [y, gate, act, *after([mixed], back_chunks[0]), masks, dt_proj, dt_bias, decay_log],
        [((states, full), F32), ((length, full), F32)],
        staged=range(5),
        held_outs=range(7),
    )
    send_pieces = after(send_pieces, decays)
    d_columns, d_mix, d_gated, gain_grad_two = run_kernel(
        mixer_grad_kernel,
        [
            ((column, length), F32),
            ((width, length), BF16),
            ((length, chans), F32),
            ((1, width), F32),
        ],
        [place, *send_pieces, residual, norm_two, cotangent, out_proj],
        [((length, width), F32), ((width, length), F32)],
        scalars=1, staged=(1, 2, 3, 4, 5, 7, 8), held_outs=(1, 2, 3))
    d_mixed_part, d_act_scan, d_gate, second = run_kernel(
        scan_backward_kernel,
        [
            ((proj, length), BF16),
            ((length, chans), F32),
            ((length, chans), BF16),
            ((width + 2 * chans, length), BF16),
        ],
        [
            d_gated,
            y_slope,
            gate_slope,
            act,
            mixed,
            dt_proj,
            decay_log,
            skip_gain,
            gain_grad_two,
            d_mix,
            decays,
            history,
            step_rows,
            drive_rows,
            step_slope,
        ],
        [
            ((states, full), F32),
            ((length, full), F32),
            ((length, full), F32),
            ((length, full), F32),
        ],
        staged=(3, 4),
        loose_outs=(0, 3),
        held_outs=(1, 2),
    )
    d_mixed_pieces = share_rows(d_mixed_part, parts)
    if near:
        second_x, second_y = swap(second, 2), swap(second, 4)
    last_rows = chans + -(-proj // 16) * 16 + tiles * 2 * VECTORS_TWO
    normed_shares, message = run_kernel(
        leave_kernel,
        [((parts, column + 16, length), BF16), ((last_rows, length), BF16)],
        [
            place,
            *d_mixed_pieces,
            d_act_scan,
            d_gate,
            conv,
            inner,
            masks,
            x_turned,
            conv_weight,
            in_turned,
            rows,
            norm_one,
        ],
        [((parts, proj, length), BF16), ((width, length), F32), ((length, full), F32)],
        scalars=1, loose_outs=(1,), staged=(1, 2, 3, 4, 7, 8, 9, 13))
    share_outs = [((2 * column + 16, length), BF16)] * parts
    if near:
        lasts = [message, swap(message, 2), swap(message, 4), swap(message, 6)]
        def first_sets(*refs):
            first_sets_kernel(refs[:10], *refs[10:])

        all_normed, all_gated, all_act = run_kernel(
            first_sets,
            [
                ((groups * length, width), BF16),
                ((chans, groups * length), BF16),
                ((chans, groups * length), BF16),
            ],
            after(firsts, message, owned),
            [((groups, width + 2 * chans, length), BF16), pltpu.SemaphoreType.DMA((10,))],
            far_args=range(10),
            held_outs=(0, 1, 2),
        )
        second_x, second_y = after([second_x, second_y], all_normed)
        grad_expert_in, grad_expert_out, *halves = run_kernel(
            functools.partial(owner_kernel, share),
            [grad_out, grad_out, half_out, half_out],
            [owned, second_x, second_y],
            [
                ((groups, 2 * share, hidden_units), BF16),
                ((groups, 2 * share, hidden_units), F32),
                ((2, *half_out[0]), BF16),
                pltpu.SemaphoreType.DMA((2 + groups,)),
                pltpu.SemaphoreType.DMA((2 + 2 * groups,)),
            ],
            far_args=(0, 1, 2),
            far_outs=(0, 1, 2, 3),
        )
        second_d = swap_across(halves)
        lasts = swap_near(after(lasts, halves))

        def back_folded(*refs):
            back_folded_kernel(share, *refs[:4], refs[4 : 4 + groups], *refs[4 + groups :])

        *shares, grad_conv_weight, grad_conv_bias = run_kernel(
            back_folded,
            [((2 * column + 16 + 2 * NORM_ROWS, length), BF16)] * parts
            + [((4, chans), F32), ((chans,), F32)],
            [place, choose, normed_shares, owned, *lasts],
            [
                slots_out,
                ((width, length), BF16),
                ((groups, tiles * 2 * VECTORS_TWO, length), BF16),
                pltpu.SemaphoreType.DMA((4 * groups,)),
            ],
            scalars=1,
            staged=(1, 2),
            far_args=range(3, 4 + groups),
            loose_outs=range(parts + 2),
        )
        norm_out = [((width,), F32)]
    else:
        shares = run_kernel(
            back_columns_kernel,
            share_outs,
            [place, choose, normed_shares, exchange_slots(moe_slots)],
            [((width, length), BF16)],
            scalars=1,
            loose_outs=(0, 1, 2, 3),
        )

        norm_out = []

        def owner_sum(values):
            got = exchange(values.reshape(groups, share, hidden_units)).astype(F32)
            return jnp.sum(got.reshape(tile_count, experts, share, hidden_units), axis=0)

        grad_expert_in = owner_sum(grad_first)
        grad_expert_out = owner_sum(grad_second)
    pieces = send_chunks(shares)
    if near:
        seconds = [second, second_x, second_y, *second_d]
        seconds = swap_near(after(seconds, grad_conv_weight))

        def wide_grads(*refs):
            wide_grads_kernel(
                (rank, states, proj), refs[:10], refs[10 : 10 + groups], *refs[10 + groups :]
            )

        (
            grad_out_proj,
            grad_in_turned,
            grad_x_turned,
            grad_dt_proj,
            grad_dt_bias,
            grad_decay_log,
            grad_skip_gain,
            grad_norm_two,
        ) = run_kernel(
            wide_grads,
            [
                ((chans, width), F32),
                ((2, chans, width), F32),
                ((proj, chans), F32),
                ((rank, chans), F32),
                ((chans,), F32),
                ((states, chans), F32),
                ((chans,), F32),
                ((width,), F32),
            ],
            [*seconds, *lasts, all_normed, all_gated, all_act],
            [
                ((groups, width + 2 * chans, length), BF16),
                ((groups, last_rows, length), BF16),
                ((groups * length, width), BF16),
                ((chans, groups * length), BF16),
                ((-(-proj // 16) * 16, groups * length), BF16),
                ((full, length), F32),
                ((3, chans, width), F32),
                pltpu.SemaphoreType.DMA((10,)),
                pltpu.SemaphoreType.DMA((groups,)),
                pltpu.SemaphoreType.DMA((4,)),
            ],
            far_args=range(10 + groups),
            far_outs=(0, 1),
            loose_outs=range(8),
        )
        pieces = after(pieces, grad_out_proj)
    else:
        top = last_rows - tiles * 2 * VECTORS_TWO
        ones = second[width + chans :].astype(F32).T
        twos = message[top:].astype(F32).reshape(tiles, 2 * VECTORS_TWO, length)
        twos = jnp.swapaxes(twos, 0, 1).reshape(2 * VECTORS_TWO, full)[:, :chans]
        plain_normed = jnp.swapaxes(normed.reshape(-1, length, 128), 0, 1).reshape(length, width)
        plain_mix = jnp.swapaxes(d_mix.reshape(-1, length, 128), 0, 1).reshape(length, width)
        grad_in_turned, grad_x_turned, grad_dt_proj, grad_out_proj, ones, twos = lax.psum(
            (
                jnp.stack(
                    [
                        dot_nn(message[:chans], plain_normed),
                        dot_nn(second[width : width + chans], plain_normed),
                    ]
                ),
                dot_nn(message[chans : chans + proj], act),
                ones[:rank],
                dot_nn(first[width : width + chans], plain_mix),
                ones[rank : rank + VECTORS_ONE]
                + ones[rank + VECTORS_ONE : rank + 2 * VECTORS_ONE],
                twos[:VECTORS_TWO] + twos[VECTORS_TWO:],
            ),
            "dp",
        )
        grad_decay_log = ones[:states]
        grad_dt_bias = ones[states]
        grad_skip_gain = ones[states + 1]
        grad_norm_two = ones[states + 2 : states + 4]
        grad_conv_weight = twos[:4]
        grad_conv_bias = twos[4]
        grad_norm_one = sum(share_rows(twos[5:7].reshape(1, width), parts)).reshape(width)
    outcome, grad_tokens, *norm_one_grad = run_kernel(
        finish_rows_kernel,
        [((column, length), BF16), ((column, length), F32)] + norm_out,
        [*pieces, residual_columns, d_columns, tokens_turned, scale, gain_columns],
        staged=range(9),
        loose_outs=(0, 1, 2),
    )
    if near:
        (grad_norm_one,) = norm_one_grad
    return (
        outcome.T,
        grad_tokens.T,
        grad_norm_one,
        jnp.swapaxes(grad_in_turned, 1, 2),
        grad_conv_weight,
        grad_conv_bias,
        grad_x_turned.T,
        grad_dt_proj,
        grad_dt_bias,
        grad_decay_log,
        grad_skip_gain,
        grad_out_proj,
        grad_norm_two.reshape(width),
        grad_expert_in,
        grad_expert_out,
    )


def solution(mesh):
    placed = (
        P("dp", "tensor"),
        P("dp"),
        P("dp", None),
        P(),
        P(None, None, "tensor"),
        P(None, "tensor"),
        P("tensor"),
        P("tensor", None),
        P(None, "tensor"),
        P("tensor"),
        P(None, "tensor"),
        P("tensor"),
        P("tensor", None),
        P(),
        P(None, "dp", "tensor"),
        P(None, "dp", "tensor"),
        P("dp", None),
    )
    return jax.shard_map(
        body,
        mesh=mesh,
        in_specs=placed,
        out_specs=(
            P("dp", "tensor"),
            P("dp", "tensor"),
            P(),
            P(None, None, "tensor"),
            P(None, "tensor"),
            P("tensor"),
            P("tensor", None),
            P(None, "tensor"),
            P("tensor"),
            P(None, "tensor"),
            P("tensor"),
            P("tensor", None),
            P(),
            P(None, "dp", "tensor"),
            P(None, "dp", "tensor"),
        ),
        check_vma=False,
    )
```

```python
import functools
import math

import jax
import jax.numpy as jnp
from jax import lax
from jax.experimental import pallas as pl
from jax.experimental.pallas import tpu as pltpu
from jax.sharding import PartitionSpec as P

EPSILON = 1e-05
F32 = jnp.float32
BF16 = jnp.bfloat16
NEVER = 1e4
LOG2E = 1.4426950408889634
GELU_SCALE = math.sqrt(2.0 / math.pi)
GELU_CUBE = 0.044715
VMEM_SPARE = 6 * 1024 * 1024
NEAR_GROUPS = 8
VECTORS_ONE = 24
VECTORS_TWO = 8
NORM_ROWS = 16


def run_kernel(
    kernel,
    outs,
    args,
    scratch=(),
    scalars=0,
    far_args=(),
    staged=(),
    far_outs=(),
    loose_outs=(),
    held_outs=(),
    alias=None,
):
    staged = tuple(staged)
    outside = {*far_args, *staged}

    def spec(index, far):
        return pl.BlockSpec(memory_space=pltpu.HBM if index in far else pltpu.VMEM)

    def held(index, shape, dtype):
        if index in loose_outs:
            return jax.ShapeDtypeStruct(shape, dtype)
        return (pltpu.VMEM if index in held_outs else pltpu.HBM)(shape, dtype)

    def body(*refs):
        refs = list(refs)
        if staged:
            *refs, semaphores = refs
            places = refs[len(refs) - len(staged) :]
            refs = refs[: len(refs) - len(staged)]
            copies = run_copies(list(zip([refs[index] for index in staged], places)), semaphores)
            for index, place in zip(staged, places):
                refs[index] = place
            for copy in copies:
                copy.wait()
        kernel(*refs)

    sizes = [(arg.shape, arg.dtype) for index, arg in enumerate(args) if index not in far_args]
    sizes += [out for index, out in enumerate(outs) if index not in far_outs]
    sizes += [shape for shape in scratch if isinstance(shape, tuple)]
    scratch = [pltpu.VMEM(*shape) if isinstance(shape, tuple) else shape for shape in scratch]
    if staged:
        scratch += [pltpu.VMEM(args[index].shape, args[index].dtype) for index in staged]
        scratch += [pltpu.SemaphoreType.DMA((len(staged),))]
    needed = sum(math.prod(shape) * jnp.dtype(dtype).itemsize for shape, dtype in sizes)
    return pl.pallas_call(
        body,
        out_shape=[held(index, shape, dtype) for index, (shape, dtype) in enumerate(outs)],
        in_specs=[
            pl.BlockSpec(memory_space=pltpu.SMEM) if index < scalars else spec(index, outside)
            for index in range(len(args))
        ],
        out_specs=[spec(index, far_outs) for index in range(len(outs))],
        scratch_shapes=scratch,
        input_output_aliases=alias or {},
        compiler_params=pltpu.CompilerParams(vmem_limit_bytes=VMEM_SPARE + needed * 5 // 4),
    )(
        *[
            pltpu.with_memory_space_constraint(arg, pltpu.HBM) if index in outside else arg
            for index, arg in enumerate(args)
        ]
    )


def dot_nn(left, right):
    return lax.dot_general(left, right, (((1,), (0,)), ((), ())), preferred_element_type=F32)


def dot_nt(left, right):
    return lax.dot_general(left, right, (((1,), (1,)), ((), ())), preferred_element_type=F32)


def dot_tn(left, right):
    return lax.dot_general(left, right, (((0,), (0,)), ((), ())), preferred_element_type=F32)


def lane_tiles(column, tiles):
    return jnp.concatenate([column] * tiles, axis=1)


def fold_tiles(values):
    total = values[:, :128]
    for tile in range(1, values.shape[1] // 128):
        total = total + values[:, 128 * tile : 128 * (tile + 1)]
    return total


def wide_masks(masks, index, chans):
    return lane_tiles(masks[index], -(-chans // 128))[:, :chans]


def rms_rate(values):
    return lax.rsqrt(jnp.mean(values * values, axis=-1, keepdims=True) + EPSILON)


def as_row(ref):
    return ref[...].reshape(1, ref.shape[0])


def softplus(values):
    return jnp.maximum(values, 0.0) + jnp.log1p(jnp.exp(-jnp.abs(values)))


def padded_copy(target, values):
    target[...] = jnp.zeros(target.shape, target.dtype)
    target[:, : values.shape[1]] = values


def put_row_chunks(place, source, outs):
    count = len(outs)
    rows = source.shape[0] // count
    for step, out in enumerate(outs):
        start = pl.multiple_of(lax.rem(place[0] + step, count) * rows, rows)
        out[pl.ds(0, rows), :] = source[pl.ds(start, rows), :].astype(out.dtype)


def take_row_pieces(place, pieces, target):
    count = len(pieces)
    rows = target.shape[0] // count
    for step, piece in enumerate(pieces):
        start = pl.multiple_of(lax.rem(place[0] - step + count, count) * rows, rows)
        target[pl.ds(start, rows), :] = piece[...].astype(target.dtype)


def sum_pieces(place, pieces, held):
    count = len(pieces)
    for step, piece in enumerate(pieces):
        held[lax.rem(place[0] - step + count, count)] = piece[...]
    total = held[0].astype(F32)
    for index in range(1, count):
        total = total + held[index].astype(F32)
    return total


def run_copies(copies, semaphores):
    started = []
    for index, (source, target) in enumerate(copies):
        copy = pltpu.make_async_copy(source, target, semaphores.at[index])
        copy.start()
        started.append(copy)
    return started


def fill_masks(resets, masks):
    length = resets.shape[1]
    square = (length, length)
    earlier = lax.broadcasted_iota(jnp.int32, square, 0)
    reset = jnp.broadcast_to(resets[...].astype(F32), square).T
    keep = jnp.where(reset == 0.0, 1.0, 0.0)
    joined = jnp.where(earlier > 0, keep, 0.0)
    one_back = pltpu.roll(joined, 1, 0)
    two_back = pltpu.roll(joined, 2, 0)
    masks[0] = keep
    masks[1] = joined
    masks[2] = joined * one_back
    masks[3] = joined * one_back * two_back


def fill_choose(capacity, block_rows, experts, routes, choose):
    length = routes.shape[1]
    square = (length, length)
    earlier = lax.broadcasted_iota(jnp.int32, square, 0)
    later = lax.broadcasted_iota(jnp.int32, square, 1)
    route_of = jnp.broadcast_to(routes[...].astype(F32), square)
    same = (route_of.T == route_of) & (earlier < later)
    if block_rows < length:
        same = same & (earlier // block_rows == later // block_rows)
    rank = jnp.sum(jnp.where(same, 1.0, 0.0), axis=0, keepdims=True).astype(jnp.int32)
    group = routes[...]
    if block_rows < length:
        group = group + experts * (later[:1] // block_rows)
    slot = group * capacity + rank
    slot_count = choose.shape[0]
    slot_ids = lax.broadcasted_iota(jnp.int32, (slot_count, length), 0)
    hit = slot_ids == jnp.broadcast_to(slot, (slot_count, length))
    choose[...] = jnp.where(hit, 1.0, 0.0).astype(BF16)


def prepare_kernel(
    experts, capacity, block_rows, resets, routes, cotangent, masks, choose, slots
):
    fill_masks(resets, masks)
    fill_choose(capacity, block_rows, experts, routes, choose)
    slots[...] = dot_nn(choose[...], cotangent[...]).astype(BF16)


def put_folded(target, slots):
    rows, width = slots.shape
    units = target.shape[1]
    half = rows // 2
    rest = width - units
    target[:rows, :] = slots[:, :units]
    target[rows:, :rest] = slots[:half, units:]
    target[rows:, rest:] = slots[half:, units:]


def unfold_copies(source, target, top, rows):
    units = source.shape[1]
    half = rows // 2
    rest = target.shape[1] - units
    copies = [(source.at[pl.ds(0, rows)], target.at[pl.ds(top, rows), pl.ds(0, units)])]
    for part in range(2):
        copies.append(
            (
                source.at[pl.ds(rows, half), pl.ds(part * rest, rest)],
                target.at[pl.ds(top + part * half, half), pl.ds(units, rest)],
            )
        )
    return copies


def pack_kernel(
    capacity,
    resets_in,
    routes_in,
    cotangent_in,
    expert_in,
    expert_out,
    masks,
    choose,
    message,
    packed,
    staged,
    resets,
    routes,
    cotangent,
    early_arrivals,
    arrivals,
    semaphores,
):
    experts, share, units = expert_in.shape
    length, width = cotangent.shape
    copies = []
    for index in range(experts):
        copies.append((expert_in.at[index], staged.at[index, 0]))
        copies.append((expert_out.at[index], staged.at[index, 1]))
    early = run_copies(
        [(resets_in, resets), (routes_in, routes), (cotangent_in, cotangent)], early_arrivals
    )
    arriving = run_copies(copies, arrivals)
    for copy in early:
        copy.wait()
    fill_choose(capacity, length, experts, routes, choose)
    slots = dot_nn(choose[...], cotangent[...]).astype(BF16)
    started = []
    for index in range(experts):
        copies = []
        for which in range(2):
            arriving[2 * index + which].wait()
            target = message.at[index, pl.ds(which * share, share)]
            copies.append((staged.at[index, which], target))
        started += run_copies(copies, semaphores.at[pl.ds(2 * index, 2)])
    copies = []
    for index in range(experts):
        put_folded(packed.at[index], slots[index * capacity : (index + 1) * capacity])
        target = message.at[index]
        copies.append((packed.at[index], target.at[pl.ds(2 * share, packed.shape[1])]))
    started += run_copies(copies, semaphores.at[pl.ds(2 * experts, experts)])
    fill_masks(resets, masks)
    for copy in started:
        copy.wait()


def pass_on(along_x, along_y, pass_y, pass_x, passed, arrivals, semaphores):
    half = passed.shape[1]
    copies = [
        (along_y.at[pl.ds(0, half)], passed.at[0]),
        (along_x.at[pl.ds(half, half)], passed.at[1]),
    ]
    for copy in run_copies(copies, arrivals):
        copy.wait()
    return run_copies([(passed.at[0], pass_y), (passed.at[1], pass_x)], semaphores)


def pass_kernel(along_x, along_y, pass_y, pass_x, passed, arrivals, semaphores):
    for copy in pass_on(along_x, along_y, pass_y, pass_x, passed, arrivals, semaphores):
        copy.wait()


def unpack_kernel(
    share,
    capacity,
    message,
    first_out,
    second_out,
    slots_out,
    d_hidden,
    first_w,
    second_w,
    grad_slots,
    semaphores,
):
    folded = capacity + capacity // 2
    copies = []
    for index in range(message.shape[0]):
        piece = message.at[index]
        rows = pl.ds(index * share, share)
        copies.append((piece.at[pl.ds(share, share)], second_w.at[rows]))
        copies += unfold_copies(
            piece.at[pl.ds(2 * share, folded)], grad_slots, index * capacity, capacity
        )
        copies.append((piece.at[pl.ds(0, share)], first_w.at[rows]))
    for copy in run_copies(copies, semaphores):
        copy.wait()
    copies = [(first_w, first_out), (second_w, second_out), (grad_slots, slots_out)]
    started = run_copies(copies, semaphores)
    d_hidden[...] = dot_nn(grad_slots[...], second_w[...])
    for copy in started:
        copy.wait()


def put_blocks(target, values):
    length = values.shape[0]
    for start in range(0, values.shape[1], 128):
        target[start : start + length, :] = values[:, start : start + 128]


def enter_kernel(
    place,
    piece_0,
    piece_1,
    piece_2,
    piece_3,
    gain_ref,
    in_proj,
    conv_weight,
    conv_bias,
    x_proj,
    masks,
    rows_out,
    normed_out,
    act_out,
    inner_out,
    conv_out,
    gate_out,
    scale_out,
    gain_out,
    mixed_out,
    turned,
):
    take_row_pieces(place, (piece_0, piece_1, piece_2, piece_3), turned)
    rows = turned[...].T
    gain = as_row(gain_ref)
    rows_out[...] = rows.astype(BF16)
    normed = (rows * rms_rate(rows) * gain).astype(BF16)
    put_blocks(normed_out, normed)
    inner = dot_nt(normed, in_proj[0])
    chans = inner.shape[1]
    inner_out[...] = inner
    total = as_row(conv_bias) + conv_weight[3:4, :] * inner
    for shift in (1, 2, 3):
        moved = pltpu.roll(inner, shift, 0) * wide_masks(masks, shift, chans)
        total = total + conv_weight[3 - shift : 4 - shift, :] * moved
    conv_out[...] = total
    act = (total * jax.nn.sigmoid(total)).astype(BF16)
    act_out[...] = act
    mixed_out[...] = dot_nt(x_proj[...], act).astype(BF16)
    gate_out[...] = dot_nt(normed, in_proj[1])
    raw = turned[...]
    scale_out[...] = lax.rsqrt(jnp.mean(raw * raw, axis=0, keepdims=True) + EPSILON)
    turned[...] = jnp.broadcast_to(gain, rows.shape).T
    column = gain_out.shape[0]
    gain_out[...] = turned[pl.ds(pl.multiple_of(place[0] * column, column), column), :]


def block_columns(transposed, block):
    length = transposed.shape[1]
    return pltpu.roll(transposed, lax.rem(length - 8 * block, length), 1)


def spread_column(columns, row, tiles):
    return lane_tiles(jnp.broadcast_to(columns[:, row : row + 1], (columns.shape[0], 128)), tiles)


def scan_forward_kernel(
    place,
    piece_0,
    piece_1,
    piece_2,
    piece_3,
    dt_proj,
    dt_bias,
    decay_log,
    skip_gain,
    act_in,
    gate_in,
    masks,
    out_proj,
    normed,
    out_0,
    out_1,
    out_2,
    out_3,
    mixed_out,
    share_out,
    y_out,
    held,
    rate,
    step_rows,
    drive_rows,
    y_rows,
    partial,
):
    rank = dt_proj.shape[0]
    states = decay_log.shape[0]
    length, chans = y_out.shape
    tiles = step_rows.shape[1] // 128
    mixed = sum_pieces(place, (piece_0, piece_1, piece_2, piece_3), held)
    mixed_out[...] = mixed
    step_size = softplus(dot_tn(mixed[:rank].astype(BF16), dt_proj[...]) + as_row(dt_bias))
    act = act_in[...].astype(F32)
    reset = NEVER * (1.0 - wide_masks(masks, 0, chans))
    padded_copy(rate, -LOG2E * jnp.exp(decay_log[...]))
    padded_copy(step_rows, step_size + reset)
    padded_copy(drive_rows, step_size * act)
    b_turned = mixed[rank : rank + states]
    c_turned = mixed[rank + states : rank + 2 * states]

    def block(index, state):
        start = pl.multiple_of(index * 8, 8)
        b_cols = block_columns(b_turned, index)
        c_cols = block_columns(c_turned, index)
        steps = step_rows[pl.ds(start, 8), :]
        drives = drive_rows[pl.ds(start, 8), :]
        rows = []
        for row in range(8):
            decay = jnp.exp2(rate[...] * steps[row : row + 1])
            state = decay * state + spread_column(b_cols, row, tiles) * drives[row : row + 1]
            rows.append(
                jnp.sum(spread_column(c_cols, row, tiles) * state, axis=0, keepdims=True)
            )
        y_rows[pl.ds(start, 8), :] = jnp.concatenate(rows, axis=0)
        return state

    lax.fori_loop(0, length // 8, block, jnp.zeros((states, 128 * tiles), F32))
    y = y_rows[:, :chans] + as_row(skip_gain) * act
    y_out[...] = y
    gate = gate_in[...]
    gated = (y * (gate * jax.nn.sigmoid(gate))).astype(BF16)
    partial[...] = dot_nn(gated, out_proj[...])
    put_row_chunks(place, partial, (out_0, out_1, out_2, out_3))
    width = normed.shape[0]
    share_out[:width] = normed[...]
    padded_copy(step_rows, gated.astype(F32))
    share_out[width : width + chans] = step_rows[...].T[:chans].astype(BF16)
    padded_copy(step_rows, act)
    share_out[width + chans :] = step_rows[...].T[:chans].astype(BF16)


def dispatch_kernel(
    place,
    piece_0,
    piece_1,
    piece_2,
    piece_3,
    rows_in,
    gain,
    choose,
    residual_out,
    columns_out,
    slots,
    turned,
):
    take_row_pieces(place, (piece_0, piece_1, piece_2, piece_3), residual_out)
    residual = rows_in[...].astype(F32) + residual_out[...]
    residual_out[...] = residual
    send = (residual * rms_rate(residual) * as_row(gain)).astype(BF16)
    slots[...] = dot_nn(choose[...], send).astype(BF16)
    turned[...] = residual.T
    column = columns_out.shape[0]
    columns_out[...] = turned[pl.ds(pl.multiple_of(place[0] * column, column), column), :]


def hidden_back_kernel(grad_slots, second_w, d_hidden):
    d_hidden[...] = dot_nn(grad_slots[...], second_w[...])


def expert_kernel(arrived, first_w, d_hidden, hidden_out, d_pre_out, d_slots):
    value = dot_nn(arrived[...], first_w[...])
    square = value * value
    bend = jnp.tanh(GELU_SCALE * (value + GELU_CUBE * value * square))
    half = 0.5 * (1.0 + bend)
    slope = half + 0.5 * value * (1.0 - bend * bend) * GELU_SCALE * (
        1.0 + 3.0 * GELU_CUBE * square
    )
    d_pre = (slope * d_hidden[...]).astype(BF16)
    d_pre_out[...] = d_pre
    d_slots[...] = dot_nt(d_pre, first_w[...]).astype(BF16)
    hidden_out[...] = (value * half).astype(BF16)


def expert_grads_kernel(arrived, grad_slots, hidden, d_pre, second_w, first_out, second_out, moe):
    first_out[...] = dot_tn(arrived[...], d_pre[...]).astype(BF16)
    second_out[...] = dot_tn(grad_slots[...], hidden[...]).astype(BF16)
    moe[...] = dot_nt(hidden[...], second_w[...]).astype(BF16)


def expert_grads_pack_kernel(
    share, capacity, arrived, grad_slots, hidden, d_pre, second_w, message, grads, packed, semaphores
):
    experts = message.shape[0]
    started = []
    for which, (left, right) in enumerate(((arrived, d_pre), (grad_slots, hidden))):
        grads[which] = dot_tn(left[...], right[...]).astype(BF16)
        copies = [
            (
                grads.at[which, pl.ds(index * share, share)],
                message.at[index, pl.ds(which * share, share)],
            )
            for index in range(experts)
        ]
        started += run_copies(copies, semaphores.at[pl.ds(which * experts, experts)])
    moe = dot_nt(hidden[...], second_w[...]).astype(BF16)
    copies = []
    for index in range(experts):
        put_folded(packed.at[index], moe[index * capacity : (index + 1) * capacity])
        copies.append(
            (packed.at[index], message.at[index, pl.ds(2 * share, packed.shape[1])])
        )
    started += run_copies(copies, semaphores.at[pl.ds(2 * experts, experts)])
    for copy in started:
        copy.wait()


def owner_kernel(
    share,
    message,
    along_x,
    along_y,
    first_out,
    second_out,
    pass_y,
    pass_x,
    low,
    wide,
    passed,
    arrivals,
    semaphores,
):
    count = message.shape[0]
    arriving = run_copies(
        [(message.at[index, pl.ds(0, 2 * share)], low.at[index]) for index in range(count)],
        arrivals.at[pl.ds(2, count)],
    )
    started = pass_on(
        along_x,
        along_y,
        pass_y,
        pass_x,
        passed,
        arrivals.at[pl.ds(0, 2)],
        semaphores.at[pl.ds(0, 2)],
    )
    for index in range(count):
        arriving[index].wait()
        wide[index] = low[index].astype(F32)
        copies = [
            (wide.at[index, pl.ds(0, share)], first_out.at[index]),
            (wide.at[index, pl.ds(share, share)], second_out.at[index]),
        ]
        started += run_copies(copies, semaphores.at[pl.ds(2 + 2 * index, 2)])
    for copy in started:
        copy.wait()


def back_rows_kernel(place, choose, slots, out_0, out_1, out_2, out_3, partial):
    partial[...] = dot_tn(choose[...], slots[...])
    put_row_chunks(place, partial, (out_0, out_1, out_2, out_3))


def back_columns_kernel(place, choose, shares, slots, out_0, out_1, out_2, out_3, rows):
    rows[...] = dot_tn(slots[...], choose[...]).astype(BF16)
    outs = (out_0, out_1, out_2, out_3)
    count, top, _ = shares.shape
    column = rows.shape[0] // count
    for step, out in enumerate(outs):
        whose = lax.rem(place[0] + step, count)
        out[:top, :] = shares[whose]
        out[top:, :] = rows[pl.ds(pl.multiple_of(whose * column, column), column), :]


def back_folded_kernel(
    share,
    place,
    choose,
    shares,
    message,
    refs,
    out_0,
    out_1,
    out_2,
    out_3,
    weight_grad,
    bias_grad,
    slots,
    rows,
    staged,
    semaphores,
):
    count = message.shape[0]
    capacity = slots.shape[0] // count
    folded = message.shape[1] - 2 * share
    copies = []
    for index in range(count):
        copies += unfold_copies(
            message.at[index, pl.ds(2 * share, folded)], slots, index * capacity, capacity
        )
    deep = 2 * VECTORS_TWO
    height = staged.shape[1]
    top = refs[0].shape[0] - height
    copies += [(ref.at[pl.ds(top, height)], staged.at[index]) for index, ref in enumerate(refs)]
    for copy in run_copies(copies, semaphores):
        copy.wait()
    total = staged[0].astype(F32)
    for index in range(1, staged.shape[0]):
        total = total + staged[index].astype(F32)
    chans = weight_grad.shape[1]
    vectors = jnp.concatenate(
        [total[start : start + deep] for start in range(0, height, deep)], axis=1
    )[:, :chans]
    vectors = vectors[:VECTORS_TWO] + vectors[VECTORS_TWO:]
    weight_grad[...] = vectors[:4]
    bias_grad[...] = vectors[4].reshape(chans)
    norm_grad = jnp.concatenate([vectors[5:6], vectors[6:7]], axis=1)
    norm_rows = [norm_grad[:, start : start + 128] for start in range(0, norm_grad.shape[1], 128)]
    spare = jnp.zeros((NORM_ROWS - len(norm_rows), 128), F32)
    upper, lower = split_vectors(jnp.concatenate([*norm_rows, spare], axis=0))
    norm_low = jnp.concatenate([upper, lower], axis=0).astype(BF16)
    outs = (out_0, out_1, out_2, out_3)
    plain = out_0.shape[0] - 2 * NORM_ROWS
    back_columns_kernel(
        place, choose, shares, slots, *[out.at[pl.ds(0, plain)] for out in outs], rows
    )
    for out in outs:
        out[plain:, :] = norm_low


def mixer_grad_kernel(
    place,
    piece_0,
    piece_1,
    piece_2,
    piece_3,
    residual_in,
    gain_ref,
    cotangent,
    out_proj,
    columns_out,
    mix_out,
    d_gated,
    gain_grad,
    d_send,
    turned,
):
    take_row_pieces(place, (piece_0, piece_1, piece_2, piece_3), d_send)
    residual = residual_in[...]
    inverse = rms_rate(residual)
    scaled = residual * inverse
    grad = d_send[...]
    pulled = grad * as_row(gain_ref)
    along = jnp.mean(pulled * scaled, axis=-1, keepdims=True)
    d_residual = cotangent[...].astype(F32) + inverse * (pulled - scaled * along)
    d_mix = d_residual.astype(BF16)
    put_blocks(mix_out, d_mix)
    d_gated[...] = dot_nt(d_mix, out_proj[...])
    gain_grad[...] = jnp.sum(grad * scaled, axis=0, keepdims=True)
    turned[...] = d_residual.T
    column = columns_out.shape[0]
    columns_out[...] = turned[pl.ds(pl.multiple_of(place[0] * column, column), column), :]


def split_vectors(vectors):
    upper = vectors.astype(BF16).astype(F32)
    return upper, vectors - upper


def scan_states_kernel(
    y_in,
    gate_in,
    act_in,
    mixed_in,
    masks,
    dt_proj,
    dt_bias,
    decay_log,
    decays,
    history,
    step_rows,
    drive_rows,
    step_slope,
    y_slope,
    gate_slope,
    rate,
    decay_rows,
):
    rank = dt_proj.shape[0]
    states = decay_log.shape[0]
    length, chans = y_in.shape
    tiles = step_rows.shape[1] // 128
    full = 128 * tiles
    mixed = mixed_in[...]
    raw_step = dot_tn(mixed[:rank].astype(BF16), dt_proj[...]) + as_row(dt_bias)
    step_size = softplus(raw_step)
    step_slope[...] = jax.nn.sigmoid(raw_step)
    reset = NEVER * (1.0 - wide_masks(masks, 0, chans))
    padded_copy(rate, -LOG2E * jnp.exp(decay_log[...]))
    padded_copy(step_rows, step_size)
    padded_copy(decay_rows, step_size + reset)
    padded_copy(drive_rows, step_size * act_in[...].astype(F32))
    gate = gate_in[...]
    gate_sig = jax.nn.sigmoid(gate)
    y_slope[...] = gate * gate_sig
    gate_slope[...] = y_in[...] * gate_sig * (1.0 + gate * (1.0 - gate_sig))
    b_turned = mixed[rank : rank + states]
    history[pl.ds(0, states), :] = jnp.zeros((states, full), F32)

    def forward_block(index, state):
        start = pl.multiple_of(index * 8, 8)
        b_cols = block_columns(b_turned, index)
        steps = decay_rows[pl.ds(start, 8), :]
        drives = drive_rows[pl.ds(start, 8), :]
        for row in range(8):
            decay = jnp.exp2(rate[...] * steps[row : row + 1])
            state = decay * state + spread_column(b_cols, row, tiles) * drives[row : row + 1]
            at = pl.multiple_of((start + row) * states, states)
            decays[pl.ds(at, states), :] = decay
            history[pl.ds(at + states, states), :] = state
        return state

    lax.fori_loop(0, length // 8, forward_block, jnp.zeros((states, full), F32))


def scan_backward_kernel(
    d_gated,
    y_slope,
    gate_slope,
    act_in,
    mixed_in,
    dt_proj,
    decay_log,
    skip_gain,
    gain_grad,
    d_mix,
    decays,
    history,
    step_rows,
    drive_rows,
    step_slope,
    d_mixed_out,
    d_act_out,
    d_gate_out,
    share_out,
    rate,
    dy_rows,
    du_rows,
    dl_rows,
):
    rank = dt_proj.shape[0]
    states = decay_log.shape[0]
    length, chans = y_slope.shape
    tiles = step_rows.shape[1] // 128
    full = 128 * tiles
    mixed = mixed_in[...]
    dt_low = mixed[:rank].astype(BF16)
    act = act_in[...].astype(F32)
    padded_copy(rate, -jnp.exp(decay_log[...]))
    d_out = d_gated[...]
    d_y = d_out * y_slope[...]
    padded_copy(dy_rows, d_y)
    d_gate = d_out * gate_slope[...]
    b_turned = mixed[rank : rank + states]
    c_turned = mixed[rank + states : rank + 2 * states]
    lanes = lax.broadcasted_iota(jnp.int32, (states, length), 1)

    def backward_block(count, carry):
        carried, d_rate, d_b, d_c = carry
        index = length // 8 - 1 - count
        start = pl.multiple_of(index * 8, 8)
        b_cols = block_columns(b_turned, index)
        c_cols = block_columns(c_turned, index)
        steps = step_rows[pl.ds(start, 8), :]
        drives = drive_rows[pl.ds(start, 8), :]
        dys = dy_rows[pl.ds(start, 8), :]
        du = [None] * 8
        dl = [None] * 8
        for row in reversed(range(8)):
            at = pl.multiple_of((start + row) * states, states)
            before = history[pl.ds(at, states), :]
            after = history[pl.ds(at + states, states), :]
            decay = decays[pl.ds(at, states), :]
            here = lanes == start + row
            dy_row = jnp.broadcast_to(dys[row : row + 1], (states, full))
            grad = spread_column(c_cols, row, tiles) * dy_row + carried
            c_part = jnp.sum(fold_tiles(dy_row * after), axis=1, keepdims=True)
            d_c = jnp.where(here, c_part, d_c)
            b_part = jnp.sum(fold_tiles(grad * drives[row : row + 1]), axis=1, keepdims=True)
            d_b = jnp.where(here, b_part, d_b)
            du[row] = jnp.sum(grad * spread_column(b_cols, row, tiles), axis=0, keepdims=True)
            carried = grad * decay
            d_log = carried * before
            dl[row] = jnp.sum(d_log * rate[...], axis=0, keepdims=True)
            d_rate = d_rate + d_log * steps[row : row + 1]
        du_rows[pl.ds(start, 8), :] = jnp.concatenate(du, axis=0)
        dl_rows[pl.ds(start, 8), :] = jnp.concatenate(dl, axis=0)
        return carried, d_rate, d_b, d_c

    nothing = jnp.zeros((states, full), F32)
    thin = jnp.zeros((states, length), F32)
    _, d_rate, d_b, d_c = lax.fori_loop(
        0, length // 8, backward_block, (nothing, nothing, thin, thin)
    )
    du = du_rows[:, :chans]
    d_step = (dl_rows[:, :chans] + du * act) * step_slope[...]
    d_step_low = d_step.astype(BF16)
    low_turned = dot_nt(dt_proj[...], d_step_low)
    d_mixed_out[...] = jnp.concatenate([low_turned, d_b, d_c], axis=0).astype(BF16)
    d_act_out[...] = du * step_rows[:, :chans] + as_row(skip_gain) * d_y
    d_gate_low = d_gate.astype(BF16)
    d_gate_out[...] = d_gate_low
    width = d_mix.shape[0]
    share_out[:width] = d_mix[...]
    padded_copy(du_rows, d_gate_low.astype(F32))
    share_out[width : width + chans] = du_rows[...].T[:chans].astype(BF16)
    gain_rows = gain_grad[...]
    upper, lower = split_vectors(
        jnp.concatenate(
            [
                (d_rate * rate[...])[:, :chans],
                jnp.sum(d_step, axis=0, keepdims=True),
                jnp.sum(d_y * act, axis=0, keepdims=True),
                gain_rows[:, :chans],
                gain_rows[:, chans:],
                jnp.zeros((VECTORS_ONE - states - 4, chans), F32),
            ],
            axis=0,
        )
    )
    dl_rows[...] = jnp.zeros(dl_rows.shape, F32)
    dl_rows[:rank, :chans] = dot_nn(dt_low, d_step_low)
    dl_rows[rank : rank + VECTORS_ONE, :chans] = upper
    dl_rows[rank + VECTORS_ONE : rank + 2 * VECTORS_ONE, :chans] = lower
    share_out[width + chans :] = dl_rows[...].T[:chans].astype(BF16)


def leave_kernel(
    place,
    piece_0,
    piece_1,
    piece_2,
    piece_3,
    d_act_scan,
    d_gate,
    conv_in,
    inner_in,
    masks,
    x_proj,
    conv_weight,
    in_proj,
    rows_in,
    gain,
    shares,
    message,
    held,
    turned,
    padded,
):
    length, chans = inner_in.shape
    width = rows_in.shape[1]
    full = padded.shape[1]
    d_mixed = sum_pieces(place, (piece_0, piece_1, piece_2, piece_3), held).astype(BF16)
    d_act = d_act_scan[...] + dot_tn(d_mixed, x_proj[...])
    conv = conv_in[...]
    sig = jax.nn.sigmoid(conv)
    d_conv = d_act * sig * (1.0 + conv * (1.0 - sig))
    inner = inner_in[...]
    d_inner = conv_weight[3:4, :] * d_conv
    weight_grads = [jnp.sum(d_conv * inner, axis=0, keepdims=True)]
    for shift in (1, 2, 3):
        masked = d_conv * wide_masks(masks, shift, chans)
        weight_grads.append(
            jnp.sum(masked * pltpu.roll(inner, shift, 0), axis=0, keepdims=True)
        )
        d_inner = d_inner + conv_weight[3 - shift : 4 - shift, :] * pltpu.roll(
            masked, length - shift, 0
        )
    d_inner_low = d_inner.astype(BF16)
    padded_copy(padded, d_inner_low.astype(F32))
    message[:chans] = padded[...].T[:chans].astype(BF16)
    proj = d_mixed.shape[0]
    top = message.shape[0] - full // 128 * 2 * VECTORS_TWO
    message[chans:top] = jnp.concatenate(
        [d_mixed.astype(F32), jnp.zeros((top - chans - proj, length), F32)], axis=0
    ).astype(BF16)
    d_normed = dot_nn(d_inner_low, in_proj[0]) + dot_nn(d_gate[...], in_proj[1])
    rows = rows_in[...].astype(F32)
    scaled = rows * rms_rate(rows)
    norm_grad = jnp.sum(d_normed * scaled, axis=0, keepdims=True)
    upper, lower = split_vectors(
        jnp.concatenate(
            [
                weight_grads[3],
                weight_grads[2],
                weight_grads[1],
                weight_grads[0],
                jnp.sum(d_conv, axis=0, keepdims=True),
                norm_grad[:, :chans],
                norm_grad[:, chans:],
                jnp.zeros((VECTORS_TWO - 7, chans), F32),
            ],
            axis=0,
        )
    )
    padded_copy(padded, jnp.zeros((length, chans), F32))
    padded[:VECTORS_TWO, :chans] = upper
    padded[VECTORS_TWO : 2 * VECTORS_TWO, :chans] = lower
    for tile in range(full // 128):
        message[top + tile * 2 * VECTORS_TWO : top + (tile + 1) * 2 * VECTORS_TWO] = padded[
            : 2 * VECTORS_TWO, tile * 128 : (tile + 1) * 128
        ].astype(BF16)
    along = jnp.mean(d_normed * as_row(gain) * scaled, axis=-1, keepdims=True)
    along = jnp.broadcast_to(along, (length, length)).T[:8]
    high = along.astype(BF16)
    low = (along - high.astype(F32)).astype(BF16)
    turned[...] = d_normed.T
    count, rows, _ = shares.shape
    column = width // count
    ends = jnp.concatenate([high, low], axis=0)
    for index in range(count):
        shares[index, :column, :] = turned[index * column : (index + 1) * column].astype(BF16)
        shares[index, column:, :] = ends


def finish_rows_kernel(
    piece_0,
    piece_1,
    piece_2,
    piece_3,
    residual,
    d_columns,
    tokens,
    scale,
    gain,
    outcome,
    grad_tokens,
    *norm_out,
):
    column = tokens.shape[0]
    total = piece_0[...].astype(F32)
    for piece in (piece_1, piece_2, piece_3):
        total = total + piece[...].astype(F32)
    along = total[column : column + 1] + total[column + 8 : column + 9]
    inverse = scale[...]
    pulled = total[:column] * gain[...]
    scaled = tokens[...].astype(F32) * inverse
    grad_tokens[...] = d_columns[...] + inverse * (pulled - scaled * along)
    plain = 2 * column + 16
    outcome[...] = (residual[...] + total[column + 16 : plain]).astype(BF16)
    for out in norm_out:
        norm = total[plain : plain + NORM_ROWS] + total[plain + NORM_ROWS :]
        width = out.shape[0]
        out[...] = jnp.concatenate(
            [norm[row : row + 1] for row in range(width // 128)], axis=1
        ).reshape(width)


def take_blocks(target, pieces):
    for index, piece in enumerate(pieces):
        for start in range(0, target.shape[1], 128):
            target[index * 128 : (index + 1) * 128, start : start + 128] = piece[
                start : start + 128
            ]


def take_turned(target, pieces, start):
    rows = target.shape[0]
    for index, piece in enumerate(pieces):
        target[:, index * 128 : (index + 1) * 128] = piece[start : start + rows]


def stage_pieces(refs, staged, semaphores, rows=None):
    copies = []
    parts = len(refs) // 2
    for index, ref in enumerate(refs):
        side, part = divmod(index, parts)
        target = staged.at[4 * side + min(part, 3)]
        if part >= 3 and parts > 4:
            height = staged.shape[1] // (parts - 3)
            target = target.at[pl.ds((part - 3) * height, height)]
        copies.append((ref if rows is None else ref.at[pl.ds(*rows)], target))
    return run_copies(copies, semaphores), [staged.at[index] for index in range(8)]


def first_sets_kernel(refs, normed, gated, acts, staged, semaphores):
    chans = gated.shape[0]
    width = normed.shape[1]
    arriving, firsts = stage_pieces(refs, staged, semaphores)
    for copy in arriving:
        copy.wait()
    take_blocks(normed, firsts)
    take_turned(gated, firsts, width)
    take_turned(acts, firsts, width + chans)


def wide_grads_kernel(
    sizes,
    second_refs,
    last_refs,
    normed,
    gated,
    acts,
    out_grad,
    in_grad,
    x_grad,
    dt_grad,
    bias_grad,
    decay_grad,
    skip_grad,
    norm_grad,
    staged,
    staged_last,
    mixed,
    d_gate,
    d_mixed,
    total,
    wide_grad,
    second_arrivals,
    last_arrivals,
    semaphores,
):
    rank, states, proj = sizes
    chans, width = out_grad.shape
    arriving_last, lasts = stage_pieces(last_refs, staged_last, last_arrivals)
    for copy in arriving_last:
        copy.wait()
    arriving, seconds = stage_pieces(second_refs, staged, second_arrivals)
    take_turned(d_gate, lasts, 0)
    wide_grad[0] = dot_nn(d_gate[...], normed[...])
    started = run_copies([(wide_grad.at[0], in_grad.at[0])], semaphores)
    for copy in arriving:
        copy.wait()
    take_turned(d_gate, seconds, width)
    wide_grad[1] = dot_nn(d_gate[...], normed[...])
    started += run_copies([(wide_grad.at[1], in_grad.at[1])], semaphores.at[pl.ds(1, 1)])
    take_blocks(mixed, seconds)
    half = chans // 2
    for index in range(2):
        rows = pl.ds(index * half, half)
        wide_grad[2, rows] = dot_nn(gated[rows], mixed[...])
        started += run_copies(
            [(wide_grad.at[2, rows], out_grad.at[rows])], semaphores.at[pl.ds(2 + index, 1)]
        )
    take_turned(d_mixed, lasts, chans)
    x_grad[...] = dot_nt(d_mixed[...], acts[...])[:proj]
    vectors = seconds[0][width + chans :].astype(F32)
    for piece in seconds[1:]:
        vectors = vectors + piece[width + chans :].astype(F32)
    total[...] = jnp.zeros(total.shape, F32)
    total[:chans] = vectors
    rows = total[...].T[:, :chans]
    dt_grad[...] = rows[:rank]
    rows = rows[rank : rank + VECTORS_ONE] + rows[rank + VECTORS_ONE : rank + 2 * VECTORS_ONE]
    decay_grad[...] = rows[:states]
    bias_grad[...] = rows[states].reshape(chans)
    skip_grad[...] = rows[states + 1].reshape(chans)
    norm_grad[...] = jnp.concatenate(
        [rows[states + 2 : states + 3], rows[states + 3 : states + 4]], axis=1
    ).reshape(width)
    for copy in started:
        copy.wait()


def send_chunks(chunks):
    count = len(chunks)
    pairs = [[(i, (i + s) % count) for i in range(count)] for s in range(count)]
    return [chunks[0]] + [lax.ppermute(chunks[s], "tensor", pairs[s]) for s in range(1, count)]


def share_rows(values, count):
    return send_chunks([values] * count)


def add_low(pieces):
    total = pieces[0].astype(F32)
    for piece in pieces[1:]:
        total = total + piece.astype(F32)
    return total.astype(BF16)


def after(values, *events):
    return list(lax.optimization_barrier((tuple(values), events))[0])


def swap(values, bits):
    return lax.ppermute(values, "dp", [(i, i ^ bits) for i in range(NEAR_GROUPS)])


def swap_across(halves):
    return [swap(halves[0], 2), swap(halves[1], 4)]


def swap_near(values):
    return [*values, *[swap(part, 1) for part in values]]


def body(
    tokens,
    resets,
    routes,
    norm_one,
    in_proj,
    conv_weight,
    conv_bias,
    x_proj,
    dt_proj,
    dt_bias,
    decay_log,
    skip_gain,
    out_proj,
    norm_two,
    expert_in,
    expert_out,
    cotangent,
):
    groups = lax.axis_size("dp")
    parts = lax.axis_size("tensor")
    place = lax.axis_index("tensor").astype(jnp.int32).reshape(1)
    length, column = tokens.shape
    width = norm_one.shape[0]
    rank, chans = dt_proj.shape
    states = decay_log.shape[0]
    experts, share, hidden_units = expert_in.shape
    proj = x_proj.shape[1]
    tile_count = groups // experts
    block_rows = length * experts // groups
    capacity = max(2, block_rows // 4)
    slot_count = groups * capacity
    tiles = -(-chans // 128)
    full = 128 * tiles
    near = groups == NEAR_GROUPS and experts == groups
    tokens_turned = tokens.T
    in_turned = jnp.swapaxes(in_proj, 1, 2)
    x_turned = x_proj.T
    resets_row = resets.reshape(1, length)
    routes_row = routes.reshape(1, length)

    def exchange(values):
        return lax.all_to_all(values, "dp", split_axis=0, concat_axis=0, tiled=True)

    def exchange_slots(slots):
        return exchange(slots.reshape(groups, capacity, width)).reshape(slot_count, width)

    token_pieces = share_rows(tokens_turned, parts)
    mask_out = ((4, length, 128), F32)
    choose_out = ((slot_count, length), BF16)
    weight_outs = [((width, hidden_units), BF16)] * 2
    slots_out = ((slot_count, width), BF16)
    hidden_out = ((slot_count, hidden_units), BF16)
    folded = capacity + capacity // 2
    message_out = ((groups, 2 * share + folded, hidden_units), BF16)
    if near:
        masks, choose, packed = run_kernel(
            functools.partial(pack_kernel, capacity),
            [mask_out, choose_out, message_out],
            [resets_row, routes_row, cotangent, expert_in, expert_out],
            [
                ((groups, folded, hidden_units), BF16),
                ((experts, 2, share, hidden_units), BF16),
                ((1, length), jnp.int32),
                ((1, length), jnp.int32),
                ((length, width), BF16),
                pltpu.SemaphoreType.DMA((3,)),
                pltpu.SemaphoreType.DMA((2 * experts,)),
                pltpu.SemaphoreType.DMA((3 * experts,)),
            ],
            far_args=range(5),
            far_outs=(2,), )
        weights = exchange(packed)
    else:
        masks, choose, grad_send = run_kernel(
            functools.partial(prepare_kernel, experts, capacity, block_rows),
            [mask_out, choose_out, slots_out],
            [resets_row, routes_row, cotangent], loose_outs=(2,))
        first_w = exchange(jnp.tile(expert_in, (tile_count, 1, 1))).reshape(weight_outs[0][0])
        second_w = exchange(jnp.tile(expert_out, (tile_count, 1, 1))).reshape(weight_outs[0][0])
        grad_slots = exchange_slots(grad_send)
        (d_hidden,) = run_kernel(
            hidden_back_kernel, [((slot_count, hidden_units), F32)], [grad_slots, second_w]
        )

    rows, normed, act, inner, conv, gate, scale, gain_columns, mixed_part = run_kernel(
        enter_kernel,
        [
            ((length, width), BF16),
            ((width, length), BF16),
            ((length, chans), BF16),
            ((length, chans), F32),
            ((length, chans), F32),
            ((length, chans), F32),
            ((1, length), F32),
            ((column, length), F32),
            ((proj, length), BF16),
        ],
        [place, *token_pieces, norm_one, in_turned, conv_weight, conv_bias, x_turned, masks],
        [((width, length), F32)],
        scalars=1, loose_outs=(8,), staged=(1, 2, 3, 4, 10))
    mixed_pieces = share_rows(mixed_part, parts)
    *mix_chunks, mixed, first, y = run_kernel(
        scan_forward_kernel,
        [((length // parts, width), BF16)] * parts
        + [
            ((proj, length), F32),
            ((width + 2 * chans, length), BF16),
            ((length, chans), F32),
        ],
        [
            place,
            *mixed_pieces,
            dt_proj,
            dt_bias,
            decay_log,
            skip_gain,
            act,
            gate,
            masks,
            out_proj,
            normed,
        ],
        [
            ((parts, proj, length), BF16),
            ((states, full), F32),
            ((length, full), F32),
            ((length, full), F32),
            ((length, full), F32),
            ((length, width), F32),
        ],
        scalars=1, loose_outs=(0, 1, 2, 3, 5), staged=(1, 2, 3, 4, 9, 10, 11, 13))
    mixer_pieces = share_rows(add_low(send_chunks(mix_chunks)), parts)
    if near:
        first_x, first_y = swap(first, 2), swap(first, 4)
    residual, residual_columns, send_slots = run_kernel(
        dispatch_kernel,
        [((length, width), F32), ((column, length), F32), slots_out],
        [place, *mixer_pieces, rows, norm_two, choose],
        [((width, length), F32)],
        scalars=1, staged=(1, 5, 7))
    if near:
        half_out = (((width + 2 * chans) // 2, length), BF16)
        first_w, second_w, grad_slots, d_hidden = run_kernel(
            functools.partial(unpack_kernel, share, capacity),
            weight_outs + [slots_out, ((slot_count, hidden_units), F32)],
            after([weights], send_slots),
            [*weight_outs, slots_out, pltpu.SemaphoreType.DMA((5 * groups,))],
            far_args=(0,),
            far_outs=(0, 1, 2),
        )
        first_x, first_y = after([first_x, first_y], d_hidden)
        halves = run_kernel(
            pass_kernel,
            [half_out, half_out],
            [first_x, first_y],
            [
                ((2, *half_out[0]), BF16),
                pltpu.SemaphoreType.DMA((2,)),
                pltpu.SemaphoreType.DMA((2,)),
            ],
            far_args=(0, 1),
            far_outs=(0, 1),
        )
        first_d = swap_across(halves)
    arrived = exchange_slots(send_slots)
    hidden, d_pre, d_slots = run_kernel(
        expert_kernel, [hidden_out, hidden_out, slots_out], [arrived, first_w, d_hidden], staged=(0, 1, 2))
    if near:
        d_slots = after([d_slots], first_d)[0]
    back_slots = exchange_slots(d_slots)
    grad_args = [arrived, grad_slots, hidden, d_pre, second_w]
    grad_out = ((experts, share, hidden_units), F32)
    if near:
        (packed,) = run_kernel(
            functools.partial(expert_grads_pack_kernel, share, capacity),
            [message_out],
            grad_args,
            [
                ((2, width, hidden_units), BF16),
                ((groups, folded, hidden_units), BF16),
                pltpu.SemaphoreType.DMA((3 * groups,)),
            ],
            far_outs=(0,), staged=range(5))
        firsts = swap_near([first, first_x, first_y, *first_d])
        back_slots = after([back_slots], packed, firsts)[0]
        packed = after([packed], back_slots)[0]
        owned = exchange(packed)
    else:
        grad_first, grad_second, moe_slots = run_kernel(
            expert_grads_kernel, weight_outs + [slots_out], grad_args, loose_outs=(0, 1, 2))
    back_chunks = run_kernel(
        back_rows_kernel,
        [((length // parts, width), BF16)] * parts,
        [place, choose, back_slots],
        [((length, width), F32)],
        scalars=1, loose_outs=(0, 1, 2, 3), staged=(1, 2))
    send_pieces = share_rows(add_low(send_chunks(back_chunks)), parts)
    decays, history, step_rows, drive_rows, step_slope, y_slope, gate_slope = run_kernel(
        scan_states_kernel,
        [
            ((length * states, full), F32),
            (((length + 1) * states, full), F32),
            ((length, full), F32),
            ((length, full), F32),
            ((length, chans), F32),
            ((length, chans), F32),
            ((length, chans), F32),
        ],
        [y, gate, act, *after([mixed], back_chunks[0]), masks, dt_proj, dt_bias, decay_log],
        [((states, full), F32), ((length, full), F32)],
        staged=range(5),
        held_outs=range(7),
    )
    send_pieces = after(send_pieces, decays)
    d_columns, d_mix, d_gated, gain_grad_two = run_kernel(
        mixer_grad_kernel,
        [
            ((column, length), F32),
            ((width, length), BF16),
            ((length, chans), F32),
            ((1, width), F32),
        ],
        [place, *send_pieces, residual, norm_two, cotangent, out_proj],
        [((length, width), F32), ((width, length), F32)],
        scalars=1, staged=(1, 5, 7, 8), held_outs=(1, 2, 3))
    d_mixed_part, d_act_scan, d_gate, second = run_kernel(
        scan_backward_kernel,
        [
            ((proj, length), BF16),
            ((length, chans), F32),
            ((length, chans), BF16),
            ((width + 2 * chans, length), BF16),
        ],
        [
            d_gated,
            y_slope,
            gate_slope,
            act,
            mixed,
            dt_proj,
            decay_log,
            skip_gain,
            gain_grad_two,
            d_mix,
            decays,
            history,
            step_rows,
            drive_rows,
            step_slope,
        ],
        [
            ((states, full), F32),
            ((length, full), F32),
            ((length, full), F32),
            ((length, full), F32),
        ],
        staged=(3, 4),
        loose_outs=(0, 3),
        held_outs=(1, 2),
    )
    d_mixed_pieces = share_rows(d_mixed_part, parts)
    if near:
        second_x, second_y = swap(second, 2), swap(second, 4)
    last_rows = chans + -(-proj // 16) * 16 + tiles * 2 * VECTORS_TWO
    normed_shares, message = run_kernel(
        leave_kernel,
        [((parts, column + 16, length), BF16), ((last_rows, length), BF16)],
        [
            place,
            *d_mixed_pieces,
            d_act_scan,
            d_gate,
            conv,
            inner,
            masks,
            x_turned,
            conv_weight,
            in_turned,
            rows,
            norm_one,
        ],
        [((parts, proj, length), BF16), ((width, length), F32), ((length, full), F32)],
        scalars=1, loose_outs=(1,), staged=(1, 7, 8, 9, 13))
    share_outs = [((2 * column + 16, length), BF16)] * parts
    if near:
        lasts = [message, swap(message, 2), swap(message, 4), swap(message, 6)]
        def first_sets(*refs):
            first_sets_kernel(refs[:10], *refs[10:])

        all_normed, all_gated, all_act = run_kernel(
            first_sets,
            [
                ((groups * length, width), BF16),
                ((chans, groups * length), BF16),
                ((chans, groups * length), BF16),
            ],
            after(firsts, message, owned),
            [((groups, width + 2 * chans, length), BF16), pltpu.SemaphoreType.DMA((10,))],
            far_args=range(10),
            held_outs=(0, 1, 2),
        )
        second_x, second_y = after([second_x, second_y], all_normed)
        grad_expert_in, grad_expert_out, *halves = run_kernel(
            functools.partial(owner_kernel, share),
            [grad_out, grad_out, half_out, half_out],
            [owned, second_x, second_y],
            [
                ((groups, 2 * share, hidden_units), BF16),
                ((groups, 2 * share, hidden_units), F32),
                ((2, *half_out[0]), BF16),
                pltpu.SemaphoreType.DMA((2 + groups,)),
                pltpu.SemaphoreType.DMA((2 + 2 * groups,)),
            ],
            far_args=(0, 1, 2),
            far_outs=(0, 1, 2, 3),
        )
        second_d = swap_across(halves)
        lasts = swap_near(after(lasts, halves))

        def back_folded(*refs):
            back_folded_kernel(share, *refs[:4], refs[4 : 4 + groups], *refs[4 + groups :])

        *shares, grad_conv_weight, grad_conv_bias = run_kernel(
            back_folded,
            [((2 * column + 16 + 2 * NORM_ROWS, length), BF16)] * parts
            + [((4, chans), F32), ((chans,), F32)],
            [place, choose, normed_shares, owned, *lasts],
            [
                slots_out,
                ((width, length), BF16),
                ((groups, tiles * 2 * VECTORS_TWO, length), BF16),
                pltpu.SemaphoreType.DMA((4 * groups,)),
            ],
            scalars=1,
            staged=(1, 2),
            far_args=range(3, 4 + groups),
            loose_outs=(parts, parts + 1),
        )
        norm_out = [((width,), F32)]
    else:
        shares = run_kernel(
            back_columns_kernel,
            share_outs,
            [place, choose, normed_shares, exchange_slots(moe_slots)],
            [((width, length), BF16)],
            scalars=1,
            loose_outs=(0, 1, 2, 3),
        )

        norm_out = []

        def owner_sum(values):
            got = exchange(values.reshape(groups, share, hidden_units)).astype(F32)
            return jnp.sum(got.reshape(tile_count, experts, share, hidden_units), axis=0)

        grad_expert_in = owner_sum(grad_first)
        grad_expert_out = owner_sum(grad_second)
    pieces = send_chunks(shares)
    if near:
        seconds = [second, second_x, second_y, *second_d]
        seconds = swap_near(after(seconds, grad_conv_weight))

        def wide_grads(*refs):
            wide_grads_kernel(
                (rank, states, proj), refs[:10], refs[10 : 10 + groups], *refs[10 + groups :]
            )

        (
            grad_out_proj,
            grad_in_turned,
            grad_x_turned,
            grad_dt_proj,
            grad_dt_bias,
            grad_decay_log,
            grad_skip_gain,
            grad_norm_two,
        ) = run_kernel(
            wide_grads,
            [
                ((chans, width), F32),
                ((2, chans, width), F32),
                ((proj, chans), F32),
                ((rank, chans), F32),
                ((chans,), F32),
                ((states, chans), F32),
                ((chans,), F32),
                ((width,), F32),
            ],
            [*seconds, *lasts, all_normed, all_gated, all_act],
            [
                ((groups, width + 2 * chans, length), BF16),
                ((groups, last_rows, length), BF16),
                ((groups * length, width), BF16),
                ((chans, groups * length), BF16),
                ((-(-proj // 16) * 16, groups * length), BF16),
                ((full, length), F32),
                ((3, chans, width), F32),
                pltpu.SemaphoreType.DMA((10,)),
                pltpu.SemaphoreType.DMA((groups,)),
                pltpu.SemaphoreType.DMA((4,)),
            ],
            far_args=range(10 + groups),
            far_outs=(0, 1),
            loose_outs=range(8),
        )
        pieces = after(pieces, grad_out_proj)
    else:
        top = last_rows - tiles * 2 * VECTORS_TWO
        ones = second[width + chans :].astype(F32).T
        twos = message[top:].astype(F32).reshape(tiles, 2 * VECTORS_TWO, length)
        twos = jnp.swapaxes(twos, 0, 1).reshape(2 * VECTORS_TWO, full)[:, :chans]
        plain_normed = jnp.swapaxes(normed.reshape(-1, length, 128), 0, 1).reshape(length, width)
        plain_mix = jnp.swapaxes(d_mix.reshape(-1, length, 128), 0, 1).reshape(length, width)
        grad_in_turned, grad_x_turned, grad_dt_proj, grad_out_proj, ones, twos = lax.psum(
            (
                jnp.stack(
                    [
                        dot_nn(message[:chans], plain_normed),
                        dot_nn(second[width : width + chans], plain_normed),
                    ]
                ),
                dot_nn(message[chans : chans + proj], act),
                ones[:rank],
                dot_nn(first[width : width + chans], plain_mix),
                ones[rank : rank + VECTORS_ONE]
                + ones[rank + VECTORS_ONE : rank + 2 * VECTORS_ONE],
                twos[:VECTORS_TWO] + twos[VECTORS_TWO:],
            ),
            "dp",
        )
        grad_decay_log = ones[:states]
        grad_dt_bias = ones[states]
        grad_skip_gain = ones[states + 1]
        grad_norm_two = ones[states + 2 : states + 4]
        grad_conv_weight = twos[:4]
        grad_conv_bias = twos[4]
        grad_norm_one = sum(share_rows(twos[5:7].reshape(1, width), parts)).reshape(width)
    outcome, grad_tokens, *norm_one_grad = run_kernel(
        finish_rows_kernel,
        [((column, length), BF16), ((column, length), F32)] + norm_out,
        [*pieces, residual_columns, d_columns, tokens_turned, scale, gain_columns],
        staged=range(4, 9),
        loose_outs=(0, 1, 2),
    )
    if near:
        (grad_norm_one,) = norm_one_grad
    return (
        outcome.T,
        grad_tokens.T,
        grad_norm_one,
        jnp.swapaxes(grad_in_turned, 1, 2),
        grad_conv_weight,
        grad_conv_bias,
        grad_x_turned.T,
        grad_dt_proj,
        grad_dt_bias,
        grad_decay_log,
        grad_skip_gain,
        grad_out_proj,
        grad_norm_two.reshape(width),
        grad_expert_in,
        grad_expert_out,
    )


def solution(mesh):
    placed = (
        P("dp", "tensor"),
        P("dp"),
        P("dp", None),
        P(),
        P(None, None, "tensor"),
        P(None, "tensor"),
        P("tensor"),
        P("tensor", None),
        P(None, "tensor"),
        P("tensor"),
        P(None, "tensor"),
        P("tensor"),
        P("tensor", None),
        P(),
        P(None, "dp", "tensor"),
        P(None, "dp", "tensor"),
        P("dp", None),
    )
    return jax.shard_map(
        body,
        mesh=mesh,
        in_specs=placed,
        out_specs=(
            P("dp", "tensor"),
            P("dp", "tensor"),
            P(),
            P(None, None, "tensor"),
            P(None, "tensor"),
            P("tensor"),
            P("tensor", None),
            P(None, "tensor"),
            P("tensor"),
            P(None, "tensor"),
            P("tensor"),
            P("tensor", None),
            P(),
            P(None, "dp", "tensor"),
            P(None, "dp", "tensor"),
        ),
        check_vma=False,
    )
```

```python
import functools
import math

import jax
import jax.numpy as jnp
from jax import lax
from jax.experimental import pallas as pl
from jax.experimental.pallas import tpu as pltpu
from jax.sharding import PartitionSpec as P

EPSILON = 1e-05
F32 = jnp.float32
BF16 = jnp.bfloat16
NEVER = 1e4
LOG2E = 1.4426950408889634
GELU_SCALE = math.sqrt(2.0 / math.pi)
GELU_CUBE = 0.044715
VMEM_SPARE = 6 * 1024 * 1024
NEAR_GROUPS = 8
VECTORS_ONE = 24
VECTORS_TWO = 8
NORM_ROWS = 16


def run_kernel(
    kernel,
    outs,
    args,
    scratch=(),
    scalars=0,
    far_args=(),
    staged=(),
    far_outs=(),
    loose_outs=(),
    held_outs=(),
    alias=None,
):
    staged = tuple(staged)
    outside = {*far_args, *staged}

    def spec(index, far):
        return pl.BlockSpec(memory_space=pltpu.HBM if index in far else pltpu.VMEM)

    def held(index, shape, dtype):
        if index in loose_outs:
            return jax.ShapeDtypeStruct(shape, dtype)
        return (pltpu.VMEM if index in held_outs else pltpu.HBM)(shape, dtype)

    def body(*refs):
        refs = list(refs)
        if staged:
            *refs, semaphores = refs
            places = refs[len(refs) - len(staged) :]
            refs = refs[: len(refs) - len(staged)]
            copies = run_copies(list(zip([refs[index] for index in staged], places)), semaphores)
            for index, place in zip(staged, places):
                refs[index] = place
            for copy in copies:
                copy.wait()
        kernel(*refs)

    sizes = [(arg.shape, arg.dtype) for index, arg in enumerate(args) if index not in far_args]
    sizes += [out for index, out in enumerate(outs) if index not in far_outs]
    sizes += [shape for shape in scratch if isinstance(shape, tuple)]
    scratch = [pltpu.VMEM(*shape) if isinstance(shape, tuple) else shape for shape in scratch]
    if staged:
        scratch += [pltpu.VMEM(args[index].shape, args[index].dtype) for index in staged]
        scratch += [pltpu.SemaphoreType.DMA((len(staged),))]
    needed = sum(math.prod(shape) * jnp.dtype(dtype).itemsize for shape, dtype in sizes)
    return pl.pallas_call(
        body,
        out_shape=[held(index, shape, dtype) for index, (shape, dtype) in enumerate(outs)],
        in_specs=[
            pl.BlockSpec(memory_space=pltpu.SMEM) if index < scalars else spec(index, outside)
            for index in range(len(args))
        ],
        out_specs=[spec(index, far_outs) for index in range(len(outs))],
        scratch_shapes=scratch,
        input_output_aliases=alias or {},
        compiler_params=pltpu.CompilerParams(vmem_limit_bytes=VMEM_SPARE + needed * 5 // 4),
    )(
        *[
            pltpu.with_memory_space_constraint(arg, pltpu.HBM) if index in outside else arg
            for index, arg in enumerate(args)
        ]
    )


def dot_nn(left, right):
    return lax.dot_general(left, right, (((1,), (0,)), ((), ())), preferred_element_type=F32)


def dot_nt(left, right):
    return lax.dot_general(left, right, (((1,), (1,)), ((), ())), preferred_element_type=F32)


def dot_tn(left, right):
    return lax.dot_general(left, right, (((0,), (0,)), ((), ())), preferred_element_type=F32)


def lane_tiles(column, tiles):
    return jnp.concatenate([column] * tiles, axis=1)


def fold_tiles(values):
    total = values[:, :128]
    for tile in range(1, values.shape[1] // 128):
        total = total + values[:, 128 * tile : 128 * (tile + 1)]
    return total


def wide_masks(masks, index, chans):
    return lane_tiles(masks[index], -(-chans // 128))[:, :chans]


def rms_rate(values):
    return lax.rsqrt(jnp.mean(values * values, axis=-1, keepdims=True) + EPSILON)


def as_row(ref):
    return ref[...].reshape(1, ref.shape[0])


def softplus(values):
    return jnp.maximum(values, 0.0) + jnp.log1p(jnp.exp(-jnp.abs(values)))


def padded_copy(target, values):
    target[...] = jnp.zeros(target.shape, target.dtype)
    target[:, : values.shape[1]] = values


def put_row_chunks(place, source, outs):
    count = len(outs)
    rows = source.shape[0] // count
    for step, out in enumerate(outs):
        start = pl.multiple_of(lax.rem(place[0] + step, count) * rows, rows)
        out[pl.ds(0, rows), :] = source[pl.ds(start, rows), :].astype(out.dtype)


def take_row_pieces(place, pieces, target):
    count = len(pieces)
    rows = target.shape[0] // count
    for step, piece in enumerate(pieces):
        start = pl.multiple_of(lax.rem(place[0] - step + count, count) * rows, rows)
        target[pl.ds(start, rows), :] = piece[...].astype(target.dtype)


def sum_pieces(place, pieces, held):
    count = len(pieces)
    for step, piece in enumerate(pieces):
        held[lax.rem(place[0] - step + count, count)] = piece[...]
    total = held[0].astype(F32)
    for index in range(1, count):
        total = total + held[index].astype(F32)
    return total


def run_copies(copies, semaphores):
    started = []
    for index, (source, target) in enumerate(copies):
        copy = pltpu.make_async_copy(source, target, semaphores.at[index])
        copy.start()
        started.append(copy)
    return started


def fill_masks(resets, masks):
    length = resets.shape[1]
    square = (length, length)
    earlier = lax.broadcasted_iota(jnp.int32, square, 0)
    reset = jnp.broadcast_to(resets[...].astype(F32), square).T
    keep = jnp.where(reset == 0.0, 1.0, 0.0)
    joined = jnp.where(earlier > 0, keep, 0.0)
    one_back = pltpu.roll(joined, 1, 0)
    two_back = pltpu.roll(joined, 2, 0)
    masks[0] = keep
    masks[1] = joined
    masks[2] = joined * one_back
    masks[3] = joined * one_back * two_back


def fill_choose(capacity, block_rows, experts, routes, choose):
    length = routes.shape[1]
    square = (length, length)
    earlier = lax.broadcasted_iota(jnp.int32, square, 0)
    later = lax.broadcasted_iota(jnp.int32, square, 1)
    route_of = jnp.broadcast_to(routes[...].astype(F32), square)
    same = (route_of.T == route_of) & (earlier < later)
    if block_rows < length:
        same = same & (earlier // block_rows == later // block_rows)
    rank = jnp.sum(jnp.where(same, 1.0, 0.0), axis=0, keepdims=True).astype(jnp.int32)
    group = routes[...]
    if block_rows < length:
        group = group + experts * (later[:1] // block_rows)
    slot = group * capacity + rank
    slot_count = choose.shape[0]
    slot_ids = lax.broadcasted_iota(jnp.int32, (slot_count, length), 0)
    hit = slot_ids == jnp.broadcast_to(slot, (slot_count, length))
    choose[...] = jnp.where(hit, 1.0, 0.0).astype(BF16)


def prepare_kernel(
    experts, capacity, block_rows, resets, routes, cotangent, masks, choose, slots
):
    fill_masks(resets, masks)
    fill_choose(capacity, block_rows, experts, routes, choose)
    slots[...] = dot_nn(choose[...], cotangent[...]).astype(BF16)


def put_folded(target, slots):
    rows, width = slots.shape
    units = target.shape[1]
    half = rows // 2
    rest = width - units
    target[:rows, :] = slots[:, :units]
    target[rows:, :rest] = slots[:half, units:]
    target[rows:, rest:] = slots[half:, units:]


def unfold_copies(source, target, top, rows):
    units = source.shape[1]
    half = rows // 2
    rest = target.shape[1] - units
    copies = [(source.at[pl.ds(0, rows)], target.at[pl.ds(top, rows), pl.ds(0, units)])]
    for part in range(2):
        copies.append(
            (
                source.at[pl.ds(rows, half), pl.ds(part * rest, rest)],
                target.at[pl.ds(top + part * half, half), pl.ds(units, rest)],
            )
        )
    return copies


def pack_kernel(
    capacity,
    resets_in,
    routes_in,
    cotangent_in,
    expert_in,
    expert_out,
    masks,
    choose,
    message,
    packed,
    staged,
    resets,
    routes,
    cotangent,
    early_arrivals,
    arrivals,
    semaphores,
):
    experts, share, units = expert_in.shape
    length, width = cotangent.shape
    copies = []
    for index in range(experts):
        copies.append((expert_in.at[index], staged.at[index, 0]))
        copies.append((expert_out.at[index], staged.at[index, 1]))
    early = run_copies(
        [(resets_in, resets), (routes_in, routes), (cotangent_in, cotangent)], early_arrivals
    )
    arriving = run_copies(copies, arrivals)
    for copy in early:
        copy.wait()
    fill_choose(capacity, length, experts, routes, choose)
    slots = dot_nn(choose[...], cotangent[...]).astype(BF16)
    started = []
    for index in range(experts):
        copies = []
        for which in range(2):
            arriving[2 * index + which].wait()
            target = message.at[index, pl.ds(which * share, share)]
            copies.append((staged.at[index, which], target))
        started += run_copies(copies, semaphores.at[pl.ds(2 * index, 2)])
    copies = []
    for index in range(experts):
        put_folded(packed.at[index], slots[index * capacity : (index + 1) * capacity])
        target = message.at[index]
        copies.append((packed.at[index], target.at[pl.ds(2 * share, packed.shape[1])]))
    started += run_copies(copies, semaphores.at[pl.ds(2 * experts, experts)])
    fill_masks(resets, masks)
    for copy in started:
        copy.wait()


def pass_on(along_x, along_y, pass_y, pass_x, passed, arrivals, semaphores):
    half = passed.shape[1]
    copies = [
        (along_y.at[pl.ds(0, half)], passed.at[0]),
        (along_x.at[pl.ds(half, half)], passed.at[1]),
    ]
    for copy in run_copies(copies, arrivals):
        copy.wait()
    return run_copies([(passed.at[0], pass_y), (passed.at[1], pass_x)], semaphores)


def pass_kernel(along_x, along_y, pass_y, pass_x, passed, arrivals, semaphores):
    for copy in pass_on(along_x, along_y, pass_y, pass_x, passed, arrivals, semaphores):
        copy.wait()


def unpack_kernel(
    share,
    capacity,
    message,
    first_out,
    second_out,
    slots_out,
    d_hidden,
    first_w,
    second_w,
    grad_slots,
    semaphores,
):
    folded = capacity + capacity // 2
    copies = []
    for index in range(message.shape[0]):
        piece = message.at[index]
        rows = pl.ds(index * share, share)
        copies.append((piece.at[pl.ds(share, share)], second_w.at[rows]))
        copies += unfold_copies(
            piece.at[pl.ds(2 * share, folded)], grad_slots, index * capacity, capacity
        )
        copies.append((piece.at[pl.ds(0, share)], first_w.at[rows]))
    for copy in run_copies(copies, semaphores):
        copy.wait()
    copies = [(first_w, first_out), (second_w, second_out), (grad_slots, slots_out)]
    started = run_copies(copies, semaphores)
    d_hidden[...] = dot_nn(grad_slots[...], second_w[...])
    for copy in started:
        copy.wait()


def put_blocks(target, values):
    length = values.shape[0]
    for start in range(0, values.shape[1], 128):
        target[start : start + length, :] = values[:, start : start + 128]


def enter_kernel(
    place,
    piece_0,
    piece_1,
    piece_2,
    piece_3,
    gain_ref,
    in_proj,
    conv_weight,
    conv_bias,
    x_proj,
    masks,
    rows_out,
    normed_out,
    act_out,
    inner_out,
    conv_out,
    gate_out,
    scale_out,
    gain_out,
    mixed_out,
    turned,
):
    take_row_pieces(place, (piece_0, piece_1, piece_2, piece_3), turned)
    rows = turned[...].T
    gain = as_row(gain_ref)
    rows_out[...] = rows.astype(BF16)
    normed = (rows * rms_rate(rows) * gain).astype(BF16)
    put_blocks(normed_out, normed)
    inner = dot_nt(normed, in_proj[0])
    chans = inner.shape[1]
    inner_out[...] = inner
    total = as_row(conv_bias) + conv_weight[3:4, :] * inner
    for shift in (1, 2, 3):
        moved = pltpu.roll(inner, shift, 0) * wide_masks(masks, shift, chans)
        total = total + conv_weight[3 - shift : 4 - shift, :] * moved
    conv_out[...] = total
    act = (total * jax.nn.sigmoid(total)).astype(BF16)
    act_out[...] = act
    mixed_out[...] = dot_nt(x_proj[...], act).astype(BF16)
    gate_out[...] = dot_nt(normed, in_proj[1])
    raw = turned[...]
    scale_out[...] = lax.rsqrt(jnp.mean(raw * raw, axis=0, keepdims=True) + EPSILON)
    turned[...] = jnp.broadcast_to(gain, rows.shape).T
    column = gain_out.shape[0]
    gain_out[...] = turned[pl.ds(pl.multiple_of(place[0] * column, column), column), :]


def block_columns(transposed, block):
    length = transposed.shape[1]
    return pltpu.roll(transposed, lax.rem(length - 8 * block, length), 1)


def spread_column(columns, row, tiles):
    return lane_tiles(jnp.broadcast_to(columns[:, row : row + 1], (columns.shape[0], 128)), tiles)


def scan_forward_kernel(
    place,
    piece_0,
    piece_1,
    piece_2,
    piece_3,
    dt_proj,
    dt_bias,
    decay_log,
    skip_gain,
    act_in,
    gate_in,
    masks,
    out_proj,
    normed,
    out_0,
    out_1,
    out_2,
    out_3,
    mixed_out,
    share_out,
    y_out,
    held,
    rate,
    step_rows,
    drive_rows,
    y_rows,
    partial,
):
    rank = dt_proj.shape[0]
    states = decay_log.shape[0]
    length, chans = y_out.shape
    tiles = step_rows.shape[1] // 128
    mixed = sum_pieces(place, (piece_0, piece_1, piece_2, piece_3), held)
    mixed_out[...] = mixed
    step_size = softplus(dot_tn(mixed[:rank].astype(BF16), dt_proj[...]) + as_row(dt_bias))
    act = act_in[...].astype(F32)
    reset = NEVER * (1.0 - wide_masks(masks, 0, chans))
    padded_copy(rate, -LOG2E * jnp.exp(decay_log[...]))
    padded_copy(step_rows, step_size + reset)
    padded_copy(drive_rows, step_size * act)
    b_turned = mixed[rank : rank + states]
    c_turned = mixed[rank + states : rank + 2 * states]

    def block(index, state):
        start = pl.multiple_of(index * 8, 8)
        b_cols = block_columns(b_turned, index)
        c_cols = block_columns(c_turned, index)
        steps = step_rows[pl.ds(start, 8), :]
        drives = drive_rows[pl.ds(start, 8), :]
        rows = []
        for row in range(8):
            decay = jnp.exp2(rate[...] * steps[row : row + 1])
            state = decay * state + spread_column(b_cols, row, tiles) * drives[row : row + 1]
            rows.append(
                jnp.sum(spread_column(c_cols, row, tiles) * state, axis=0, keepdims=True)
            )
        y_rows[pl.ds(start, 8), :] = jnp.concatenate(rows, axis=0)
        return state

    lax.fori_loop(0, length // 8, block, jnp.zeros((states, 128 * tiles), F32))
    y = y_rows[:, :chans] + as_row(skip_gain) * act
    y_out[...] = y
    gate = gate_in[...]
    gated = (y * (gate * jax.nn.sigmoid(gate))).astype(BF16)
    partial[...] = dot_nn(gated, out_proj[...])
    put_row_chunks(place, partial, (out_0, out_1, out_2, out_3))
    width = normed.shape[0]
    share_out[:width] = normed[...]
    padded_copy(step_rows, gated.astype(F32))
    share_out[width : width + chans] = step_rows[...].T[:chans].astype(BF16)
    padded_copy(step_rows, act)
    share_out[width + chans :] = step_rows[...].T[:chans].astype(BF16)


def dispatch_kernel(
    place,
    piece_0,
    piece_1,
    piece_2,
    piece_3,
    rows_in,
    gain,
    choose,
    residual_out,
    columns_out,
    slots,
    turned,
):
    take_row_pieces(place, (piece_0, piece_1, piece_2, piece_3), residual_out)
    residual = rows_in[...].astype(F32) + residual_out[...]
    residual_out[...] = residual
    send = (residual * rms_rate(residual) * as_row(gain)).astype(BF16)
    slots[...] = dot_nn(choose[...], send).astype(BF16)
    turned[...] = residual.T
    column = columns_out.shape[0]
    columns_out[...] = turned[pl.ds(pl.multiple_of(place[0] * column, column), column), :]


def hidden_back_kernel(grad_slots, second_w, d_hidden):
    d_hidden[...] = dot_nn(grad_slots[...], second_w[...])


def expert_kernel(arrived, first_w, d_hidden, hidden_out, d_pre_out, d_slots):
    value = dot_nn(arrived[...], first_w[...])
    square = value * value
    bend = jnp.tanh(GELU_SCALE * (value + GELU_CUBE * value * square))
    half = 0.5 * (1.0 + bend)
    slope = half + 0.5 * value * (1.0 - bend * bend) * GELU_SCALE * (
        1.0 + 3.0 * GELU_CUBE * square
    )
    d_pre = (slope * d_hidden[...]).astype(BF16)
    d_pre_out[...] = d_pre
    d_slots[...] = dot_nt(d_pre, first_w[...]).astype(BF16)
    hidden_out[...] = (value * half).astype(BF16)


def expert_grads_kernel(arrived, grad_slots, hidden, d_pre, second_w, first_out, second_out, moe):
    first_out[...] = dot_tn(arrived[...], d_pre[...]).astype(BF16)
    second_out[...] = dot_tn(grad_slots[...], hidden[...]).astype(BF16)
    moe[...] = dot_nt(hidden[...], second_w[...]).astype(BF16)


def expert_grads_pack_kernel(
    share, capacity, arrived, grad_slots, hidden, d_pre, second_w, message, grads, packed, semaphores
):
    experts = message.shape[0]
    started = []
    for which, (left, right) in enumerate(((arrived, d_pre), (grad_slots, hidden))):
        grads[which] = dot_tn(left[...], right[...]).astype(BF16)
        copies = [
            (
                grads.at[which, pl.ds(index * share, share)],
                message.at[index, pl.ds(which * share, share)],
            )
            for index in range(experts)
        ]
        started += run_copies(copies, semaphores.at[pl.ds(which * experts, experts)])
    moe = dot_nt(hidden[...], second_w[...]).astype(BF16)
    copies = []
    for index in range(experts):
        put_folded(packed.at[index], moe[index * capacity : (index + 1) * capacity])
        copies.append(
            (packed.at[index], message.at[index, pl.ds(2 * share, packed.shape[1])])
        )
    started += run_copies(copies, semaphores.at[pl.ds(2 * experts, experts)])
    for copy in started:
        copy.wait()


def owner_kernel(share, message, first_out, second_out, low, wide, arrivals, semaphores):
    count = message.shape[0]
    arriving = run_copies(
        [(message.at[index, pl.ds(0, 2 * share)], low.at[index]) for index in range(count)],
        arrivals,
    )
    started = []
    for index in range(count):
        arriving[index].wait()
        wide[index] = low[index].astype(F32)
        copies = [
            (wide.at[index, pl.ds(0, share)], first_out.at[index]),
            (wide.at[index, pl.ds(share, share)], second_out.at[index]),
        ]
        started += run_copies(copies, semaphores.at[pl.ds(2 * index, 2)])
    for copy in started:
        copy.wait()


def back_rows_kernel(place, choose, slots, out_0, out_1, out_2, out_3, partial):
    partial[...] = dot_tn(choose[...], slots[...])
    put_row_chunks(place, partial, (out_0, out_1, out_2, out_3))


def back_columns_kernel(place, choose, shares, slots, out_0, out_1, out_2, out_3, rows):
    rows[...] = dot_tn(slots[...], choose[...]).astype(BF16)
    outs = (out_0, out_1, out_2, out_3)
    count, top, _ = shares.shape
    column = rows.shape[0] // count
    for step, out in enumerate(outs):
        whose = lax.rem(place[0] + step, count)
        out[:top, :] = shares[whose]
        out[top:, :] = rows[pl.ds(pl.multiple_of(whose * column, column), column), :]


def back_folded_kernel(
    share,
    place,
    choose,
    shares,
    message,
    refs,
    out_0,
    out_1,
    out_2,
    out_3,
    weight_grad,
    bias_grad,
    slots,
    rows,
    staged,
    semaphores,
):
    count = message.shape[0]
    capacity = slots.shape[0] // count
    folded = message.shape[1] - 2 * share
    copies = []
    for index in range(count):
        copies += unfold_copies(
            message.at[index, pl.ds(2 * share, folded)], slots, index * capacity, capacity
        )
    deep = 2 * VECTORS_TWO
    height = staged.shape[1]
    top = refs[0].shape[0] - height
    copies += [(ref.at[pl.ds(top, height)], staged.at[index]) for index, ref in enumerate(refs)]
    for copy in run_copies(copies, semaphores):
        copy.wait()
    total = staged[0].astype(F32)
    for index in range(1, staged.shape[0]):
        total = total + staged[index].astype(F32)
    chans = weight_grad.shape[1]
    vectors = jnp.concatenate(
        [total[start : start + deep] for start in range(0, height, deep)], axis=1
    )[:, :chans]
    vectors = vectors[:VECTORS_TWO] + vectors[VECTORS_TWO:]
    weight_grad[...] = vectors[:4]
    bias_grad[...] = vectors[4].reshape(chans)
    norm_grad = jnp.concatenate([vectors[5:6], vectors[6:7]], axis=1)
    norm_rows = [norm_grad[:, start : start + 128] for start in range(0, norm_grad.shape[1], 128)]
    spare = jnp.zeros((NORM_ROWS - len(norm_rows), 128), F32)
    upper, lower = split_vectors(jnp.concatenate([*norm_rows, spare], axis=0))
    norm_low = jnp.concatenate([upper, lower], axis=0).astype(BF16)
    outs = (out_0, out_1, out_2, out_3)
    plain = out_0.shape[0] - 2 * NORM_ROWS
    back_columns_kernel(
        place, choose, shares, slots, *[out.at[pl.ds(0, plain)] for out in outs], rows
    )
    for out in outs:
        out[plain:, :] = norm_low


def mixer_grad_kernel(
    place,
    piece_0,
    piece_1,
    piece_2,
    piece_3,
    residual_in,
    gain_ref,
    cotangent,
    out_proj,
    columns_out,
    mix_out,
    d_gated,
    gain_grad,
    d_send,
    turned,
):
    take_row_pieces(place, (piece_0, piece_1, piece_2, piece_3), d_send)
    residual = residual_in[...]
    inverse = rms_rate(residual)
    scaled = residual * inverse
    grad = d_send[...]
    pulled = grad * as_row(gain_ref)
    along = jnp.mean(pulled * scaled, axis=-1, keepdims=True)
    d_residual = cotangent[...].astype(F32) + inverse * (pulled - scaled * along)
    d_mix = d_residual.astype(BF16)
    put_blocks(mix_out, d_mix)
    d_gated[...] = dot_nt(d_mix, out_proj[...])
    gain_grad[...] = jnp.sum(grad * scaled, axis=0, keepdims=True)
    turned[...] = d_residual.T
    column = columns_out.shape[0]
    columns_out[...] = turned[pl.ds(pl.multiple_of(place[0] * column, column), column), :]


def split_vectors(vectors):
    upper = vectors.astype(BF16).astype(F32)
    return upper, vectors - upper


def scan_states_kernel(
    y_in,
    gate_in,
    act_in,
    mixed_in,
    masks,
    dt_proj,
    dt_bias,
    decay_log,
    decays,
    history,
    step_rows,
    drive_rows,
    step_slope,
    y_slope,
    gate_slope,
    rate,
    decay_rows,
):
    rank = dt_proj.shape[0]
    states = decay_log.shape[0]
    length, chans = y_in.shape
    tiles = step_rows.shape[1] // 128
    full = 128 * tiles
    mixed = mixed_in[...]
    raw_step = dot_tn(mixed[:rank].astype(BF16), dt_proj[...]) + as_row(dt_bias)
    step_size = softplus(raw_step)
    step_slope[...] = jax.nn.sigmoid(raw_step)
    reset = NEVER * (1.0 - wide_masks(masks, 0, chans))
    padded_copy(rate, -LOG2E * jnp.exp(decay_log[...]))
    padded_copy(step_rows, step_size)
    padded_copy(decay_rows, step_size + reset)
    padded_copy(drive_rows, step_size * act_in[...].astype(F32))
    gate = gate_in[...]
    gate_sig = jax.nn.sigmoid(gate)
    y_slope[...] = gate * gate_sig
    gate_slope[...] = y_in[...] * gate_sig * (1.0 + gate * (1.0 - gate_sig))
    b_turned = mixed[rank : rank + states]
    history[pl.ds(0, states), :] = jnp.zeros((states, full), F32)

    def forward_block(index, state):
        start = pl.multiple_of(index * 8, 8)
        b_cols = block_columns(b_turned, index)
        steps = decay_rows[pl.ds(start, 8), :]
        drives = drive_rows[pl.ds(start, 8), :]
        for row in range(8):
            decay = jnp.exp2(rate[...] * steps[row : row + 1])
            state = decay * state + spread_column(b_cols, row, tiles) * drives[row : row + 1]
            at = pl.multiple_of((start + row) * states, states)
            decays[pl.ds(at, states), :] = decay
            history[pl.ds(at + states, states), :] = state
        return state

    lax.fori_loop(0, length // 8, forward_block, jnp.zeros((states, full), F32))


def scan_backward_kernel(
    d_gated,
    y_slope,
    gate_slope,
    act_in,
    mixed_in,
    dt_proj,
    decay_log,
    skip_gain,
    gain_grad,
    d_mix,
    decays,
    history,
    step_rows,
    drive_rows,
    step_slope,
    d_mixed_out,
    d_act_out,
    d_gate_out,
    share_out,
    rate,
    dy_rows,
    du_rows,
    dl_rows,
):
    rank = dt_proj.shape[0]
    states = decay_log.shape[0]
    length, chans = y_slope.shape
    tiles = step_rows.shape[1] // 128
    full = 128 * tiles
    mixed = mixed_in[...]
    dt_low = mixed[:rank].astype(BF16)
    act = act_in[...].astype(F32)
    padded_copy(rate, -jnp.exp(decay_log[...]))
    d_out = d_gated[...]
    d_y = d_out * y_slope[...]
    padded_copy(dy_rows, d_y)
    d_gate = d_out * gate_slope[...]
    b_turned = mixed[rank : rank + states]
    c_turned = mixed[rank + states : rank + 2 * states]
    lanes = lax.broadcasted_iota(jnp.int32, (states, length), 1)

    def backward_block(count, carry):
        carried, d_rate, d_b, d_c = carry
        index = length // 8 - 1 - count
        start = pl.multiple_of(index * 8, 8)
        b_cols = block_columns(b_turned, index)
        c_cols = block_columns(c_turned, index)
        steps = step_rows[pl.ds(start, 8), :]
        drives = drive_rows[pl.ds(start, 8), :]
        dys = dy_rows[pl.ds(start, 8), :]
        du = [None] * 8
        dl = [None] * 8
        for row in reversed(range(8)):
            at = pl.multiple_of((start + row) * states, states)
            before = history[pl.ds(at, states), :]
            after = history[pl.ds(at + states, states), :]
            decay = decays[pl.ds(at, states), :]
            here = lanes == start + row
            dy_row = jnp.broadcast_to(dys[row : row + 1], (states, full))
            grad = spread_column(c_cols, row, tiles) * dy_row + carried
            c_part = jnp.sum(fold_tiles(dy_row * after), axis=1, keepdims=True)
            d_c = jnp.where(here, c_part, d_c)
            b_part = jnp.sum(fold_tiles(grad * drives[row : row + 1]), axis=1, keepdims=True)
            d_b = jnp.where(here, b_part, d_b)
            du[row] = jnp.sum(grad * spread_column(b_cols, row, tiles), axis=0, keepdims=True)
            carried = grad * decay
            d_log = carried * before
            dl[row] = jnp.sum(d_log * rate[...], axis=0, keepdims=True)
            d_rate = d_rate + d_log * steps[row : row + 1]
        du_rows[pl.ds(start, 8), :] = jnp.concatenate(du, axis=0)
        dl_rows[pl.ds(start, 8), :] = jnp.concatenate(dl, axis=0)
        return carried, d_rate, d_b, d_c

    nothing = jnp.zeros((states, full), F32)
    thin = jnp.zeros((states, length), F32)
    _, d_rate, d_b, d_c = lax.fori_loop(
        0, length // 8, backward_block, (nothing, nothing, thin, thin)
    )
    du = du_rows[:, :chans]
    d_step = (dl_rows[:, :chans] + du * act) * step_slope[...]
    d_step_low = d_step.astype(BF16)
    low_turned = dot_nt(dt_proj[...], d_step_low)
    d_mixed_out[...] = jnp.concatenate([low_turned, d_b, d_c], axis=0).astype(BF16)
    d_act_out[...] = du * step_rows[:, :chans] + as_row(skip_gain) * d_y
    d_gate_low = d_gate.astype(BF16)
    d_gate_out[...] = d_gate_low
    width = d_mix.shape[0]
    share_out[:width] = d_mix[...]
    padded_copy(du_rows, d_gate_low.astype(F32))
    share_out[width : width + chans] = du_rows[...].T[:chans].astype(BF16)
    gain_rows = gain_grad[...]
    upper, lower = split_vectors(
        jnp.concatenate(
            [
                (d_rate * rate[...])[:, :chans],
                jnp.sum(d_step, axis=0, keepdims=True),
                jnp.sum(d_y * act, axis=0, keepdims=True),
                gain_rows[:, :chans],
                gain_rows[:, chans:],
                jnp.zeros((VECTORS_ONE - states - 4, chans), F32),
            ],
            axis=0,
        )
    )
    dl_rows[...] = jnp.zeros(dl_rows.shape, F32)
    dl_rows[:rank, :chans] = dot_nn(dt_low, d_step_low)
    dl_rows[rank : rank + VECTORS_ONE, :chans] = upper
    dl_rows[rank + VECTORS_ONE : rank + 2 * VECTORS_ONE, :chans] = lower
    share_out[width + chans :] = dl_rows[...].T[:chans].astype(BF16)


def leave_kernel(
    place,
    piece_0,
    piece_1,
    piece_2,
    piece_3,
    d_act_scan,
    d_gate,
    conv_in,
    inner_in,
    masks,
    x_proj,
    conv_weight,
    in_proj,
    rows_in,
    gain,
    shares,
    message,
    held,
    turned,
    padded,
):
    length, chans = inner_in.shape
    width = rows_in.shape[1]
    full = padded.shape[1]
    d_mixed = sum_pieces(place, (piece_0, piece_1, piece_2, piece_3), held).astype(BF16)
    d_act = d_act_scan[...] + dot_tn(d_mixed, x_proj[...])
    conv = conv_in[...]
    sig = jax.nn.sigmoid(conv)
    d_conv = d_act * sig * (1.0 + conv * (1.0 - sig))
    inner = inner_in[...]
    d_inner = conv_weight[3:4, :] * d_conv
    weight_grads = [jnp.sum(d_conv * inner, axis=0, keepdims=True)]
    for shift in (1, 2, 3):
        masked = d_conv * wide_masks(masks, shift, chans)
        weight_grads.append(
            jnp.sum(masked * pltpu.roll(inner, shift, 0), axis=0, keepdims=True)
        )
        d_inner = d_inner + conv_weight[3 - shift : 4 - shift, :] * pltpu.roll(
            masked, length - shift, 0
        )
    d_inner_low = d_inner.astype(BF16)
    padded_copy(padded, d_inner_low.astype(F32))
    message[:chans] = padded[...].T[:chans].astype(BF16)
    proj = d_mixed.shape[0]
    top = message.shape[0] - full // 128 * 2 * VECTORS_TWO
    message[chans:top] = jnp.concatenate(
        [d_mixed.astype(F32), jnp.zeros((top - chans - proj, length), F32)], axis=0
    ).astype(BF16)
    d_normed = dot_nn(d_inner_low, in_proj[0]) + dot_nn(d_gate[...], in_proj[1])
    rows = rows_in[...].astype(F32)
    scaled = rows * rms_rate(rows)
    norm_grad = jnp.sum(d_normed * scaled, axis=0, keepdims=True)
    upper, lower = split_vectors(
        jnp.concatenate(
            [
                weight_grads[3],
                weight_grads[2],
                weight_grads[1],
                weight_grads[0],
                jnp.sum(d_conv, axis=0, keepdims=True),
                norm_grad[:, :chans],
                norm_grad[:, chans:],
                jnp.zeros((VECTORS_TWO - 7, chans), F32),
            ],
            axis=0,
        )
    )
    padded_copy(padded, jnp.zeros((length, chans), F32))
    padded[:VECTORS_TWO, :chans] = upper
    padded[VECTORS_TWO : 2 * VECTORS_TWO, :chans] = lower
    for tile in range(full // 128):
        message[top + tile * 2 * VECTORS_TWO : top + (tile + 1) * 2 * VECTORS_TWO] = padded[
            : 2 * VECTORS_TWO, tile * 128 : (tile + 1) * 128
        ].astype(BF16)
    along = jnp.mean(d_normed * as_row(gain) * scaled, axis=-1, keepdims=True)
    along = jnp.broadcast_to(along, (length, length)).T[:8]
    high = along.astype(BF16)
    low = (along - high.astype(F32)).astype(BF16)
    turned[...] = d_normed.T
    count, rows, _ = shares.shape
    column = width // count
    ends = jnp.concatenate([high, low], axis=0)
    for index in range(count):
        shares[index, :column, :] = turned[index * column : (index + 1) * column].astype(BF16)
        shares[index, column:, :] = ends


def finish_rows_kernel(
    piece_0,
    piece_1,
    piece_2,
    piece_3,
    residual,
    d_columns,
    tokens,
    scale,
    gain,
    outcome,
    grad_tokens,
    *norm_out,
):
    column = tokens.shape[0]
    total = piece_0[...].astype(F32)
    for piece in (piece_1, piece_2, piece_3):
        total = total + piece[...].astype(F32)
    along = total[column : column + 1] + total[column + 8 : column + 9]
    inverse = scale[...]
    pulled = total[:column] * gain[...]
    scaled = tokens[...].astype(F32) * inverse
    grad_tokens[...] = d_columns[...] + inverse * (pulled - scaled * along)
    plain = 2 * column + 16
    outcome[...] = (residual[...] + total[column + 16 : plain]).astype(BF16)
    for out in norm_out:
        norm = total[plain : plain + NORM_ROWS] + total[plain + NORM_ROWS :]
        width = out.shape[0]
        out[...] = jnp.concatenate(
            [norm[row : row + 1] for row in range(width // 128)], axis=1
        ).reshape(width)


def take_blocks(target, pieces):
    for index, piece in enumerate(pieces):
        for start in range(0, target.shape[1], 128):
            target[index * 128 : (index + 1) * 128, start : start + 128] = piece[
                start : start + 128
            ]


def take_turned(target, pieces, start):
    rows = target.shape[0]
    for index, piece in enumerate(pieces):
        target[:, index * 128 : (index + 1) * 128] = piece[start : start + rows]


def stage_pieces(refs, staged, semaphores, rows=None):
    copies = []
    parts = len(refs) // 2
    for index, ref in enumerate(refs):
        side, part = divmod(index, parts)
        target = staged.at[4 * side + min(part, 3)]
        if part >= 3 and parts > 4:
            height = staged.shape[1] // (parts - 3)
            target = target.at[pl.ds((part - 3) * height, height)]
        copies.append((ref if rows is None else ref.at[pl.ds(*rows)], target))
    return run_copies(copies, semaphores), [staged.at[index] for index in range(8)]


def first_sets_kernel(refs, normed, gated, acts, staged, semaphores):
    chans = gated.shape[0]
    width = normed.shape[1]
    arriving, firsts = stage_pieces(refs, staged, semaphores)
    for copy in arriving:
        copy.wait()
    take_blocks(normed, firsts)
    take_turned(gated, firsts, width)
    take_turned(acts, firsts, width + chans)


def wide_grads_kernel(
    sizes,
    second_refs,
    last_refs,
    normed,
    gated,
    acts,
    out_grad,
    in_grad,
    x_grad,
    dt_grad,
    bias_grad,
    decay_grad,
    skip_grad,
    norm_grad,
    staged,
    staged_last,
    mixed,
    d_gate,
    d_mixed,
    total,
    wide_grad,
    second_arrivals,
    last_arrivals,
    semaphores,
):
    rank, states, proj = sizes
    chans, width = out_grad.shape
    arriving_last, lasts = stage_pieces(last_refs, staged_last, last_arrivals)
    for copy in arriving_last:
        copy.wait()
    arriving, seconds = stage_pieces(second_refs, staged, second_arrivals)
    take_turned(d_gate, lasts, 0)
    wide_grad[0] = dot_nn(d_gate[...], normed[...])
    started = run_copies([(wide_grad.at[0], in_grad.at[0])], semaphores)
    for copy in arriving:
        copy.wait()
    take_turned(d_gate, seconds, width)
    wide_grad[1] = dot_nn(d_gate[...], normed[...])
    started += run_copies([(wide_grad.at[1], in_grad.at[1])], semaphores.at[pl.ds(1, 1)])
    take_blocks(mixed, seconds)
    half = chans // 2
    for index in range(2):
        rows = pl.ds(index * half, half)
        wide_grad[2, rows] = dot_nn(gated[rows], mixed[...])
        started += run_copies(
            [(wide_grad.at[2, rows], out_grad.at[rows])], semaphores.at[pl.ds(2 + index, 1)]
        )
    take_turned(d_mixed, lasts, chans)
    x_grad[...] = dot_nt(d_mixed[...], acts[...])[:proj]
    vectors = seconds[0][width + chans :].astype(F32)
    for piece in seconds[1:]:
        vectors = vectors + piece[width + chans :].astype(F32)
    total[...] = jnp.zeros(total.shape, F32)
    total[:chans] = vectors
    rows = total[...].T[:, :chans]
    dt_grad[...] = rows[:rank]
    rows = rows[rank : rank + VECTORS_ONE] + rows[rank + VECTORS_ONE : rank + 2 * VECTORS_ONE]
    decay_grad[...] = rows[:states]
    bias_grad[...] = rows[states].reshape(chans)
    skip_grad[...] = rows[states + 1].reshape(chans)
    norm_grad[...] = jnp.concatenate(
        [rows[states + 2 : states + 3], rows[states + 3 : states + 4]], axis=1
    ).reshape(width)
    for copy in started:
        copy.wait()


def send_chunks(chunks):
    count = len(chunks)
    pairs = [[(i, (i + s) % count) for i in range(count)] for s in range(count)]
    return [chunks[0]] + [lax.ppermute(chunks[s], "tensor", pairs[s]) for s in range(1, count)]


def share_rows(values, count):
    return send_chunks([values] * count)


def add_low(pieces):
    total = pieces[0].astype(F32)
    for piece in pieces[1:]:
        total = total + piece.astype(F32)
    return total.astype(BF16)


def after(values, *events):
    return list(lax.optimization_barrier((tuple(values), events))[0])


def swap(values, bits):
    return lax.ppermute(values, "dp", [(i, i ^ bits) for i in range(NEAR_GROUPS)])


def swap_across(halves):
    return [swap(halves[0], 2), swap(halves[1], 4)]


def swap_near(values):
    return [*values, *[swap(part, 1) for part in values]]


def body(
    tokens,
    resets,
    routes,
    norm_one,
    in_proj,
    conv_weight,
    conv_bias,
    x_proj,
    dt_proj,
    dt_bias,
    decay_log,
    skip_gain,
    out_proj,
    norm_two,
    expert_in,
    expert_out,
    cotangent,
):
    groups = lax.axis_size("dp")
    parts = lax.axis_size("tensor")
    place = lax.axis_index("tensor").astype(jnp.int32).reshape(1)
    length, column = tokens.shape
    width = norm_one.shape[0]
    rank, chans = dt_proj.shape
    states = decay_log.shape[0]
    experts, share, hidden_units = expert_in.shape
    proj = x_proj.shape[1]
    tile_count = groups // experts
    block_rows = length * experts // groups
    capacity = max(2, block_rows // 4)
    slot_count = groups * capacity
    tiles = -(-chans // 128)
    full = 128 * tiles
    near = groups == NEAR_GROUPS and experts == groups
    tokens_turned = tokens.T
    in_turned = jnp.swapaxes(in_proj, 1, 2)
    x_turned = x_proj.T
    resets_row = resets.reshape(1, length)
    routes_row = routes.reshape(1, length)

    def exchange(values):
        return lax.all_to_all(values, "dp", split_axis=0, concat_axis=0, tiled=True)

    def exchange_slots(slots):
        return exchange(slots.reshape(groups, capacity, width)).reshape(slot_count, width)

    half_out = (((width + 2 * chans) // 2, length), BF16)

    def pass_halves(along_x, along_y):
        return run_kernel(
            pass_kernel,
            [half_out, half_out],
            [along_x, along_y],
            [
                ((2, *half_out[0]), BF16),
                pltpu.SemaphoreType.DMA((2,)),
                pltpu.SemaphoreType.DMA((2,)),
            ],
            far_args=(0, 1),
            far_outs=(0, 1),
        )

    token_pieces = share_rows(tokens_turned, parts)
    mask_out = ((4, length, 128), F32)
    choose_out = ((slot_count, length), BF16)
    weight_outs = [((width, hidden_units), BF16)] * 2
    slots_out = ((slot_count, width), BF16)
    hidden_out = ((slot_count, hidden_units), BF16)
    folded = capacity + capacity // 2
    message_out = ((groups, 2 * share + folded, hidden_units), BF16)
    if near:
        masks, choose, packed = run_kernel(
            functools.partial(pack_kernel, capacity),
            [mask_out, choose_out, message_out],
            [resets_row, routes_row, cotangent, expert_in, expert_out],
            [
                ((groups, folded, hidden_units), BF16),
                ((experts, 2, share, hidden_units), BF16),
                ((1, length), jnp.int32),
                ((1, length), jnp.int32),
                ((length, width), BF16),
                pltpu.SemaphoreType.DMA((3,)),
                pltpu.SemaphoreType.DMA((2 * experts,)),
                pltpu.SemaphoreType.DMA((3 * experts,)),
            ],
            far_args=range(5),
            far_outs=(2,), )
        weights = exchange(packed)
    else:
        masks, choose, grad_send = run_kernel(
            functools.partial(prepare_kernel, experts, capacity, block_rows),
            [mask_out, choose_out, slots_out],
            [resets_row, routes_row, cotangent], loose_outs=(2,))
        first_w = exchange(jnp.tile(expert_in, (tile_count, 1, 1))).reshape(weight_outs[0][0])
        second_w = exchange(jnp.tile(expert_out, (tile_count, 1, 1))).reshape(weight_outs[0][0])
        grad_slots = exchange_slots(grad_send)
        (d_hidden,) = run_kernel(
            hidden_back_kernel, [((slot_count, hidden_units), F32)], [grad_slots, second_w]
        )

    rows, normed, act, inner, conv, gate, scale, gain_columns, mixed_part = run_kernel(
        enter_kernel,
        [
            ((length, width), BF16),
            ((width, length), BF16),
            ((length, chans), BF16),
            ((length, chans), F32),
            ((length, chans), F32),
            ((length, chans), F32),
            ((1, length), F32),
            ((column, length), F32),
            ((proj, length), BF16),
        ],
        [place, *token_pieces, norm_one, in_turned, conv_weight, conv_bias, x_turned, masks],
        [((width, length), F32)],
        scalars=1, loose_outs=(8,), staged=(1, 2, 3, 4, 10))
    mixed_pieces = share_rows(mixed_part, parts)
    *mix_chunks, mixed, first, y = run_kernel(
        scan_forward_kernel,
        [((length // parts, width), BF16)] * parts
        + [
            ((proj, length), F32),
            ((width + 2 * chans, length), BF16),
            ((length, chans), F32),
        ],
        [
            place,
            *mixed_pieces,
            dt_proj,
            dt_bias,
            decay_log,
            skip_gain,
            act,
            gate,
            masks,
            out_proj,
            normed,
        ],
        [
            ((parts, proj, length), BF16),
            ((states, full), F32),
            ((length, full), F32),
            ((length, full), F32),
            ((length, full), F32),
            ((length, width), F32),
        ],
        scalars=1, loose_outs=(0, 1, 2, 3, 5), staged=(1, 2, 3, 4, 9, 10, 11, 13))
    mixer_pieces = share_rows(add_low(send_chunks(mix_chunks)), parts)
    if near:
        first_x, first_y = swap(first, 2), swap(first, 4)
    residual, residual_columns, send_slots = run_kernel(
        dispatch_kernel,
        [((length, width), F32), ((column, length), F32), slots_out],
        [place, *mixer_pieces, rows, norm_two, choose],
        [((width, length), F32)],
        scalars=1, staged=(1, 5, 7))
    if near:
        first_w, second_w, grad_slots, d_hidden = run_kernel(
            functools.partial(unpack_kernel, share, capacity),
            weight_outs + [slots_out, ((slot_count, hidden_units), F32)],
            after([weights], send_slots),
            [*weight_outs, slots_out, pltpu.SemaphoreType.DMA((5 * groups,))],
            far_args=(0,),
            far_outs=(0, 1, 2),
        )
        first_x, first_y = after([first_x, first_y], d_hidden)
        halves = pass_halves(first_x, first_y)
        first_d = swap_across(halves)
    arrived = exchange_slots(send_slots)
    hidden, d_pre, d_slots = run_kernel(
        expert_kernel, [hidden_out, hidden_out, slots_out], [arrived, first_w, d_hidden], staged=(0, 1, 2))
    if near:
        d_slots = after([d_slots], first_d)[0]
    back_slots = exchange_slots(d_slots)
    grad_args = [arrived, grad_slots, hidden, d_pre, second_w]
    grad_out = ((experts, share, hidden_units), F32)
    if near:
        (packed,) = run_kernel(
            functools.partial(expert_grads_pack_kernel, share, capacity),
            [message_out],
            grad_args,
            [
                ((2, width, hidden_units), BF16),
                ((groups, folded, hidden_units), BF16),
                pltpu.SemaphoreType.DMA((3 * groups,)),
            ],
            far_outs=(0,), staged=range(5))
        firsts = swap_near([first, first_x, first_y, *first_d])
        back_slots = after([back_slots], packed, firsts)[0]
        packed = after([packed], back_slots)[0]
        owned = exchange(packed)
    else:
        grad_first, grad_second, moe_slots = run_kernel(
            expert_grads_kernel, weight_outs + [slots_out], grad_args, loose_outs=(0, 1, 2))
    back_chunks = run_kernel(
        back_rows_kernel,
        [((length // parts, width), BF16)] * parts,
        [place, choose, back_slots],
        [((length, width), F32)],
        scalars=1, loose_outs=(0, 1, 2, 3), staged=(1, 2))
    send_pieces = share_rows(add_low(send_chunks(back_chunks)), parts)
    decays, history, step_rows, drive_rows, step_slope, y_slope, gate_slope = run_kernel(
        scan_states_kernel,
        [
            ((length * states, full), F32),
            (((length + 1) * states, full), F32),
            ((length, full), F32),
            ((length, full), F32),
            ((length, chans), F32),
            ((length, chans), F32),
            ((length, chans), F32),
        ],
        [y, gate, act, *after([mixed], back_chunks[0]), masks, dt_proj, dt_bias, decay_log],
        [((states, full), F32), ((length, full), F32)],
        staged=range(5),
        held_outs=range(7),
    )
    send_pieces = after(send_pieces, decays)
    d_columns, d_mix, d_gated, gain_grad_two = run_kernel(
        mixer_grad_kernel,
        [
            ((column, length), F32),
            ((width, length), BF16),
            ((length, chans), F32),
            ((1, width), F32),
        ],
        [place, *send_pieces, residual, norm_two, cotangent, out_proj],
        [((length, width), F32), ((width, length), F32)],
        scalars=1, staged=(1, 5, 7, 8), held_outs=(1, 2, 3))
    d_mixed_part, d_act_scan, d_gate, second = run_kernel(
        scan_backward_kernel,
        [
            ((proj, length), BF16),
            ((length, chans), F32),
            ((length, chans), BF16),
            ((width + 2 * chans, length), BF16),
        ],
        [
            d_gated,
            y_slope,
            gate_slope,
            act,
            mixed,
            dt_proj,
            decay_log,
            skip_gain,
            gain_grad_two,
            d_mix,
            decays,
            history,
            step_rows,
            drive_rows,
            step_slope,
        ],
        [
            ((states, full), F32),
            ((length, full), F32),
            ((length, full), F32),
            ((length, full), F32),
        ],
        staged=(3, 4),
        loose_outs=(0, 3),
        held_outs=(1, 2),
    )
    d_mixed_pieces = share_rows(d_mixed_part, parts)
    if near:
        second_x, second_y = swap(second, 2), swap(second, 4)
    last_rows = chans + -(-proj // 16) * 16 + tiles * 2 * VECTORS_TWO
    normed_shares, message = run_kernel(
        leave_kernel,
        [((parts, column + 16, length), BF16), ((last_rows, length), BF16)],
        [
            place,
            *d_mixed_pieces,
            d_act_scan,
            d_gate,
            conv,
            inner,
            masks,
            x_turned,
            conv_weight,
            in_turned,
            rows,
            norm_one,
        ],
        [((parts, proj, length), BF16), ((width, length), F32), ((length, full), F32)],
        scalars=1, loose_outs=(1,), staged=(1, 7, 8, 9, 13))
    share_outs = [((2 * column + 16, length), BF16)] * parts
    if near:
        lasts = [message, swap(message, 2), swap(message, 4), swap(message, 6)]
        def first_sets(*refs):
            first_sets_kernel(refs[:10], *refs[10:])

        all_normed, all_gated, all_act = run_kernel(
            first_sets,
            [
                ((groups * length, width), BF16),
                ((chans, groups * length), BF16),
                ((chans, groups * length), BF16),
            ],
            after(firsts, message, owned),
            [((groups, width + 2 * chans, length), BF16), pltpu.SemaphoreType.DMA((10,))],
            far_args=range(10),
            held_outs=(0, 1, 2),
        )
        grad_expert_in, grad_expert_out = run_kernel(
            functools.partial(owner_kernel, share),
            [grad_out, grad_out],
            after([owned], all_normed),
            [
                ((groups, 2 * share, hidden_units), BF16),
                ((groups, 2 * share, hidden_units), F32),
                pltpu.SemaphoreType.DMA((groups,)),
                pltpu.SemaphoreType.DMA((2 * groups,)),
            ],
            far_args=(0,),
            far_outs=(0, 1),
        )
        second_x, second_y = after([second_x, second_y], grad_expert_in)
        halves = pass_halves(second_x, second_y)
        second_d = swap_across(halves)
        lasts = swap_near(after(lasts, halves))

        def back_folded(*refs):
            back_folded_kernel(share, *refs[:4], refs[4 : 4 + groups], *refs[4 + groups :])

        *shares, grad_conv_weight, grad_conv_bias = run_kernel(
            back_folded,
            [((2 * column + 16 + 2 * NORM_ROWS, length), BF16)] * parts
            + [((4, chans), F32), ((chans,), F32)],
            [place, choose, normed_shares, owned, *lasts],
            [
                slots_out,
                ((width, length), BF16),
                ((groups, tiles * 2 * VECTORS_TWO, length), BF16),
                pltpu.SemaphoreType.DMA((4 * groups,)),
            ],
            scalars=1,
            staged=(1, 2),
            far_args=range(3, 4 + groups),
            loose_outs=(parts, parts + 1),
        )
        norm_out = [((width,), F32)]
    else:
        shares = run_kernel(
            back_columns_kernel,
            share_outs,
            [place, choose, normed_shares, exchange_slots(moe_slots)],
            [((width, length), BF16)],
            scalars=1,
            loose_outs=(0, 1, 2, 3),
        )

        norm_out = []

        def owner_sum(values):
            got = exchange(values.reshape(groups, share, hidden_units)).astype(F32)
            return jnp.sum(got.reshape(tile_count, experts, share, hidden_units), axis=0)

        grad_expert_in = owner_sum(grad_first)
        grad_expert_out = owner_sum(grad_second)
    pieces = send_chunks(shares)
    if near:
        seconds = [second, second_x, second_y, *second_d]
        seconds = swap_near(after(seconds, grad_conv_weight))

        def wide_grads(*refs):
            wide_grads_kernel(
                (rank, states, proj), refs[:10], refs[10 : 10 + groups], *refs[10 + groups :]
            )

        (
            grad_out_proj,
            grad_in_turned,
            grad_x_turned,
            grad_dt_proj,
            grad_dt_bias,
            grad_decay_log,
            grad_skip_gain,
            grad_norm_two,
        ) = run_kernel(
            wide_grads,
            [
                ((chans, width), F32),
                ((2, chans, width), F32),
                ((proj, chans), F32),
                ((rank, chans), F32),
                ((chans,), F32),
                ((states, chans), F32),
                ((chans,), F32),
                ((width,), F32),
            ],
            [*seconds, *lasts, all_normed, all_gated, all_act],
            [
                ((groups, width + 2 * chans, length), BF16),
                ((groups, last_rows, length), BF16),
                ((groups * length, width), BF16),
                ((chans, groups * length), BF16),
                ((-(-proj // 16) * 16, groups * length), BF16),
                ((full, length), F32),
                ((3, chans, width), F32),
                pltpu.SemaphoreType.DMA((10,)),
                pltpu.SemaphoreType.DMA((groups,)),
                pltpu.SemaphoreType.DMA((4,)),
            ],
            far_args=[index for index in range(10 + groups) if index not in range(3, 10)],
            far_outs=(0, 1),
            loose_outs=range(8),
        )
        pieces = after(pieces, grad_out_proj)
    else:
        top = last_rows - tiles * 2 * VECTORS_TWO
        ones = second[width + chans :].astype(F32).T
        twos = message[top:].astype(F32).reshape(tiles, 2 * VECTORS_TWO, length)
        twos = jnp.swapaxes(twos, 0, 1).reshape(2 * VECTORS_TWO, full)[:, :chans]
        plain_normed = jnp.swapaxes(normed.reshape(-1, length, 128), 0, 1).reshape(length, width)
        plain_mix = jnp.swapaxes(d_mix.reshape(-1, length, 128), 0, 1).reshape(length, width)
        grad_in_turned, grad_x_turned, grad_dt_proj, grad_out_proj, ones, twos = lax.psum(
            (
                jnp.stack(
                    [
                        dot_nn(message[:chans], plain_normed),
                        dot_nn(second[width : width + chans], plain_normed),
                    ]
                ),
                dot_nn(message[chans : chans + proj], act),
                ones[:rank],
                dot_nn(first[width : width + chans], plain_mix),
                ones[rank : rank + VECTORS_ONE]
                + ones[rank + VECTORS_ONE : rank + 2 * VECTORS_ONE],
                twos[:VECTORS_TWO] + twos[VECTORS_TWO:],
            ),
            "dp",
        )
        grad_decay_log = ones[:states]
        grad_dt_bias = ones[states]
        grad_skip_gain = ones[states + 1]
        grad_norm_two = ones[states + 2 : states + 4]
        grad_conv_weight = twos[:4]
        grad_conv_bias = twos[4]
        grad_norm_one = sum(share_rows(twos[5:7].reshape(1, width), parts)).reshape(width)
    outcome, grad_tokens, *norm_one_grad = run_kernel(
        finish_rows_kernel,
        [((column, length), BF16), ((column, length), F32)] + norm_out,
        [*pieces, residual_columns, d_columns, tokens_turned, scale, gain_columns],
        staged=range(4, 9),
        loose_outs=(0, 1, 2),
    )
    if near:
        (grad_norm_one,) = norm_one_grad
    return (
        outcome.T,
        grad_tokens.T,
        grad_norm_one,
        jnp.swapaxes(grad_in_turned, 1, 2),
        grad_conv_weight,
        grad_conv_bias,
        grad_x_turned.T,
        grad_dt_proj,
        grad_dt_bias,
        grad_decay_log,
        grad_skip_gain,
        grad_out_proj,
        grad_norm_two.reshape(width),
        grad_expert_in,
        grad_expert_out,
    )


def solution(mesh):
    placed = (
        P("dp", "tensor"),
        P("dp"),
        P("dp", None),
        P(),
        P(None, None, "tensor"),
        P(None, "tensor"),
        P("tensor"),
        P("tensor", None),
        P(None, "tensor"),
        P("tensor"),
        P(None, "tensor"),
        P("tensor"),
        P("tensor", None),
        P(),
        P(None, "dp", "tensor"),
        P(None, "dp", "tensor"),
        P("dp", None),
    )
    return jax.shard_map(
        body,
        mesh=mesh,
        in_specs=placed,
        out_specs=(
            P("dp", "tensor"),
            P("dp", "tensor"),
            P(),
            P(None, None, "tensor"),
            P(None, "tensor"),
            P("tensor"),
            P("tensor", None),
            P(None, "tensor"),
            P("tensor"),
            P(None, "tensor"),
            P("tensor"),
            P("tensor", None),
            P(),
            P(None, "dp", "tensor"),
            P(None, "dp", "tensor"),
        ),
        check_vma=False,
    )
```

```python
import functools
import math

import jax
import jax.numpy as jnp
from jax import lax
from jax.experimental import pallas as pl
from jax.experimental.pallas import tpu as pltpu
from jax.sharding import PartitionSpec as P

EPSILON = 1e-05
F32 = jnp.float32
BF16 = jnp.bfloat16
NEVER = 1e4
LOG2E = 1.4426950408889634
GELU_SCALE = math.sqrt(2.0 / math.pi)
GELU_CUBE = 0.044715
VMEM_SPARE = 6 * 1024 * 1024
NEAR_GROUPS = 8
VECTORS_ONE = 24
VECTORS_TWO = 8
NORM_ROWS = 16


def run_kernel(
    kernel,
    outs,
    args,
    scratch=(),
    scalars=0,
    far_args=(),
    staged=(),
    far_outs=(),
    loose_outs=(),
    held_outs=(),
    alias=None,
):
    staged = tuple(staged)
    outside = {*far_args, *staged}

    def spec(index, far):
        return pl.BlockSpec(memory_space=pltpu.HBM if index in far else pltpu.VMEM)

    def held(index, shape, dtype):
        if index in loose_outs:
            return jax.ShapeDtypeStruct(shape, dtype)
        return (pltpu.VMEM if index in held_outs else pltpu.HBM)(shape, dtype)

    def body(*refs):
        refs = list(refs)
        if staged:
            *refs, semaphores = refs
            places = refs[len(refs) - len(staged) :]
            refs = refs[: len(refs) - len(staged)]
            copies = run_copies(list(zip([refs[index] for index in staged], places)), semaphores)
            for index, place in zip(staged, places):
                refs[index] = place
            for copy in copies:
                copy.wait()
        kernel(*refs)

    sizes = [(arg.shape, arg.dtype) for index, arg in enumerate(args) if index not in far_args]
    sizes += [out for index, out in enumerate(outs) if index not in far_outs]
    sizes += [shape for shape in scratch if isinstance(shape, tuple)]
    scratch = [pltpu.VMEM(*shape) if isinstance(shape, tuple) else shape for shape in scratch]
    if staged:
        scratch += [pltpu.VMEM(args[index].shape, args[index].dtype) for index in staged]
        scratch += [pltpu.SemaphoreType.DMA((len(staged),))]
    needed = sum(math.prod(shape) * jnp.dtype(dtype).itemsize for shape, dtype in sizes)
    return pl.pallas_call(
        body,
        out_shape=[held(index, shape, dtype) for index, (shape, dtype) in enumerate(outs)],
        in_specs=[
            pl.BlockSpec(memory_space=pltpu.SMEM) if index < scalars else spec(index, outside)
            for index in range(len(args))
        ],
        out_specs=[spec(index, far_outs) for index in range(len(outs))],
        scratch_shapes=scratch,
        input_output_aliases=alias or {},
        compiler_params=pltpu.CompilerParams(vmem_limit_bytes=VMEM_SPARE + needed * 5 // 4),
    )(
        *[
            pltpu.with_memory_space_constraint(arg, pltpu.HBM) if index in outside else arg
            for index, arg in enumerate(args)
        ]
    )


def dot_nn(left, right):
    return lax.dot_general(left, right, (((1,), (0,)), ((), ())), preferred_element_type=F32)


def dot_nt(left, right):
    return lax.dot_general(left, right, (((1,), (1,)), ((), ())), preferred_element_type=F32)


def dot_tn(left, right):
    return lax.dot_general(left, right, (((0,), (0,)), ((), ())), preferred_element_type=F32)


def lane_tiles(column, tiles):
    return jnp.concatenate([column] * tiles, axis=1)


def fold_tiles(values):
    total = values[:, :128]
    for tile in range(1, values.shape[1] // 128):
        total = total + values[:, 128 * tile : 128 * (tile + 1)]
    return total


def wide_masks(masks, index, chans):
    return lane_tiles(masks[index], -(-chans // 128))[:, :chans]


def rms_rate(values):
    return lax.rsqrt(jnp.mean(values * values, axis=-1, keepdims=True) + EPSILON)


def as_row(ref):
    return ref[...].reshape(1, ref.shape[0])


def softplus(values):
    return jnp.maximum(values, 0.0) + jnp.log1p(jnp.exp(-jnp.abs(values)))


def padded_copy(target, values):
    target[...] = jnp.zeros(target.shape, target.dtype)
    target[:, : values.shape[1]] = values


def put_row_chunks(place, source, outs):
    count = len(outs)
    rows = source.shape[0] // count
    for step, out in enumerate(outs):
        start = pl.multiple_of(lax.rem(place[0] + step, count) * rows, rows)
        out[pl.ds(0, rows), :] = source[pl.ds(start, rows), :].astype(out.dtype)


def take_row_pieces(place, pieces, target):
    count = len(pieces)
    rows = target.shape[0] // count
    for step, piece in enumerate(pieces):
        start = pl.multiple_of(lax.rem(place[0] - step + count, count) * rows, rows)
        target[pl.ds(start, rows), :] = piece[...].astype(target.dtype)


def sum_pieces(place, pieces, held):
    count = len(pieces)
    for step, piece in enumerate(pieces):
        held[lax.rem(place[0] - step + count, count)] = piece[...]
    total = held[0].astype(F32)
    for index in range(1, count):
        total = total + held[index].astype(F32)
    return total


def run_copies(copies, semaphores):
    started = []
    for index, (source, target) in enumerate(copies):
        copy = pltpu.make_async_copy(source, target, semaphores.at[index])
        copy.start()
        started.append(copy)
    return started


def fill_masks(resets, masks):
    length = resets.shape[1]
    square = (length, length)
    earlier = lax.broadcasted_iota(jnp.int32, square, 0)
    reset = jnp.broadcast_to(resets[...].astype(F32), square).T
    keep = jnp.where(reset == 0.0, 1.0, 0.0)
    joined = jnp.where(earlier > 0, keep, 0.0)
    one_back = pltpu.roll(joined, 1, 0)
    two_back = pltpu.roll(joined, 2, 0)
    masks[0] = keep
    masks[1] = joined
    masks[2] = joined * one_back
    masks[3] = joined * one_back * two_back


def fill_choose(capacity, block_rows, experts, routes, choose):
    length = routes.shape[1]
    square = (length, length)
    earlier = lax.broadcasted_iota(jnp.int32, square, 0)
    later = lax.broadcasted_iota(jnp.int32, square, 1)
    route_of = jnp.broadcast_to(routes[...].astype(F32), square)
    same = (route_of.T == route_of) & (earlier < later)
    if block_rows < length:
        same = same & (earlier // block_rows == later // block_rows)
    rank = jnp.sum(jnp.where(same, 1.0, 0.0), axis=0, keepdims=True).astype(jnp.int32)
    group = routes[...]
    if block_rows < length:
        group = group + experts * (later[:1] // block_rows)
    slot = group * capacity + rank
    slot_count = choose.shape[0]
    slot_ids = lax.broadcasted_iota(jnp.int32, (slot_count, length), 0)
    hit = slot_ids == jnp.broadcast_to(slot, (slot_count, length))
    choose[...] = jnp.where(hit, 1.0, 0.0).astype(BF16)


def prepare_kernel(
    experts, capacity, block_rows, resets, routes, cotangent, masks, choose, slots
):
    fill_masks(resets, masks)
    fill_choose(capacity, block_rows, experts, routes, choose)
    slots[...] = dot_nn(choose[...], cotangent[...]).astype(BF16)


def put_folded(target, slots):
    rows, width = slots.shape
    units = target.shape[1]
    half = rows // 2
    rest = width - units
    target[:rows, :] = slots[:, :units]
    target[rows:, :rest] = slots[:half, units:]
    target[rows:, rest:] = slots[half:, units:]


def unfold_copies(source, target, top, rows):
    units = source.shape[1]
    half = rows // 2
    rest = target.shape[1] - units
    copies = [(source.at[pl.ds(0, rows)], target.at[pl.ds(top, rows), pl.ds(0, units)])]
    for part in range(2):
        copies.append(
            (
                source.at[pl.ds(rows, half), pl.ds(part * rest, rest)],
                target.at[pl.ds(top + part * half, half), pl.ds(units, rest)],
            )
        )
    return copies


def pack_kernel(
    capacity,
    resets_in,
    routes_in,
    cotangent_in,
    expert_in,
    expert_out,
    masks,
    choose,
    message,
    packed,
    staged,
    resets,
    routes,
    cotangent,
    early_arrivals,
    arrivals,
    semaphores,
):
    experts, share, units = expert_in.shape
    length, width = cotangent.shape
    copies = []
    for index in range(experts):
        copies.append((expert_in.at[index], staged.at[index, 0]))
        copies.append((expert_out.at[index], staged.at[index, 1]))
    early = run_copies(
        [(resets_in, resets), (routes_in, routes), (cotangent_in, cotangent)], early_arrivals
    )
    arriving = run_copies(copies, arrivals)
    started = []
    for index in range(experts):
        copies = []
        for which in range(2):
            arriving[2 * index + which].wait()
            target = message.at[index, pl.ds(which * share, share)]
            copies.append((staged.at[index, which], target))
        started += run_copies(copies, semaphores.at[pl.ds(2 * index, 2)])
    for copy in early:
        copy.wait()
    fill_choose(capacity, length, experts, routes, choose)
    slots = dot_nn(choose[...], cotangent[...]).astype(BF16)
    copies = []
    for index in range(experts):
        put_folded(packed.at[index], slots[index * capacity : (index + 1) * capacity])
        target = message.at[index]
        copies.append((packed.at[index], target.at[pl.ds(2 * share, packed.shape[1])]))
    started += run_copies(copies, semaphores.at[pl.ds(2 * experts, experts)])
    fill_masks(resets, masks)
    for copy in started:
        copy.wait()


def pass_on(along_x, along_y, pass_y, pass_x, passed, arrivals, semaphores):
    half = passed.shape[1]
    copies = [
        (along_y.at[pl.ds(0, half)], passed.at[0]),
        (along_x.at[pl.ds(half, half)], passed.at[1]),
    ]
    for copy in run_copies(copies, arrivals):
        copy.wait()
    return run_copies([(passed.at[0], pass_y), (passed.at[1], pass_x)], semaphores)


def pass_kernel(along_x, along_y, pass_y, pass_x, passed, arrivals, semaphores):
    for copy in pass_on(along_x, along_y, pass_y, pass_x, passed, arrivals, semaphores):
        copy.wait()


def unpack_kernel(
    share,
    capacity,
    message,
    first_out,
    second_out,
    slots_out,
    d_hidden,
    first_w,
    second_w,
    grad_slots,
    semaphores,
):
    folded = capacity + capacity // 2
    copies = []
    for index in range(message.shape[0]):
        piece = message.at[index]
        rows = pl.ds(index * share, share)
        copies.append((piece.at[pl.ds(share, share)], second_w.at[rows]))
        copies += unfold_copies(
            piece.at[pl.ds(2 * share, folded)], grad_slots, index * capacity, capacity
        )
        copies.append((piece.at[pl.ds(0, share)], first_w.at[rows]))
    for copy in run_copies(copies, semaphores):
        copy.wait()
    copies = [(first_w, first_out), (second_w, second_out), (grad_slots, slots_out)]
    started = run_copies(copies, semaphores)
    d_hidden[...] = dot_nn(grad_slots[...], second_w[...])
    for copy in started:
        copy.wait()


def put_blocks(target, values):
    length = values.shape[0]
    for start in range(0, values.shape[1], 128):
        target[start : start + length, :] = values[:, start : start + 128]


def enter_kernel(
    place,
    piece_0,
    piece_1,
    piece_2,
    piece_3,
    gain_ref,
    in_proj,
    conv_weight,
    conv_bias,
    x_proj,
    masks,
    rows_out,
    normed_out,
    act_out,
    inner_out,
    conv_out,
    gate_out,
    scale_out,
    gain_out,
    mixed_out,
    turned,
):
    take_row_pieces(place, (piece_0, piece_1, piece_2, piece_3), turned)
    rows = turned[...].T
    gain = as_row(gain_ref)
    rows_out[...] = rows.astype(BF16)
    normed = (rows * rms_rate(rows) * gain).astype(BF16)
    put_blocks(normed_out, normed)
    inner = dot_nt(normed, in_proj[0])
    chans = inner.shape[1]
    inner_out[...] = inner
    total = as_row(conv_bias) + conv_weight[3:4, :] * inner
    for shift in (1, 2, 3):
        moved = pltpu.roll(inner, shift, 0) * wide_masks(masks, shift, chans)
        total = total + conv_weight[3 - shift : 4 - shift, :] * moved
    conv_out[...] = total
    act = (total * jax.nn.sigmoid(total)).astype(BF16)
    act_out[...] = act
    mixed_out[...] = dot_nt(x_proj[...], act).astype(BF16)
    gate_out[...] = dot_nt(normed, in_proj[1])
    raw = turned[...]
    scale_out[...] = lax.rsqrt(jnp.mean(raw * raw, axis=0, keepdims=True) + EPSILON)
    turned[...] = jnp.broadcast_to(gain, rows.shape).T
    column = gain_out.shape[0]
    gain_out[...] = turned[pl.ds(pl.multiple_of(place[0] * column, column), column), :]


def block_columns(transposed, block):
    length = transposed.shape[1]
    return pltpu.roll(transposed, lax.rem(length - 8 * block, length), 1)


def spread_column(columns, row, tiles):
    return lane_tiles(jnp.broadcast_to(columns[:, row : row + 1], (columns.shape[0], 128)), tiles)


def scan_forward_kernel(
    place,
    piece_0,
    piece_1,
    piece_2,
    piece_3,
    dt_proj,
    dt_bias,
    decay_log,
    skip_gain,
    act_in,
    gate_in,
    masks,
    out_proj,
    normed,
    out_0,
    out_1,
    out_2,
    out_3,
    mixed_out,
    share_out,
    y_out,
    held,
    rate,
    step_rows,
    drive_rows,
    y_rows,
    partial,
):
    rank = dt_proj.shape[0]
    states = decay_log.shape[0]
    length, chans = y_out.shape
    tiles = step_rows.shape[1] // 128
    mixed = sum_pieces(place, (piece_0, piece_1, piece_2, piece_3), held)
    mixed_out[...] = mixed
    step_size = softplus(dot_tn(mixed[:rank].astype(BF16), dt_proj[...]) + as_row(dt_bias))
    act = act_in[...].astype(F32)
    reset = NEVER * (1.0 - wide_masks(masks, 0, chans))
    padded_copy(rate, -LOG2E * jnp.exp(decay_log[...]))
    padded_copy(step_rows, step_size + reset)
    padded_copy(drive_rows, step_size * act)
    b_turned = mixed[rank : rank + states]
    c_turned = mixed[rank + states : rank + 2 * states]

    def block(index, state):
        start = pl.multiple_of(index * 8, 8)
        b_cols = block_columns(b_turned, index)
        c_cols = block_columns(c_turned, index)
        steps = step_rows[pl.ds(start, 8), :]
        drives = drive_rows[pl.ds(start, 8), :]
        rows = []
        for row in range(8):
            decay = jnp.exp2(rate[...] * steps[row : row + 1])
            state = decay * state + spread_column(b_cols, row, tiles) * drives[row : row + 1]
            rows.append(
                jnp.sum(spread_column(c_cols, row, tiles) * state, axis=0, keepdims=True)
            )
        y_rows[pl.ds(start, 8), :] = jnp.concatenate(rows, axis=0)
        return state

    lax.fori_loop(0, length // 8, block, jnp.zeros((states, 128 * tiles), F32))
    y = y_rows[:, :chans] + as_row(skip_gain) * act
    y_out[...] = y
    gate = gate_in[...]
    gated = (y * (gate * jax.nn.sigmoid(gate))).astype(BF16)
    partial[...] = dot_nn(gated, out_proj[...])
    put_row_chunks(place, partial, (out_0, out_1, out_2, out_3))
    width = normed.shape[0]
    share_out[:width] = normed[...]
    padded_copy(step_rows, gated.astype(F32))
    share_out[width : width + chans] = step_rows[...].T[:chans].astype(BF16)
    padded_copy(step_rows, act)
    share_out[width + chans :] = step_rows[...].T[:chans].astype(BF16)


def dispatch_kernel(
    place,
    piece_0,
    piece_1,
    piece_2,
    piece_3,
    rows_in,
    gain,
    choose,
    residual_out,
    columns_out,
    slots,
    turned,
):
    take_row_pieces(place, (piece_0, piece_1, piece_2, piece_3), residual_out)
    residual = rows_in[...].astype(F32) + residual_out[...]
    residual_out[...] = residual
    send = (residual * rms_rate(residual) * as_row(gain)).astype(BF16)
    slots[...] = dot_nn(choose[...], send).astype(BF16)
    turned[...] = residual.T
    column = columns_out.shape[0]
    columns_out[...] = turned[pl.ds(pl.multiple_of(place[0] * column, column), column), :]


def hidden_back_kernel(grad_slots, second_w, d_hidden):
    d_hidden[...] = dot_nn(grad_slots[...], second_w[...])


def expert_kernel(arrived, first_w, d_hidden, hidden_out, d_pre_out, d_slots):
    value = dot_nn(arrived[...], first_w[...])
    square = value * value
    bend = jnp.tanh(GELU_SCALE * (value + GELU_CUBE * value * square))
    half = 0.5 * (1.0 + bend)
    slope = half + 0.5 * value * (1.0 - bend * bend) * GELU_SCALE * (
        1.0 + 3.0 * GELU_CUBE * square
    )
    d_pre = (slope * d_hidden[...]).astype(BF16)
    d_pre_out[...] = d_pre
    d_slots[...] = dot_nt(d_pre, first_w[...]).astype(BF16)
    hidden_out[...] = (value * half).astype(BF16)


def expert_grads_kernel(arrived, grad_slots, hidden, d_pre, second_w, first_out, second_out, moe):
    first_out[...] = dot_tn(arrived[...], d_pre[...]).astype(BF16)
    second_out[...] = dot_tn(grad_slots[...], hidden[...]).astype(BF16)
    moe[...] = dot_nt(hidden[...], second_w[...]).astype(BF16)


def expert_grads_pack_kernel(
    share, capacity, arrived, grad_slots, hidden, d_pre, second_w, message, grads, packed, semaphores
):
    experts = message.shape[0]
    started = []
    for which, (left, right) in enumerate(((arrived, d_pre), (grad_slots, hidden))):
        grads[which] = dot_tn(left[...], right[...]).astype(BF16)
        copies = [
            (
                grads.at[which, pl.ds(index * share, share)],
                message.at[index, pl.ds(which * share, share)],
            )
            for index in range(experts)
        ]
        started += run_copies(copies, semaphores.at[pl.ds(which * experts, experts)])
    moe = dot_nt(hidden[...], second_w[...]).astype(BF16)
    copies = []
    for index in range(experts):
        put_folded(packed.at[index], moe[index * capacity : (index + 1) * capacity])
        copies.append(
            (packed.at[index], message.at[index, pl.ds(2 * share, packed.shape[1])])
        )
    started += run_copies(copies, semaphores.at[pl.ds(2 * experts, experts)])
    for copy in started:
        copy.wait()


def owner_kernel(share, message, first_out, second_out, low, wide, arrivals, semaphores):
    count = message.shape[0]
    arriving = run_copies(
        [(message.at[index, pl.ds(0, 2 * share)], low.at[index]) for index in range(count)],
        arrivals,
    )
    started = []
    for index in range(count):
        arriving[index].wait()
        wide[index] = low[index].astype(F32)
        copies = [
            (wide.at[index, pl.ds(0, share)], first_out.at[index]),
            (wide.at[index, pl.ds(share, share)], second_out.at[index]),
        ]
        started += run_copies(copies, semaphores.at[pl.ds(2 * index, 2)])
    for copy in started:
        copy.wait()


def back_rows_kernel(place, choose, slots, out_0, out_1, out_2, out_3, partial):
    partial[...] = dot_tn(choose[...], slots[...])
    put_row_chunks(place, partial, (out_0, out_1, out_2, out_3))


def back_columns_kernel(place, choose, shares, slots, out_0, out_1, out_2, out_3, rows):
    rows[...] = dot_tn(slots[...], choose[...]).astype(BF16)
    outs = (out_0, out_1, out_2, out_3)
    count, top, _ = shares.shape
    column = rows.shape[0] // count
    for step, out in enumerate(outs):
        whose = lax.rem(place[0] + step, count)
        out[:top, :] = shares[whose]
        out[top:, :] = rows[pl.ds(pl.multiple_of(whose * column, column), column), :]


def back_folded_kernel(
    share,
    place,
    choose,
    shares,
    message,
    refs,
    out_0,
    out_1,
    out_2,
    out_3,
    weight_grad,
    bias_grad,
    slots,
    rows,
    staged,
    semaphores,
):
    count = message.shape[0]
    capacity = slots.shape[0] // count
    folded = message.shape[1] - 2 * share
    copies = []
    for index in range(count):
        copies += unfold_copies(
            message.at[index, pl.ds(2 * share, folded)], slots, index * capacity, capacity
        )
    deep = 2 * VECTORS_TWO
    height = staged.shape[1]
    top = refs[0].shape[0] - height
    copies += [(ref.at[pl.ds(top, height)], staged.at[index]) for index, ref in enumerate(refs)]
    for copy in run_copies(copies, semaphores):
        copy.wait()
    total = staged[0].astype(F32)
    for index in range(1, staged.shape[0]):
        total = total + staged[index].astype(F32)
    chans = weight_grad.shape[1]
    vectors = jnp.concatenate(
        [total[start : start + deep] for start in range(0, height, deep)], axis=1
    )[:, :chans]
    vectors = vectors[:VECTORS_TWO] + vectors[VECTORS_TWO:]
    weight_grad[...] = vectors[:4]
    bias_grad[...] = vectors[4].reshape(chans)
    norm_grad = jnp.concatenate([vectors[5:6], vectors[6:7]], axis=1)
    norm_rows = [norm_grad[:, start : start + 128] for start in range(0, norm_grad.shape[1], 128)]
    spare = jnp.zeros((NORM_ROWS - len(norm_rows), 128), F32)
    upper, lower = split_vectors(jnp.concatenate([*norm_rows, spare], axis=0))
    norm_low = jnp.concatenate([upper, lower], axis=0).astype(BF16)
    outs = (out_0, out_1, out_2, out_3)
    plain = out_0.shape[0] - 2 * NORM_ROWS
    back_columns_kernel(
        place, choose, shares, slots, *[out.at[pl.ds(0, plain)] for out in outs], rows
    )
    for out in outs:
        out[plain:, :] = norm_low


def mixer_grad_kernel(
    place,
    piece_0,
    piece_1,
    piece_2,
    piece_3,
    residual_in,
    gain_ref,
    cotangent,
    out_proj,
    columns_out,
    mix_out,
    d_gated,
    gain_grad,
    d_send,
    turned,
):
    take_row_pieces(place, (piece_0, piece_1, piece_2, piece_3), d_send)
    residual = residual_in[...]
    inverse = rms_rate(residual)
    scaled = residual * inverse
    grad = d_send[...]
    pulled = grad * as_row(gain_ref)
    along = jnp.mean(pulled * scaled, axis=-1, keepdims=True)
    d_residual = cotangent[...].astype(F32) + inverse * (pulled - scaled * along)
    d_mix = d_residual.astype(BF16)
    put_blocks(mix_out, d_mix)
    d_gated[...] = dot_nt(d_mix, out_proj[...])
    gain_grad[...] = jnp.sum(grad * scaled, axis=0, keepdims=True)
    turned[...] = d_residual.T
    column = columns_out.shape[0]
    columns_out[...] = turned[pl.ds(pl.multiple_of(place[0] * column, column), column), :]


def split_vectors(vectors):
    upper = vectors.astype(BF16).astype(F32)
    return upper, vectors - upper


def scan_states_kernel(
    y_in,
    gate_in,
    act_in,
    mixed_in,
    masks,
    dt_proj,
    dt_bias,
    decay_log,
    decays,
    history,
    step_rows,
    drive_rows,
    step_slope,
    y_slope,
    gate_slope,
    rate,
    decay_rows,
):
    rank = dt_proj.shape[0]
    states = decay_log.shape[0]
    length, chans = y_in.shape
    tiles = step_rows.shape[1] // 128
    full = 128 * tiles
    mixed = mixed_in[...]
    raw_step = dot_tn(mixed[:rank].astype(BF16), dt_proj[...]) + as_row(dt_bias)
    step_size = softplus(raw_step)
    step_slope[...] = jax.nn.sigmoid(raw_step)
    reset = NEVER * (1.0 - wide_masks(masks, 0, chans))
    padded_copy(rate, -LOG2E * jnp.exp(decay_log[...]))
    padded_copy(step_rows, step_size)
    padded_copy(decay_rows, step_size + reset)
    padded_copy(drive_rows, step_size * act_in[...].astype(F32))
    gate = gate_in[...]
    gate_sig = jax.nn.sigmoid(gate)
    y_slope[...] = gate * gate_sig
    gate_slope[...] = y_in[...] * gate_sig * (1.0 + gate * (1.0 - gate_sig))
    b_turned = mixed[rank : rank + states]
    history[pl.ds(0, states), :] = jnp.zeros((states, full), F32)

    def forward_block(index, state):
        start = pl.multiple_of(index * 8, 8)
        b_cols = block_columns(b_turned, index)
        steps = decay_rows[pl.ds(start, 8), :]
        drives = drive_rows[pl.ds(start, 8), :]
        for row in range(8):
            decay = jnp.exp2(rate[...] * steps[row : row + 1])
            state = decay * state + spread_column(b_cols, row, tiles) * drives[row : row + 1]
            at = pl.multiple_of((start + row) * states, states)
            decays[pl.ds(at, states), :] = decay
            history[pl.ds(at + states, states), :] = state
        return state

    lax.fori_loop(0, length // 8, forward_block, jnp.zeros((states, full), F32))


def scan_backward_kernel(
    d_gated,
    y_slope,
    gate_slope,
    act_in,
    mixed_in,
    dt_proj,
    decay_log,
    skip_gain,
    gain_grad,
    d_mix,
    decays,
    history,
    step_rows,
    drive_rows,
    step_slope,
    d_mixed_out,
    d_act_out,
    d_gate_out,
    share_out,
    rate,
    dy_rows,
    du_rows,
    dl_rows,
):
    rank = dt_proj.shape[0]
    states = decay_log.shape[0]
    length, chans = y_slope.shape
    tiles = step_rows.shape[1] // 128
    full = 128 * tiles
    mixed = mixed_in[...]
    dt_low = mixed[:rank].astype(BF16)
    act = act_in[...].astype(F32)
    padded_copy(rate, -jnp.exp(decay_log[...]))
    d_out = d_gated[...]
    d_y = d_out * y_slope[...]
    padded_copy(dy_rows, d_y)
    d_gate = d_out * gate_slope[...]
    b_turned = mixed[rank : rank + states]
    c_turned = mixed[rank + states : rank + 2 * states]
    lanes = lax.broadcasted_iota(jnp.int32, (states, length), 1)

    def backward_block(count, carry):
        carried, d_rate, d_b, d_c = carry
        index = length // 8 - 1 - count
        start = pl.multiple_of(index * 8, 8)
        b_cols = block_columns(b_turned, index)
        c_cols = block_columns(c_turned, index)
        steps = step_rows[pl.ds(start, 8), :]
        drives = drive_rows[pl.ds(start, 8), :]
        dys = dy_rows[pl.ds(start, 8), :]
        du = [None] * 8
        dl = [None] * 8
        for row in reversed(range(8)):
            at = pl.multiple_of((start + row) * states, states)
            before = history[pl.ds(at, states), :]
            after = history[pl.ds(at + states, states), :]
            decay = decays[pl.ds(at, states), :]
            here = lanes == start + row
            dy_row = jnp.broadcast_to(dys[row : row + 1], (states, full))
            grad = spread_column(c_cols, row, tiles) * dy_row + carried
            c_part = jnp.sum(fold_tiles(dy_row * after), axis=1, keepdims=True)
            d_c = jnp.where(here, c_part, d_c)
            b_part = jnp.sum(fold_tiles(grad * drives[row : row + 1]), axis=1, keepdims=True)
            d_b = jnp.where(here, b_part, d_b)
            du[row] = jnp.sum(grad * spread_column(b_cols, row, tiles), axis=0, keepdims=True)
            carried = grad * decay
            d_log = carried * before
            dl[row] = jnp.sum(d_log * rate[...], axis=0, keepdims=True)
            d_rate = d_rate + d_log * steps[row : row + 1]
        du_rows[pl.ds(start, 8), :] = jnp.concatenate(du, axis=0)
        dl_rows[pl.ds(start, 8), :] = jnp.concatenate(dl, axis=0)
        return carried, d_rate, d_b, d_c

    nothing = jnp.zeros((states, full), F32)
    thin = jnp.zeros((states, length), F32)
    _, d_rate, d_b, d_c = lax.fori_loop(
        0, length // 8, backward_block, (nothing, nothing, thin, thin)
    )
    du = du_rows[:, :chans]
    d_step = (dl_rows[:, :chans] + du * act) * step_slope[...]
    d_step_low = d_step.astype(BF16)
    low_turned = dot_nt(dt_proj[...], d_step_low)
    d_mixed_out[...] = jnp.concatenate([low_turned, d_b, d_c], axis=0).astype(BF16)
    d_act_out[...] = du * step_rows[:, :chans] + as_row(skip_gain) * d_y
    d_gate_low = d_gate.astype(BF16)
    d_gate_out[...] = d_gate_low
    width = d_mix.shape[0]
    share_out[:width] = d_mix[...]
    padded_copy(du_rows, d_gate_low.astype(F32))
    share_out[width : width + chans] = du_rows[...].T[:chans].astype(BF16)
    gain_rows = gain_grad[...]
    upper, lower = split_vectors(
        jnp.concatenate(
            [
                (d_rate * rate[...])[:, :chans],
                jnp.sum(d_step, axis=0, keepdims=True),
                jnp.sum(d_y * act, axis=0, keepdims=True),
                gain_rows[:, :chans],
                gain_rows[:, chans:],
                jnp.zeros((VECTORS_ONE - states - 4, chans), F32),
            ],
            axis=0,
        )
    )
    dl_rows[...] = jnp.zeros(dl_rows.shape, F32)
    dl_rows[:rank, :chans] = dot_nn(dt_low, d_step_low)
    dl_rows[rank : rank + VECTORS_ONE, :chans] = upper
    dl_rows[rank + VECTORS_ONE : rank + 2 * VECTORS_ONE, :chans] = lower
    share_out[width + chans :] = dl_rows[...].T[:chans].astype(BF16)


def leave_kernel(
    place,
    piece_0,
    piece_1,
    piece_2,
    piece_3,
    d_act_scan,
    d_gate,
    conv_in,
    inner_in,
    masks,
    x_proj,
    conv_weight,
    in_proj,
    rows_in,
    gain,
    shares,
    message,
    held,
    turned,
    padded,
):
    length, chans = inner_in.shape
    width = rows_in.shape[1]
    full = padded.shape[1]
    d_mixed = sum_pieces(place, (piece_0, piece_1, piece_2, piece_3), held).astype(BF16)
    d_act = d_act_scan[...] + dot_tn(d_mixed, x_proj[...])
    conv = conv_in[...]
    sig = jax.nn.sigmoid(conv)
    d_conv = d_act * sig * (1.0 + conv * (1.0 - sig))
    inner = inner_in[...]
    d_inner = conv_weight[3:4, :] * d_conv
    weight_grads = [jnp.sum(d_conv * inner, axis=0, keepdims=True)]
    for shift in (1, 2, 3):
        masked = d_conv * wide_masks(masks, shift, chans)
        weight_grads.append(
            jnp.sum(masked * pltpu.roll(inner, shift, 0), axis=0, keepdims=True)
        )
        d_inner = d_inner + conv_weight[3 - shift : 4 - shift, :] * pltpu.roll(
            masked, length - shift, 0
        )
    d_inner_low = d_inner.astype(BF16)
    padded_copy(padded, d_inner_low.astype(F32))
    message[:chans] = padded[...].T[:chans].astype(BF16)
    proj = d_mixed.shape[0]
    top = message.shape[0] - full // 128 * 2 * VECTORS_TWO
    message[chans:top] = jnp.concatenate(
        [d_mixed.astype(F32), jnp.zeros((top - chans - proj, length), F32)], axis=0
    ).astype(BF16)
    d_normed = dot_nn(d_inner_low, in_proj[0]) + dot_nn(d_gate[...], in_proj[1])
    rows = rows_in[...].astype(F32)
    scaled = rows * rms_rate(rows)
    norm_grad = jnp.sum(d_normed * scaled, axis=0, keepdims=True)
    upper, lower = split_vectors(
        jnp.concatenate(
            [
                weight_grads[3],
                weight_grads[2],
                weight_grads[1],
                weight_grads[0],
                jnp.sum(d_conv, axis=0, keepdims=True),
                norm_grad[:, :chans],
                norm_grad[:, chans:],
                jnp.zeros((VECTORS_TWO - 7, chans), F32),
            ],
            axis=0,
        )
    )
    padded_copy(padded, jnp.zeros((length, chans), F32))
    padded[:VECTORS_TWO, :chans] = upper
    padded[VECTORS_TWO : 2 * VECTORS_TWO, :chans] = lower
    for tile in range(full // 128):
        message[top + tile * 2 * VECTORS_TWO : top + (tile + 1) * 2 * VECTORS_TWO] = padded[
            : 2 * VECTORS_TWO, tile * 128 : (tile + 1) * 128
        ].astype(BF16)
    along = jnp.mean(d_normed * as_row(gain) * scaled, axis=-1, keepdims=True)
    along = jnp.broadcast_to(along, (length, length)).T[:8]
    high = along.astype(BF16)
    low = (along - high.astype(F32)).astype(BF16)
    turned[...] = d_normed.T
    count, rows, _ = shares.shape
    column = width // count
    ends = jnp.concatenate([high, low], axis=0)
    for index in range(count):
        shares[index, :column, :] = turned[index * column : (index + 1) * column].astype(BF16)
        shares[index, column:, :] = ends


def finish_rows_kernel(
    piece_0,
    piece_1,
    piece_2,
    piece_3,
    residual,
    d_columns,
    tokens,
    scale,
    gain,
    outcome,
    grad_tokens,
    *norm_out,
):
    column = tokens.shape[0]
    total = piece_0[...].astype(F32)
    for piece in (piece_1, piece_2, piece_3):
        total = total + piece[...].astype(F32)
    along = total[column : column + 1] + total[column + 8 : column + 9]
    inverse = scale[...]
    pulled = total[:column] * gain[...]
    scaled = tokens[...].astype(F32) * inverse
    grad_tokens[...] = d_columns[...] + inverse * (pulled - scaled * along)
    plain = 2 * column + 16
    outcome[...] = (residual[...] + total[column + 16 : plain]).astype(BF16)
    for out in norm_out:
        norm = total[plain : plain + NORM_ROWS] + total[plain + NORM_ROWS :]
        width = out.shape[0]
        out[...] = jnp.concatenate(
            [norm[row : row + 1] for row in range(width // 128)], axis=1
        ).reshape(width)


def take_blocks(target, pieces):
    for index, piece in enumerate(pieces):
        for start in range(0, target.shape[1], 128):
            target[index * 128 : (index + 1) * 128, start : start + 128] = piece[
                start : start + 128
            ]


def take_turned(target, pieces, start):
    rows = target.shape[0]
    for index, piece in enumerate(pieces):
        target[:, index * 128 : (index + 1) * 128] = piece[start : start + rows]


def stage_pieces(refs, staged, semaphores, rows=None):
    copies = []
    parts = len(refs) // 2
    for index, ref in enumerate(refs):
        side, part = divmod(index, parts)
        target = staged.at[4 * side + min(part, 3)]
        if part >= 3 and parts > 4:
            height = staged.shape[1] // (parts - 3)
            target = target.at[pl.ds((part - 3) * height, height)]
        copies.append((ref if rows is None else ref.at[pl.ds(*rows)], target))
    return run_copies(copies, semaphores), [staged.at[index] for index in range(8)]


def first_sets_kernel(refs, normed, gated, acts, staged, semaphores):
    chans = gated.shape[0]
    width = normed.shape[1]
    arriving, firsts = stage_pieces(refs, staged, semaphores)
    for copy in arriving:
        copy.wait()
    take_blocks(normed, firsts)
    take_turned(gated, firsts, width)
    take_turned(acts, firsts, width + chans)


def wide_grads_kernel(
    sizes,
    second_refs,
    last_refs,
    normed,
    gated,
    acts,
    out_grad,
    in_grad,
    x_grad,
    dt_grad,
    bias_grad,
    decay_grad,
    skip_grad,
    norm_grad,
    staged,
    staged_last,
    mixed,
    d_gate,
    d_mixed,
    total,
    wide_grad,
    second_arrivals,
    last_arrivals,
    semaphores,
):
    rank, states, proj = sizes
    chans, width = out_grad.shape
    arriving_last, lasts = stage_pieces(last_refs, staged_last, last_arrivals)
    for copy in arriving_last:
        copy.wait()
    arriving, seconds = stage_pieces(second_refs, staged, second_arrivals)
    take_turned(d_gate, lasts, 0)
    wide_grad[0] = dot_nn(d_gate[...], normed[...])
    started = run_copies([(wide_grad.at[0], in_grad.at[0])], semaphores)
    for copy in arriving:
        copy.wait()
    take_turned(d_gate, seconds, width)
    wide_grad[1] = dot_nn(d_gate[...], normed[...])
    started += run_copies([(wide_grad.at[1], in_grad.at[1])], semaphores.at[pl.ds(1, 1)])
    take_blocks(mixed, seconds)
    half = chans // 2
    for index in range(2):
        rows = pl.ds(index * half, half)
        wide_grad[2, rows] = dot_nn(gated[rows], mixed[...])
        started += run_copies(
            [(wide_grad.at[2, rows], out_grad.at[rows])], semaphores.at[pl.ds(2 + index, 1)]
        )
    take_turned(d_mixed, lasts, chans)
    x_grad[...] = dot_nt(d_mixed[...], acts[...])[:proj]
    vectors = seconds[0][width + chans :].astype(F32)
    for piece in seconds[1:]:
        vectors = vectors + piece[width + chans :].astype(F32)
    total[...] = jnp.zeros(total.shape, F32)
    total[:chans] = vectors
    rows = total[...].T[:, :chans]
    dt_grad[...] = rows[:rank]
    rows = rows[rank : rank + VECTORS_ONE] + rows[rank + VECTORS_ONE : rank + 2 * VECTORS_ONE]
    decay_grad[...] = rows[:states]
    bias_grad[...] = rows[states].reshape(chans)
    skip_grad[...] = rows[states + 1].reshape(chans)
    norm_grad[...] = jnp.concatenate(
        [rows[states + 2 : states + 3], rows[states + 3 : states + 4]], axis=1
    ).reshape(width)
    for copy in started:
        copy.wait()


def send_chunks(chunks):
    count = len(chunks)
    pairs = [[(i, (i + s) % count) for i in range(count)] for s in range(count)]
    return [chunks[0]] + [lax.ppermute(chunks[s], "tensor", pairs[s]) for s in range(1, count)]


def share_rows(values, count):
    return send_chunks([values] * count)


def add_low(pieces):
    total = pieces[0].astype(F32)
    for piece in pieces[1:]:
        total = total + piece.astype(F32)
    return total.astype(BF16)


def after(values, *events):
    return list(lax.optimization_barrier((tuple(values), events))[0])


def swap(values, bits):
    return lax.ppermute(values, "dp", [(i, i ^ bits) for i in range(NEAR_GROUPS)])


def swap_across(halves):
    return [swap(halves[0], 2), swap(halves[1], 4)]


def swap_near(values):
    return [*values, *[swap(part, 1) for part in values]]


def body(
    tokens,
    resets,
    routes,
    norm_one,
    in_proj,
    conv_weight,
    conv_bias,
    x_proj,
    dt_proj,
    dt_bias,
    decay_log,
    skip_gain,
    out_proj,
    norm_two,
    expert_in,
    expert_out,
    cotangent,
):
    groups = lax.axis_size("dp")
    parts = lax.axis_size("tensor")
    place = lax.axis_index("tensor").astype(jnp.int32).reshape(1)
    length, column = tokens.shape
    width = norm_one.shape[0]
    rank, chans = dt_proj.shape
    states = decay_log.shape[0]
    experts, share, hidden_units = expert_in.shape
    proj = x_proj.shape[1]
    tile_count = groups // experts
    block_rows = length * experts // groups
    capacity = max(2, block_rows // 4)
    slot_count = groups * capacity
    tiles = -(-chans // 128)
    full = 128 * tiles
    near = groups == NEAR_GROUPS and experts == groups
    tokens_turned = tokens.T
    in_turned = jnp.swapaxes(in_proj, 1, 2)
    x_turned = x_proj.T
    resets_row = resets.reshape(1, length)
    routes_row = routes.reshape(1, length)

    def exchange(values):
        return lax.all_to_all(values, "dp", split_axis=0, concat_axis=0, tiled=True)

    def exchange_slots(slots):
        return exchange(slots.reshape(groups, capacity, width)).reshape(slot_count, width)

    half_out = (((width + 2 * chans) // 2, length), BF16)

    def pass_halves(along_x, along_y):
        return run_kernel(
            pass_kernel,
            [half_out, half_out],
            [along_x, along_y],
            [
                ((2, *half_out[0]), BF16),
                pltpu.SemaphoreType.DMA((2,)),
                pltpu.SemaphoreType.DMA((2,)),
            ],
            far_args=(0, 1),
            far_outs=(0, 1),
        )

    token_pieces = share_rows(tokens_turned, parts)
    mask_out = ((4, length, 128), F32)
    choose_out = ((slot_count, length), BF16)
    weight_outs = [((width, hidden_units), BF16)] * 2
    slots_out = ((slot_count, width), BF16)
    hidden_out = ((slot_count, hidden_units), BF16)
    folded = capacity + capacity // 2
    message_out = ((groups, 2 * share + folded, hidden_units), BF16)
    if near:
        masks, choose, packed = run_kernel(
            functools.partial(pack_kernel, capacity),
            [mask_out, choose_out, message_out],
            [resets_row, routes_row, cotangent, expert_in, expert_out],
            [
                ((groups, folded, hidden_units), BF16),
                ((experts, 2, share, hidden_units), BF16),
                ((1, length), jnp.int32),
                ((1, length), jnp.int32),
                ((length, width), BF16),
                pltpu.SemaphoreType.DMA((3,)),
                pltpu.SemaphoreType.DMA((2 * experts,)),
                pltpu.SemaphoreType.DMA((3 * experts,)),
            ],
            far_args=range(5),
            far_outs=(2,), )
        weights = exchange(packed)
    else:
        masks, choose, grad_send = run_kernel(
            functools.partial(prepare_kernel, experts, capacity, block_rows),
            [mask_out, choose_out, slots_out],
            [resets_row, routes_row, cotangent], loose_outs=(2,))
        first_w = exchange(jnp.tile(expert_in, (tile_count, 1, 1))).reshape(weight_outs[0][0])
        second_w = exchange(jnp.tile(expert_out, (tile_count, 1, 1))).reshape(weight_outs[0][0])
        grad_slots = exchange_slots(grad_send)
        (d_hidden,) = run_kernel(
            hidden_back_kernel, [((slot_count, hidden_units), F32)], [grad_slots, second_w]
        )

    rows, normed, act, inner, conv, gate, scale, gain_columns, mixed_part = run_kernel(
        enter_kernel,
        [
            ((length, width), BF16),
            ((width, length), BF16),
            ((length, chans), BF16),
            ((length, chans), F32),
            ((length, chans), F32),
            ((length, chans), F32),
            ((1, length), F32),
            ((column, length), F32),
            ((proj, length), BF16),
        ],
        [place, *token_pieces, norm_one, in_turned, conv_weight, conv_bias, x_turned, masks],
        [((width, length), F32)],
        scalars=1, loose_outs=(8,), staged=(1, 2, 3, 4, 10))
    mixed_pieces = share_rows(mixed_part, parts)
    *mix_chunks, mixed, first, y = run_kernel(
        scan_forward_kernel,
        [((length // parts, width), BF16)] * parts
        + [
            ((proj, length), F32),
            ((width + 2 * chans, length), BF16),
            ((length, chans), F32),
        ],
        [
            place,
            *mixed_pieces,
            dt_proj,
            dt_bias,
            decay_log,
            skip_gain,
            act,
            gate,
            masks,
            out_proj,
            normed,
        ],
        [
            ((parts, proj, length), BF16),
            ((states, full), F32),
            ((length, full), F32),
            ((length, full), F32),
            ((length, full), F32),
            ((length, width), F32),
        ],
        scalars=1, loose_outs=(0, 1, 2, 3, 5), staged=(1, 2, 3, 4, 9, 10, 11, 13))
    mixer_pieces = share_rows(add_low(send_chunks(mix_chunks)), parts)
    if near:
        first_x, first_y = swap(first, 2), swap(first, 4)
    residual, residual_columns, send_slots = run_kernel(
        dispatch_kernel,
        [((length, width), F32), ((column, length), F32), slots_out],
        [place, *mixer_pieces, rows, norm_two, choose],
        [((width, length), F32)],
        scalars=1, staged=(1, 5, 7))
    if near:
        first_w, second_w, grad_slots, d_hidden = run_kernel(
            functools.partial(unpack_kernel, share, capacity),
            weight_outs + [slots_out, ((slot_count, hidden_units), F32)],
            after([weights], send_slots),
            [*weight_outs, slots_out, pltpu.SemaphoreType.DMA((5 * groups,))],
            far_args=(0,),
            far_outs=(0, 1, 2),
        )
        first_x, first_y = after([first_x, first_y], d_hidden)
        halves = pass_halves(first_x, first_y)
        first_d = swap_across(halves)
    arrived = exchange_slots(send_slots)
    hidden, d_pre, d_slots = run_kernel(
        expert_kernel, [hidden_out, hidden_out, slots_out], [arrived, first_w, d_hidden], staged=(0, 1, 2))
    if near:
        d_slots = after([d_slots], first_d)[0]
    back_slots = exchange_slots(d_slots)
    grad_args = [arrived, grad_slots, hidden, d_pre, second_w]
    grad_out = ((experts, share, hidden_units), F32)
    if near:
        (packed,) = run_kernel(
            functools.partial(expert_grads_pack_kernel, share, capacity),
            [message_out],
            grad_args,
            [
                ((2, width, hidden_units), BF16),
                ((groups, folded, hidden_units), BF16),
                pltpu.SemaphoreType.DMA((3 * groups,)),
            ],
            far_outs=(0,), staged=range(5))
        firsts = swap_near([first, first_x, first_y, *first_d])
        back_slots = after([back_slots], packed, firsts)[0]
        packed = after([packed], back_slots)[0]
        owned = exchange(packed)
    else:
        grad_first, grad_second, moe_slots = run_kernel(
            expert_grads_kernel, weight_outs + [slots_out], grad_args, loose_outs=(0, 1, 2))
    back_chunks = run_kernel(
        back_rows_kernel,
        [((length // parts, width), BF16)] * parts,
        [place, choose, back_slots],
        [((length, width), F32)],
        scalars=1, loose_outs=(0, 1, 2, 3), staged=(1, 2))
    send_pieces = share_rows(add_low(send_chunks(back_chunks)), parts)
    decays, history, step_rows, drive_rows, step_slope, y_slope, gate_slope = run_kernel(
        scan_states_kernel,
        [
            ((length * states, full), F32),
            (((length + 1) * states, full), F32),
            ((length, full), F32),
            ((length, full), F32),
            ((length, chans), F32),
            ((length, chans), F32),
            ((length, chans), F32),
        ],
        [y, gate, act, *after([mixed], back_chunks[0]), masks, dt_proj, dt_bias, decay_log],
        [((states, full), F32), ((length, full), F32)],
        staged=range(5),
        held_outs=range(7),
    )
    send_pieces = after(send_pieces, decays)
    d_columns, d_mix, d_gated, gain_grad_two = run_kernel(
        mixer_grad_kernel,
        [
            ((column, length), F32),
            ((width, length), BF16),
            ((length, chans), F32),
            ((1, width), F32),
        ],
        [place, *send_pieces, residual, norm_two, cotangent, out_proj],
        [((length, width), F32), ((width, length), F32)],
        scalars=1, staged=(1, 5, 7, 8), held_outs=(1, 2, 3))
    d_mixed_part, d_act_scan, d_gate, second = run_kernel(
        scan_backward_kernel,
        [
            ((proj, length), BF16),
            ((length, chans), F32),
            ((length, chans), BF16),
            ((width + 2 * chans, length), BF16),
        ],
        [
            d_gated,
            y_slope,
            gate_slope,
            act,
            mixed,
            dt_proj,
            decay_log,
            skip_gain,
            gain_grad_two,
            d_mix,
            decays,
            history,
            step_rows,
            drive_rows,
            step_slope,
        ],
        [
            ((states, full), F32),
            ((length, full), F32),
            ((length, full), F32),
            ((length, full), F32),
        ],
        staged=(3, 4),
        loose_outs=(0, 3),
        held_outs=(1, 2),
    )
    d_mixed_pieces = share_rows(d_mixed_part, parts)
    if near:
        second_x, second_y = swap(second, 2), swap(second, 4)
    last_rows = chans + -(-proj // 16) * 16 + tiles * 2 * VECTORS_TWO
    normed_shares, message = run_kernel(
        leave_kernel,
        [((parts, column + 16, length), BF16), ((last_rows, length), BF16)],
        [
            place,
            *d_mixed_pieces,
            d_act_scan,
            d_gate,
            conv,
            inner,
            masks,
            x_turned,
            conv_weight,
            in_turned,
            rows,
            norm_one,
        ],
        [((parts, proj, length), BF16), ((width, length), F32), ((length, full), F32)],
        scalars=1, loose_outs=(1,), staged=(1, 7, 8, 9, 13))
    share_outs = [((2 * column + 16, length), BF16)] * parts
    if near:
        lasts = [message, swap(message, 2), swap(message, 4), swap(message, 6)]
        def first_sets(*refs):
            first_sets_kernel(refs[:10], *refs[10:])

        all_normed, all_gated, all_act = run_kernel(
            first_sets,
            [
                ((groups * length, width), BF16),
                ((chans, groups * length), BF16),
                ((chans, groups * length), BF16),
            ],
            after(firsts, message, owned),
            [((groups, width + 2 * chans, length), BF16), pltpu.SemaphoreType.DMA((10,))],
            far_args=range(10),
            held_outs=(0, 1, 2),
        )
        grad_expert_in, grad_expert_out = run_kernel(
            functools.partial(owner_kernel, share),
            [grad_out, grad_out],
            after([owned], all_normed),
            [
                ((groups, 2 * share, hidden_units), BF16),
                ((groups, 2 * share, hidden_units), F32),
                pltpu.SemaphoreType.DMA((groups,)),
                pltpu.SemaphoreType.DMA((2 * groups,)),
            ],
            far_args=(0,),
            far_outs=(0, 1),
        )
        second_x, second_y = after([second_x, second_y], grad_expert_in)
        halves = pass_halves(second_x, second_y)
        second_d = swap_across(halves)
        lasts = swap_near(after(lasts, halves))

        def back_folded(*refs):
            back_folded_kernel(share, *refs[:4], refs[4 : 4 + groups], *refs[4 + groups :])

        *shares, grad_conv_weight, grad_conv_bias = run_kernel(
            back_folded,
            [((2 * column + 16 + 2 * NORM_ROWS, length), BF16)] * parts
            + [((4, chans), F32), ((chans,), F32)],
            [place, choose, normed_shares, owned, *lasts],
            [
                slots_out,
                ((width, length), BF16),
                ((groups, tiles * 2 * VECTORS_TWO, length), BF16),
                pltpu.SemaphoreType.DMA((4 * groups,)),
            ],
            scalars=1,
            staged=(1, 2),
            far_args=range(3, 4 + groups),
            loose_outs=(parts, parts + 1),
        )
        norm_out = [((width,), F32)]
    else:
        shares = run_kernel(
            back_columns_kernel,
            share_outs,
            [place, choose, normed_shares, exchange_slots(moe_slots)],
            [((width, length), BF16)],
            scalars=1,
            loose_outs=(0, 1, 2, 3),
        )

        norm_out = []

        def owner_sum(values):
            got = exchange(values.reshape(groups, share, hidden_units)).astype(F32)
            return jnp.sum(got.reshape(tile_count, experts, share, hidden_units), axis=0)

        grad_expert_in = owner_sum(grad_first)
        grad_expert_out = owner_sum(grad_second)
    pieces = send_chunks(shares)
    if near:
        seconds = [second, second_x, second_y, *second_d]
        seconds = swap_near(after(seconds, grad_conv_weight))

        def wide_grads(*refs):
            wide_grads_kernel(
                (rank, states, proj), refs[:10], refs[10 : 10 + groups], *refs[10 + groups :]
            )

        (
            grad_out_proj,
            grad_in_turned,
            grad_x_turned,
            grad_dt_proj,
            grad_dt_bias,
            grad_decay_log,
            grad_skip_gain,
            grad_norm_two,
        ) = run_kernel(
            wide_grads,
            [
                ((chans, width), F32),
                ((2, chans, width), F32),
                ((proj, chans), F32),
                ((rank, chans), F32),
                ((chans,), F32),
                ((states, chans), F32),
                ((chans,), F32),
                ((width,), F32),
            ],
            [*seconds, *lasts, all_normed, all_gated, all_act],
            [
                ((groups, width + 2 * chans, length), BF16),
                ((groups, last_rows, length), BF16),
                ((groups * length, width), BF16),
                ((chans, groups * length), BF16),
                ((-(-proj // 16) * 16, groups * length), BF16),
                ((full, length), F32),
                ((3, chans, width), F32),
                pltpu.SemaphoreType.DMA((10,)),
                pltpu.SemaphoreType.DMA((groups,)),
                pltpu.SemaphoreType.DMA((4,)),
            ],
            far_args=[index for index in range(10 + groups) if index not in range(3, 10)],
            far_outs=(0, 1),
            loose_outs=range(8),
        )
        pieces = after(pieces, grad_out_proj)
    else:
        top = last_rows - tiles * 2 * VECTORS_TWO
        ones = second[width + chans :].astype(F32).T
        twos = message[top:].astype(F32).reshape(tiles, 2 * VECTORS_TWO, length)
        twos = jnp.swapaxes(twos, 0, 1).reshape(2 * VECTORS_TWO, full)[:, :chans]
        plain_normed = jnp.swapaxes(normed.reshape(-1, length, 128), 0, 1).reshape(length, width)
        plain_mix = jnp.swapaxes(d_mix.reshape(-1, length, 128), 0, 1).reshape(length, width)
        grad_in_turned, grad_x_turned, grad_dt_proj, grad_out_proj, ones, twos = lax.psum(
            (
                jnp.stack(
                    [
                        dot_nn(message[:chans], plain_normed),
                        dot_nn(second[width : width + chans], plain_normed),
                    ]
                ),
                dot_nn(message[chans : chans + proj], act),
                ones[:rank],
                dot_nn(first[width : width + chans], plain_mix),
                ones[rank : rank + VECTORS_ONE]
                + ones[rank + VECTORS_ONE : rank + 2 * VECTORS_ONE],
                twos[:VECTORS_TWO] + twos[VECTORS_TWO:],
            ),
            "dp",
        )
        grad_decay_log = ones[:states]
        grad_dt_bias = ones[states]
        grad_skip_gain = ones[states + 1]
        grad_norm_two = ones[states + 2 : states + 4]
        grad_conv_weight = twos[:4]
        grad_conv_bias = twos[4]
        grad_norm_one = sum(share_rows(twos[5:7].reshape(1, width), parts)).reshape(width)
    outcome, grad_tokens, *norm_one_grad = run_kernel(
        finish_rows_kernel,
        [((column, length), BF16), ((column, length), F32)] + norm_out,
        [*pieces, residual_columns, d_columns, tokens_turned, scale, gain_columns],
        staged=range(4, 9),
        loose_outs=(0, 1, 2),
    )
    if near:
        (grad_norm_one,) = norm_one_grad
    return (
        outcome.T,
        grad_tokens.T,
        grad_norm_one,
        jnp.swapaxes(grad_in_turned, 1, 2),
        grad_conv_weight,
        grad_conv_bias,
        grad_x_turned.T,
        grad_dt_proj,
        grad_dt_bias,
        grad_decay_log,
        grad_skip_gain,
        grad_out_proj,
        grad_norm_two.reshape(width),
        grad_expert_in,
        grad_expert_out,
    )


def solution(mesh):
    placed = (
        P("dp", "tensor"),
        P("dp"),
        P("dp", None),
        P(),
        P(None, None, "tensor"),
        P(None, "tensor"),
        P("tensor"),
        P("tensor", None),
        P(None, "tensor"),
        P("tensor"),
        P(None, "tensor"),
        P("tensor"),
        P("tensor", None),
        P(),
        P(None, "dp", "tensor"),
        P(None, "dp", "tensor"),
        P("dp", None),
    )
    return jax.shard_map(
        body,
        mesh=mesh,
        in_specs=placed,
        out_specs=(
            P("dp", "tensor"),
            P("dp", "tensor"),
            P(),
            P(None, None, "tensor"),
            P(None, "tensor"),
            P("tensor"),
            P("tensor", None),
            P(None, "tensor"),
            P("tensor"),
            P(None, "tensor"),
            P("tensor"),
            P("tensor", None),
            P(),
            P(None, "dp", "tensor"),
            P(None, "dp", "tensor"),
        ),
        check_vma=False,
    )
```
